32 devices in a mesh: dp: 32 (over z, y, x, core).
Axes of the slice: x: 2, y: 2, z: 4, core: 2. Of those that a mesh axis runs over, the one named last changes fastest.
Arguments:
- experience_buffer: float32 [42, 524288], P(None, 'dp'), may hold values from -6 to 6, as said below
- sampled_indices: int32 [32, 32, 256], P('dp'), may hold values from 0 to 16383
- filled_lengths: int32 [32, 32], P('dp'), may hold values from 1 to 256, as said below
- randomizer_numbers: int32 [32, 32, 256], P('dp'), may hold values from 0 to 524287
- agent_first_matrix: float32 [17, 256], replicated, may hold values from -1.5 to 1.5
- agent_first_offset: float32 [256], replicated, may hold values from -1.5 to 1.5
- agent_second_matrix: float32 [256, 256], replicated, may hold values from -0.375 to 0.375
- agent_second_offset: float32 [256], replicated, may hold values from -1.5 to 1.5
- agent_head_matrix: float32 [256, 12], replicated, may hold values from -0.375 to 0.375
- agent_head_offset: float32 [12], replicated, may hold values from -1.5 to 1.5
- judge_first_matrix: float32 [2, 23, 256], replicated, may hold values from -1.25 to 1.25
- judge_first_offset: float32 [2, 256], replicated, may hold values from -1.5 to 1.5
- judge_second_matrix: float32 [2, 256, 256], replicated, may hold values from -0.375 to 0.375
- judge_second_offset: float32 [2, 256], replicated, may hold values from -1.5 to 1.5
- judge_output_vector: float32 [2, 256], replicated, may hold values from -0.375 to 0.375
- judge_output_offset: float32 [2], replicated, may hold values from -1.5 to 1.5
- lagged_first_matrix: float32 [2, 23, 256], replicated, may hold values from -1.25 to 1.25
- lagged_first_offset: float32 [2, 256], replicated, may hold values from -1.5 to 1.5
- lagged_second_matrix: float32 [2, 256, 256], replicated, may hold values from -0.375 to 0.375
- lagged_second_offset: float32 [2, 256], replicated, may hold values from -1.5 to 1.5
- lagged_output_vector: float32 [2, 256], replicated, may hold values from -0.375 to 0.375
- lagged_output_offset: float32 [2], replicated, may hold values from -1.5 to 1.5
- heat_exponent_level: float32 [], replicated, may hold values from -2 to 0
Outputs:
- d_actor_w1: float32 [17, 256], replicated
- d_actor_b1: float32 [256], replicated
- d_actor_w2: float32 [256, 256], replicated
- d_actor_b2: float32 [256], replicated
- d_actor_w3: float32 [256, 12], replicated
- d_actor_b3: float32 [12], replicated
- d_critic_w1: float32 [2, 23, 256], replicated
- d_critic_b1: float32 [2, 256], replicated
- d_critic_w2: float32 [2, 256, 256], replicated
- d_critic_b2: float32 [2, 256], replicated
- d_critic_w3: float32 [2, 256], replicated
- d_critic_b3: float32 [2], replicated
- d_log_alpha: float32 [], replicated
- losses: float32 [3], replicated
The draws below stay inside these ranges and needn't reach their ends.
Inputs may be any that keep to these rules, and one draw needn't show every extreme that they name: `experience_buffer`: columns in order: state (17), action (6), reward, next state (17), done flag of 0 or 1. filled_lengths[o, p] is how many leading entries of owner o's list for storage device p are used; in every draw one storage device, drawn from the seed, receives full lists of 256 from every owner.
All inputs are finite; a program needn't handle non-finite values.
Results may differ from the reference program's by a relative error of at most 0.0003.
Values sent between devices are 32-bit elements; how exact they have to be, the bound alone decides.
A program may use at most 256 MiB of HBM per device.

```python
import math
import jax
import jax.numpy as jnp
from jax import lax

OBS = 17
CONTROL_WIDTH = 6
HID = 256
SLOT_DEV = 8192
R_DEV = 16384
CAP = 256
N_DP = 32


def draw_experience_buffer(key, part):
    key = jax.random.fold_in(key, 11)
    keys = jax.random.split(key, 5)
    width = R_DEV * N_DP
    present_sensed_world = jnp.clip(jax.random.normal(keys[0], (OBS, width), jnp.float32), -6.0, 6.0)
    following_observations = jnp.clip(jax.random.normal(keys[1], (OBS, width), jnp.float32), -6.0, 6.0)
    immediate_payoff = jnp.clip(jax.random.normal(keys[2], (1, width), jnp.float32), -6.0, 6.0)
    picked_controls = jax.random.uniform(keys[3], (CONTROL_WIDTH, width), jnp.float32, -0.95, 0.95)
    terminal_flags = jax.random.bernoulli(keys[4], 0.1, (1, width)).astype(jnp.float32)
    return jnp.concatenate([present_sensed_world, picked_controls, immediate_payoff, following_observations, terminal_flags], axis=0)


def draw_filled_lengths(key, part):
    key = jax.random.fold_in(key, 12)
    first_key, second_key = jax.random.split(key)
    capacity = SLOT_DEV // N_DP
    owner_ids = jnp.arange(N_DP, dtype=jnp.int32)
    floor_row = jnp.maximum(1, capacity * owner_ids // N_DP)
    ceil_row = jnp.minimum(capacity, capacity // 2 + capacity * owner_ids // N_DP)
    drawn = jax.random.randint(first_key, (N_DP, N_DP), floor_row[:, None], ceil_row[:, None] + 1)
    full_peer = jax.random.randint(second_key, (), 0, N_DP)
    return jnp.where(owner_ids[None, :] == full_peer, capacity, drawn).astype(jnp.int32)


def touch_ends(array, own_key, smallest, largest):
    spot = [jax.random.randint(jax.random.fold_in(own_key, axis), (), 0, length) for axis, length in enumerate(array.shape)]
    widest = array.shape.index(max(array.shape))
    next_to = spot[:widest] + [(spot[widest] + 1) % array.shape[widest]] + spot[widest + 1:]
    return array.at[tuple(spot)].set(smallest).at[tuple(next_to)].set(largest)


def centred(key, extent, scale, reach, kind=jnp.bfloat16):
    return jnp.clip(scale * jax.random.normal(key, extent, jnp.float32), -reach, reach).astype(kind)


def setup_inputs(seed: int = 0) -> dict:
    key_list = jax.random.split(jax.random.key(seed), 24)
    return {
        "experience_buffer": draw_experience_buffer(jax.random.fold_in(key_list[23], 71), 0),
        "sampled_indices": touch_ends(jax.random.randint(key_list[1], (N_DP, N_DP, CAP), 0, R_DEV), jax.random.fold_in(key_list[1], 1), 0, R_DEV - 1).astype(jnp.int32),
        "filled_lengths": draw_filled_lengths(jax.random.fold_in(key_list[23], 71), 0),
        "randomizer_numbers": touch_ends(jax.random.randint(key_list[3], (N_DP, N_DP, CAP), 0, 524288), jax.random.fold_in(key_list[3], 1), 0, 524287).astype(jnp.int32),
        "agent_first_matrix": centred(key_list[4], (OBS, HID), OBS ** -0.5, 1.5, jnp.float32),
        "agent_first_offset": centred(key_list[5], (HID,), 0.3, 1.5, jnp.float32),
        "agent_second_matrix": centred(key_list[6], (HID, HID), HID ** -0.5, 0.375, jnp.float32),
        "agent_second_offset": centred(key_list[7], (HID,), 0.3, 1.5, jnp.float32),
        "agent_head_matrix": centred(key_list[8], (HID, 2 * CONTROL_WIDTH), HID ** -0.5, 0.375, jnp.float32),
        "agent_head_offset": centred(key_list[9], (2 * CONTROL_WIDTH,), 0.3, 1.5, jnp.float32),
        "judge_first_matrix": centred(key_list[10], (2, OBS + CONTROL_WIDTH, HID), (OBS + CONTROL_WIDTH) ** -0.5, 1.25, jnp.float32),
        "judge_first_offset": centred(key_list[11], (2, HID), 0.3, 1.5, jnp.float32),
        "judge_second_matrix": centred(key_list[12], (2, HID, HID), HID ** -0.5, 0.375, jnp.float32),
        "judge_second_offset": centred(key_list[13], (2, HID), 0.3, 1.5, jnp.float32),
        "judge_output_vector": centred(key_list[14], (2, HID), HID ** -0.5, 0.375, jnp.float32),
        "judge_output_offset": centred(key_list[15], (2,), 0.3, 1.5, jnp.float32),
        "lagged_first_matrix": centred(key_list[16], (2, OBS + CONTROL_WIDTH, HID), (OBS + CONTROL_WIDTH) ** -0.5, 1.25, jnp.float32),
        "lagged_first_offset": centred(key_list[17], (2, HID), 0.3, 1.5, jnp.float32),
        "lagged_second_matrix": centred(key_list[18], (2, HID, HID), HID ** -0.5, 0.375, jnp.float32),
        "lagged_second_offset": centred(key_list[19], (2, HID), 0.3, 1.5, jnp.float32),
        "lagged_output_vector": centred(key_list[20], (2, HID), HID ** -0.5, 0.375, jnp.float32),
        "lagged_output_offset": centred(key_list[21], (2,), 0.3, 1.5, jnp.float32),
        "heat_exponent_level": jnp.clip(jax.random.uniform(key_list[22], (), jnp.float32, -2.0, 0.0), -2.0, 0.0),
    }


@jax.custom_vjp
def low(v):
    return lax.optimization_barrier(v.astype(jnp.bfloat16)).astype(jnp.float32)

@jax.custom_vjp
def low_back(v):
    return v

def low_keep(v):
    return (low(v), None)

def low_pass(kept, grad):
    return (grad,)

def back_keep(v):
    return (v, None)

def back_low(kept, grad):
    return (low(grad),)
low.defvjp(low_keep, low_pass)
low_back.defvjp(back_keep, back_low)
PRECISE = lax.Precision.HIGHEST
GAMMA_FACTOR = 0.99
LOG_FLOOR = -5.0
LOG_CEIL = 2.0
SOFTNESS = 0.25

def stochastic_samples_from(seed_rows, first, number):
    components = first + jnp.arange(number, dtype=jnp.int32)
    seed_base = (seed_rows % 65521)[:, None]
    mixed = (seed_base * 257 + components[None, :] * 7919 + 1) % 65521
    first_hash = (mixed * 32749 + 12345) % 65521
    second_hash = (first_hash * 32749 + 54321) % 65521
    u_one = (first_hash.astype(jnp.float32) + 0.5) / 65521.0
    u_two = (second_hash.astype(jnp.float32) + 0.5) / 65521.0
    return jnp.sqrt(-2.0 * jnp.log(u_one)) * jnp.cos(2.0 * math.pi * u_two)

def linear(inputs, weight, offset):
    return jnp.dot(inputs, weight, precision=PRECISE) + offset

def actor_forward(controller_params_pack, present_sensed_world, normal_jitter):
    first_w, first_b, second_w, second_b, third_w, third_b = controller_params_pack
    hidden = jax.nn.silu(linear(present_sensed_world, first_w, first_b))
    hidden = jax.nn.silu(linear(hidden, second_w, second_b))
    output = linear(hidden, third_w, third_b)
    center = output[:, :CONTROL_WIDTH]
    spread = LOG_FLOOR + 0.5 * (LOG_CEIL - LOG_FLOOR) * (jnp.tanh(output[:, CONTROL_WIDTH:]) + 1.0)
    latent = center + jnp.exp(spread) * normal_jitter
    squashed = jnp.tanh(latent)
    squash = 2.0 * (math.log(2.0) - latent - jax.nn.softplus(-2.0 * latent))
    chosen_move_logprob = lax.optimization_barrier(jnp.sum(-0.5 * normal_jitter * normal_jitter - spread - 0.5 * math.log(2.0 * math.pi) - squash, axis=1))
    return (squashed, chosen_move_logprob)

def critic_forward(scorer_params_pack, member, present_sensed_world, picked_controls):
    first_w, first_b, second_w, second_b, third_w, third_b = scorer_params_pack
    joined = jnp.concatenate([present_sensed_world, picked_controls], axis=1)
    hidden = jax.nn.silu(linear(joined, first_w[member], first_b[member]))
    hidden = jax.nn.silu(linear(hidden, second_w[member], second_b[member]))
    return jnp.dot(hidden, third_w[member], precision=PRECISE) + third_b[member]

def soft_min(left_q, right_q):
    return -SOFTNESS * jnp.logaddexp(-left_q / SOFTNESS, -right_q / SOFTNESS)

def split_fields(fetched):
    present_sensed_world = fetched[:, :OBS]
    picked_controls = fetched[:, OBS:OBS + CONTROL_WIDTH]
    immediate_payoff = fetched[:, OBS + CONTROL_WIDTH]
    following_observations = fetched[:, OBS + CONTROL_WIDTH + 1:2 * OBS + CONTROL_WIDTH + 1]
    terminal_flags = fetched[:, 2 * OBS + CONTROL_WIDTH + 1]
    return (present_sensed_world, picked_controls, immediate_payoff, following_observations, terminal_flags)

def backed_up_returns(controller_params_pack, lagged_weights_tuple, alpha_coefficient, following_observations, immediate_payoff, terminal_flags, following_gaussian_draw):
    next_actions, following_move_logprob = actor_forward(controller_params_pack, following_observations, following_gaussian_draw)
    lesser_twin_quality = soft_min(critic_forward(lagged_weights_tuple, 0, following_observations, next_actions), critic_forward(lagged_weights_tuple, 1, following_observations, next_actions))
    return immediate_payoff + GAMMA_FACTOR * (1.0 - terminal_flags) * (lesser_twin_quality - alpha_coefficient * following_move_logprob)

def slice_costs(controller_params_pack, scorer_params_pack, heat_exponent_level, present_sensed_world, picked_controls, fitting_aims, normal_jitter, occupied_marker):
    alpha_coefficient = jnp.exp(heat_exponent_level)
    q_first = critic_forward(scorer_params_pack, 0, present_sensed_world, picked_controls) - fitting_aims
    q_second = critic_forward(scorer_params_pack, 1, present_sensed_world, picked_controls) - fitting_aims
    critic_loss = jnp.sum(occupied_marker * 0.5 * (q_first * q_first + q_second * q_second))
    fresh, chosen_move_logprob = actor_forward(controller_params_pack, present_sensed_world, normal_jitter)
    judged_quality = soft_min(critic_forward(scorer_params_pack, 0, present_sensed_world, fresh), critic_forward(scorer_params_pack, 1, present_sensed_world, fresh))
    agent_penalty_amount = jnp.sum(occupied_marker * (alpha_coefficient * chosen_move_logprob - judged_quality))
    alpha_penalty = jnp.sum(occupied_marker * (-heat_exponent_level * (chosen_move_logprob - CONTROL_WIDTH)))
    return (critic_loss, agent_penalty_amount, alpha_penalty)

def reference(experience_buffer, sampled_indices, filled_lengths, randomizer_numbers, agent_first_matrix, agent_first_offset, agent_second_matrix, agent_second_offset, agent_head_matrix, agent_head_offset, judge_first_matrix, judge_first_offset, judge_second_matrix, judge_second_offset, judge_output_vector, judge_output_offset, lagged_first_matrix, lagged_first_offset, lagged_second_matrix, lagged_second_offset, lagged_output_vector, lagged_output_offset, heat_exponent_level):
    controller_params_pack = (agent_first_matrix, agent_first_offset, agent_second_matrix, agent_second_offset, agent_head_matrix, agent_head_offset)
    scorer_params_pack = (judge_first_matrix, judge_first_offset, judge_second_matrix, judge_second_offset, judge_output_vector, judge_output_offset)
    lagged_weights_tuple = (lagged_first_matrix, lagged_first_offset, lagged_second_matrix, lagged_second_offset, lagged_output_vector, lagged_output_offset)
    owner_ids = jnp.arange(N_DP, dtype=jnp.int32)
    positions = owner_ids[None, :, None] * R_DEV + sampled_indices

    def gather_owner(position, valid_count, seed_row):
        fetched = jnp.take(experience_buffer, position.reshape(-1), axis=1).T
        occupied_marker = (jnp.arange(CAP, dtype=jnp.int32)[None, :] < valid_count[:, None]).reshape(-1).astype(jnp.float32)
        return (fetched, occupied_marker, seed_row.reshape(-1))

    def target_block(pieces):
        position, valid_count, seed_row = pieces
        fetched, occupied_marker, plain_seed_stream = gather_owner(position, valid_count, seed_row)
        present_sensed_world, picked_controls, immediate_payoff, following_observations, terminal_flags = split_fields(fetched)
        return backed_up_returns(controller_params_pack, lagged_weights_tuple, jnp.exp(heat_exponent_level), following_observations, immediate_payoff, terminal_flags, stochastic_samples_from(plain_seed_stream, CONTROL_WIDTH, CONTROL_WIDTH))
    fitting_aims = lax.map(target_block, (positions, filled_lengths, randomizer_numbers))

    def evaluate_network(present_controller, present_scorer, present_heat):

        def owner_block(running, pieces):
            position, valid_count, seed_row, aimed_record = pieces
            fetched, occupied_marker, plain_seed_stream = gather_owner(position, valid_count, seed_row)
            present_sensed_world, picked_controls, immediate_payoff, following_observations, terminal_flags = split_fields(fetched)
            device_splits = slice_costs(present_controller, present_scorer, present_heat, present_sensed_world, picked_controls, aimed_record, stochastic_samples_from(plain_seed_stream, 0, CONTROL_WIDTH), occupied_marker)
            return ((running[0] + device_splits[0], running[1] + device_splits[1], running[2] + device_splits[2]), None)
        zero_val = jnp.zeros((), jnp.float32)
        running, unused = lax.scan(jax.checkpoint(owner_block), (zero_val, zero_val, zero_val), (positions, filled_lengths, randomizer_numbers, fitting_aims))
        return running
    penalty_totals, reverse_derivative = jax.vjp(evaluate_network, controller_params_pack, scorer_params_pack, heat_exponent_level)
    valid_total = jnp.sum(filled_lengths).astype(jnp.float32)
    zero_val = jnp.zeros((), jnp.float32)
    unit_val = jnp.ones((), jnp.float32) / valid_total
    critic_grads = reverse_derivative((unit_val, zero_val, zero_val))[1]
    actor_grads = reverse_derivative((zero_val, unit_val, zero_val))[0]
    alpha_grad = reverse_derivative((zero_val, zero_val, unit_val))[2]
    losses = jnp.stack([penalty_totals[0], penalty_totals[1], penalty_totals[2]]) / valid_total
    return (actor_grads[0], actor_grads[1], actor_grads[2], actor_grads[3], actor_grads[4], actor_grads[5], critic_grads[0], critic_grads[1], critic_grads[2], critic_grads[3], critic_grads[4], critic_grads[5], alpha_grad, losses)
```

```python
import functools
import math

import jax
import jax.numpy as jnp
from jax import lax
from jax.experimental import pallas as pl
from jax.experimental.pallas import tpu as pltpu
from jax.sharding import PartitionSpec as P

OBS = 17
ACT = 6
HID = 256
GAMMA = 0.99
PRIME = 65521
TILE = 1024
BF = jnp.bfloat16
F32 = jnp.float32


def dot(a, b):
    return jnp.dot(a, b, preferred_element_type=F32)


def dot_t(a, b):
    return lax.dot_general(a, b, (((1,), (1,)), ((), ())), preferred_element_type=F32)


def split(x):
    hi = x.astype(BF).astype(F32)
    return hi, x - hi


def mod_prime(x):
    y = ((x >> 16) * 15) + (x & 65535)
    y = ((y >> 16) * 15) + (y & 65535)
    return jnp.where(y >= PRIME, y - PRIME, y)


def noise(seeds, rows):
    comp = jnp.where(rows >= 8, rows - 2, rows)
    z = mod_prime(seeds)
    h0 = mod_prime(z * 257 + comp * 7919 + 1)
    h1 = mod_prime(h0 * 32749 + 12345)
    h2 = mod_prime(h1 * 32749 + 54321)
    u1 = (h1.astype(F32) + 0.5) / float(PRIME)
    u2 = (h2.astype(F32) + 0.5) / float(PRIME)
    return jnp.sqrt(-2.0 * jnp.log(u1)) * jnp.cos(2.0 * math.pi * u2)


def fold(x):
    return functools.reduce(lambda a, b: a + b, [x[:, k * 128 : (k + 1) * 128] for k in range(x.shape[1] // 128)])


def net_kernel(
    idx_s, cnt_s, alpha_s, hb3_s, jb3_s, lb3_s,
    buf, seeds,
    aw1, ab1, aw2, ab2, aw3,
    jw1, jb1, jw2, jb2, jw3,
    lw1, lb1, lw2, lb2, lw3,
    gw2, gaw1, gcw1, gaw3, gcol, gmisc,
    tab, xrow, w1all, f2, b2, head, headb, da_w, col, tmp, rowbuf,
    *, cap, width, slots,
):
    T = min(TILE, slots)
    nt = slots // T
    lists = T // cap

    @pl.loop(0, width // 128)
    def _(c):
        blk = buf[:, pl.ds(pl.multiple_of(c * 128, 128), 128)]
        tab[pl.ds(pl.multiple_of(c * 128, 128), 128), 0:42] = blk.T

    rowbuf[...] = jnp.zeros_like(rowbuf)
    for l, (w1, b1, k) in enumerate(((aw1, ab1, None), (jw1, jb1, 0), (jw1, jb1, 1), (lw1, lb1, 0), (lw1, lb1, 1))):
        if k is None:
            tmp[0:6, :] = jnp.zeros((6, HID), F32)
            tmp[6:7, :] = b1[...]
            tmp[7:8, :] = w1[16:17, :]
            tmp[8:24, :] = w1[0:16, :]
        else:
            tmp[0:6, :] = w1[k, 17:23, :]
            tmp[6:7, :] = b1[k : k + 1, :]
            tmp[7:8, :] = w1[k, 16:17, :]
            tmp[8:24, :] = w1[k, 0:16, :]
        hi, lo = split(0.5 * tmp[0:24, :])
        w1all[l * HID : (l + 1) * HID, :] = jnp.concatenate([hi, hi, lo], axis=0).T.astype(BF)
        if l in (1, 2):
            hi, lo = split(tmp[0:8, :])
            da_w[l - 1] = jnp.concatenate([hi, lo], axis=0).astype(BF)
    for l, w in enumerate((aw2[...], jw2[0], jw2[1], lw2[0], lw2[1])):
        hi, lo = split(0.5 * w)
        if l < 3:
            b2[l, 0:HID, :] = hi.astype(BF)
            b2[l, HID:, :] = lo.astype(BF)
        f2[l, 0:HID, :] = hi.T.astype(BF)
        f2[l, HID:, :] = lo.T.astype(BF)
    tmp[0:12, :] = aw3[...].T
    w_mean = tmp[0:8, :]
    w_ls = tmp[6:14, :]
    r8 = lax.broadcasted_iota(jnp.int32, (8, HID), 0)
    w_head = jnp.concatenate([jnp.where(r8 < 6, w_mean, 0.0), jnp.where(r8 < 6, w_ls, 0.0)], axis=0)
    hi, lo = split(w_head)
    head[...] = jnp.concatenate([hi, lo], axis=0).astype(BF)
    headb[...] = (0.5 * jnp.concatenate([hi, lo], axis=0)).T.astype(BF)
    rowbuf[0:1, :] = 0.5 * ab2[...]
    rowbuf[1:3, :] = 0.5 * jb2[...]
    rowbuf[3:5, :] = 0.5 * lb2[...]
    rowbuf[5:7, :] = jw3[...]
    rowbuf[7:9, :] = lw3[...]
    col[:, 0:16] = rowbuf[...].T
    rows16 = lax.broadcasted_iota(jnp.int32, (16, 1), 0)
    hb = jnp.zeros((16, 1), F32)
    for k in range(12):
        hb = jnp.where(rows16 == (k if k < 6 else k + 2), hb3_s[k], hb)

    gw2[...] = jnp.zeros_like(gw2)
    gaw1[...] = jnp.zeros_like(gaw1)
    gcw1[...] = jnp.zeros_like(gcw1)
    gaw3[...] = jnp.zeros_like(gaw3)
    gcol[...] = jnp.zeros_like(gcol)
    gmisc[...] = jnp.zeros_like(gmisc)
    level = alpha_s[0]

    def act(u):
        t = jnp.tanh(u)
        p = 1.0 + t
        h = u * p
        return h, p + h * (2.0 - p)

    def layer2(l, h):
        r = dot(f2[l], h.astype(BF))
        return act(r[:HID] + r[HID:] + col[:, l : l + 1])

    def first(l0, l1, x24):
        hi, lo = split(x24)
        xs = jnp.concatenate([hi, lo, hi], axis=0).astype(BF)
        return dot(w1all[l0 * HID : l1 * HID, :], xs)

    def back2(l, g):
        r = dot(b2[l], g)
        return r[:HID] + r[HID:]

    def head_out(h2):
        r = dot(head[...], h2.astype(BF))
        o = r[0:16] + r[16:32] + hb
        mean = o[0:8]
        t = jnp.tanh(o[8:16])
        ls = -5.0 + 3.5 * (t + 1.0)
        return mean, t, ls

    def sample(mean, ls, e, live):
        sg = jnp.exp(ls)
        u = mean + sg * e
        a = jnp.tanh(u)
        au = jnp.abs(u)
        sq = 2.0 * (math.log(2.0) - au - jnp.log1p(jnp.exp(-2.0 * au)))
        lp = -0.5 * e * e - ls - 0.5 * math.log(2.0 * math.pi) - sq
        return a, sg, jnp.sum(jnp.where(live, lp, 0.0), axis=0, keepdims=True)

    def q_of(h2, wcol, b):
        return jnp.sum(h2 * wcol, axis=0, keepdims=True) + b

    def softmin(q, w):
        a, b = -4.0 * q, -4.0 * w
        m = jnp.maximum(a, b)
        return -0.25 * (m + jnp.log1p(jnp.exp(-jnp.abs(a - b))))

    @pl.loop(0, nt)
    def _(i):
        @pl.loop(0, T, unroll=8)
        def _(j):
            xrow[pl.ds(j, 1), :] = tab[pl.ds(idx_s[i * T + j], 1), :]

        xt = xrow[...].T
        row8 = lax.broadcasted_iota(jnp.int32, (8, T), 0)
        row16 = lax.broadcasted_iota(jnp.int32, (16, T), 0)
        live = row8 < ACT
        eps = noise(seeds[pl.ds(i, 1), :], row16)
        lane = lax.broadcasted_iota(jnp.int32, (1, cap), 1)
        mask = jnp.concatenate(
            [jnp.where(lane < cnt_s[i * lists + k], 1.0, 0.0).astype(F32) for k in range(lists)], axis=1
        )
        alpha = jnp.exp(jnp.full((1, T), level, F32))
        b1 = pltpu.roll(xt[16:24], 7, 0)
        reward = b1[6:7]
        xa = jnp.concatenate([jnp.where(row8 == 6, 1.0, b1), xt[0:16]], axis=0)
        b2_ = pltpu.roll(xt[40:48], 7, 0)
        done = b2_[0:1]
        n_lo = jnp.where(row8 == 7, b2_, jnp.where(row8 == 6, 1.0, 0.0))
        xn = jnp.concatenate([n_lo, xt[24:40]], axis=0)

        h1, _ = act(first(0, 1, xn))
        h2, _ = layer2(0, h1)
        mean, _, ls = head_out(h2)
        a2, _, lp2 = sample(mean, ls, eps[8:16], live)
        xn = jnp.concatenate([jnp.where(live, a2, n_lo), xt[24:40]], axis=0)
        r = first(3, 5, xn)
        qs = []
        for k in range(2):
            h1, _ = act(r[k * HID : (k + 1) * HID])
            h2, _ = layer2(3 + k, h1)
            qs.append(q_of(h2, col[:, 7 + k : 8 + k], lb3_s[k]))
        y = reward + GAMMA * (1.0 - done) * (softmin(qs[0], qs[1]) - alpha * lp2)

        hi, lo = split(xa)
        xs = jnp.concatenate([hi, lo, hi], axis=0).astype(BF)
        xw = jnp.concatenate([hi, lo], axis=0).astype(BF)
        r = dot(w1all[0 : 3 * HID, :], xs)
        closs = jnp.zeros((1, T), F32)
        for k in range(2):
            h1, d1 = act(r[(1 + k) * HID : (2 + k) * HID])
            h1b = h1.astype(BF)
            h2, d2 = layer2(1 + k, h1b)
            w3 = col[:, 5 + k : 6 + k]
            dq = q_of(h2, w3, jb3_s[k]) - y
            mdq = dq * mask
            closs = closs + 0.5 * (mdq * dq)
            gcol[2 + k] += fold(h2 * mdq)
            g2 = (0.5 * w3) * mdq * d2
            gcol[k] += fold(g2)
            g2 = g2.astype(BF)
            gw2[1 + k] += dot_t(h1b, g2)
            g1 = (back2(1 + k, g2) * d1).astype(BF)
            w = dot_t(xw, g1)
            gcw1[k] += w[0:24] + w[24:48]
            gmisc[k : k + 1, :] += fold(mdq)

        h1a, d1a = act(r[0:HID])
        h1ab = h1a.astype(BF)
        h2a, d2a = layer2(0, h1ab)
        h2ab = h2a.astype(BF)
        mean, t, ls = head_out(h2ab)
        e = eps[0:8]
        a1, sg, lp = sample(mean, ls, e, live)
        xq = jnp.concatenate([jnp.where(live, a1, xa[0:8]), xt[0:16]], axis=0)
        r = first(1, 3, xq)
        qs, d1s, d2s = [], [], []
        for k in range(2):
            h1, d1 = act(r[k * HID : (k + 1) * HID])
            h2, d2 = layer2(1 + k, h1)
            qs.append(q_of(h2, col[:, 5 + k : 6 + k], jb3_s[k]))
            d1s.append(d1)
            d2s.append(d2)
        sm = softmin(qs[0], qs[1])
        p0 = 1.0 / (1.0 + jnp.exp(4.0 * (qs[0] - qs[1])))
        da = jnp.zeros((8, T), F32)
        for k, pk in enumerate((p0, 1.0 - p0)):
            g2 = ((0.5 * col[:, 5 + k : 6 + k]) * (-pk * mask) * d2s[k]).astype(BF)
            g1 = (back2(1 + k, g2) * d1s[k]).astype(BF)
            w = dot(da_w[k], g1)
            da = da + w[0:8] + w[8:16]
        ma = mask * alpha
        du = da * (1.0 - a1 * a1) + ma * (2.0 * a1)
        dls = (du * sg * e - ma) * (3.5 * (1.0 - t * t))
        do = jnp.concatenate([jnp.where(live, du, 0.0), jnp.where(live, dls, 0.0)], axis=0)
        gcol[5] += jnp.concatenate([fold(do), jnp.zeros((HID - 16, 128), F32)], axis=0)
        dob = do.astype(BF)
        gaw3[...] += dot_t(dob, h2ab)
        g2 = dot(headb[...], jnp.concatenate([dob, dob], axis=0)) * d2a
        gcol[4] += fold(g2)
        g2 = g2.astype(BF)
        gw2[0] += dot_t(h1ab, g2)
        g1 = (back2(0, g2) * d1a).astype(BF)
        w = dot_t(xw, g1)
        gaw1[...] += w[0:24] + w[24:48]
        gmisc[2:3, :] += fold(closs)
        gmisc[3:4, :] += fold(mask * (alpha * lp - sm))
        gmisc[4:5, :] += fold(mask * (lp - 6.0))
        gmisc[5:6, :] += fold(mask)


def local_grads(experience_buffer, idx, counts, seeds, params):
    (aw1, ab1, aw2, ab2, aw3, ab3, jw1, jb1, jw2, jb2, jw3, jb3, lw1, lb1, lw2, lb2, lw3, lb3, level) = params
    feats, width = experience_buffer.shape
    peers, cap = idx.shape
    slots = peers * cap
    T = min(TILE, slots)
    vm = pl.BlockSpec(memory_space=pltpu.VMEM)
    sm = pl.BlockSpec(memory_space=pltpu.SMEM)
    out = [
        jax.ShapeDtypeStruct((3, HID, HID), F32),
        jax.ShapeDtypeStruct((24, HID), F32),
        jax.ShapeDtypeStruct((2, 24, HID), F32),
        jax.ShapeDtypeStruct((16, HID), F32),
        jax.ShapeDtypeStruct((6, HID, 128), F32),
        jax.ShapeDtypeStruct((8, 128), F32),
    ]
    return pl.pallas_call(
        functools.partial(net_kernel, cap=cap, width=width, slots=slots),
        out_shape=out,
        in_specs=[sm] * 6 + [vm] * 17,
        out_specs=[vm] * 6,
        scratch_shapes=[
            pltpu.VMEM((width, 128), F32),
            pltpu.VMEM((T, 128), F32),
            pltpu.VMEM((5 * HID, 72), BF),
            pltpu.VMEM((5, 2 * HID, HID), BF),
            pltpu.VMEM((3, 2 * HID, HID), BF),
            pltpu.VMEM((32, HID), BF),
            pltpu.VMEM((HID, 32), BF),
            pltpu.VMEM((2, 16, HID), BF),
            pltpu.VMEM((HID, 128), F32),
            pltpu.VMEM((32, HID), F32),
            pltpu.VMEM((16, HID), F32),
        ],
        compiler_params=pltpu.CompilerParams(vmem_limit_bytes=60 << 20),
        name="networks",
    )(
        idx.reshape(-1), counts, level.reshape(1), ab3, jb3, lb3,
        experience_buffer, seeds.reshape(slots // T, T),
        aw1, ab1.reshape(1, HID), aw2, ab2.reshape(1, HID), aw3,
        jw1, jb1, jw2, jb2, jw3,
        lw1, lb1, lw2, lb2, lw3,
    )


def body(experience_buffer, sampled_indices, filled_lengths, randomizer_numbers, *params):
    peers, cap = sampled_indices.shape[1:]
    level = params[-1]
    message = jnp.concatenate(
        [sampled_indices[0], randomizer_numbers[0], jnp.broadcast_to(filled_lengths[0][:, None], (peers, 128))], axis=1
    )
    got = lax.all_to_all(message, "dp", split_axis=0, concat_axis=0, tiled=True)
    idx, seeds, counts = got[:, :cap], got[:, cap : 2 * cap], got[:, 2 * cap]
    gw2, gaw1, gcw1, gaw3, gcol, gmisc = local_grads(experience_buffer, idx, counts, seeds, params)
    cols = jnp.sum(gcol, axis=2)
    misc = jnp.sum(gmisc, axis=1)
    gw2, gaw1, gcw1, gaw3, cols, misc = lax.psum((gw2, gaw1, gcw1, gaw3, cols, misc), "dp")
    n = misc[5]
    inv = 1.0 / n

    def w1_of(g):
        return jnp.concatenate([g[8:24], g[7:8]], axis=0), g[0:6], g[6]

    s, _, b1 = w1_of(gaw1)
    c = [w1_of(gcw1[k]) for k in range(2)]
    outs = (
        s, b1, gw2[0], cols[4], jnp.concatenate([gaw3[0:6], gaw3[8:14]], axis=0).T, jnp.concatenate([cols[5, 0:6], cols[5, 8:14]]),
        jnp.stack([jnp.concatenate([x[0], x[1]], axis=0) for x in c]), jnp.stack([x[2] for x in c]),
        gw2[1:3], cols[0:2], cols[2:4], misc[0:2],
    )
    outs = tuple(o / n for o in outs)
    losses = jnp.stack([misc[2], misc[3], -level * misc[4]]) / n
    return outs + (-misc[4] / n, losses)


def solution(mesh):
    in_specs = (P(None, "dp"), P("dp", None, None), P("dp", None), P("dp", None, None)) + (P(),) * 19
    return jax.shard_map(body, mesh=mesh, in_specs=in_specs, out_specs=(P(),) * 14, check_vma=False)
```

```python
import functools
import math

import jax
import jax.numpy as jnp
from jax import lax
from jax.experimental import pallas as pl
from jax.experimental.pallas import tpu as pltpu
from jax.sharding import PartitionSpec as P

OBS = 17
ACT = 6
HID = 256
GAMMA = 0.99
PRIME = 65521
TILE = 1024
R_AW1 = 6 * HID
R_CW1 = R_AW1 + 48
R_AW3 = R_CW1 + 96
R_COL = R_AW3 + 32
R_MISC = R_COL + 16
R_END = R_MISC + 8
BF = jnp.bfloat16
F32 = jnp.float32


def dot(a, b):
    return jnp.dot(a, b, preferred_element_type=F32)


def dot_t(a, b):
    return lax.dot_general(a, b, (((1,), (1,)), ((), ())), preferred_element_type=F32)


def split(x):
    hi = x.astype(BF).astype(F32)
    return hi, x - hi


def mod_prime(x):
    y = ((x >> 16) * 15) + (x & 65535)
    y = ((y >> 16) * 15) + (y & 65535)
    return jnp.where(y >= PRIME, y - PRIME, y)


def noise(seeds, rows):
    comp = jnp.where(rows >= 8, rows - 2, rows)
    z = mod_prime(seeds)
    h0 = mod_prime(z * 257 + comp * 7919 + 1)
    h1 = mod_prime(h0 * 32749 + 12345)
    h2 = mod_prime(h1 * 32749 + 54321)
    u1 = (h1.astype(F32) + 0.5) / float(PRIME)
    u2 = (h2.astype(F32) + 0.5) / float(PRIME)
    return jnp.sqrt(-2.0 * jnp.log(u1)) * jnp.cos(2.0 * math.pi * u2)


def fold(x):
    return functools.reduce(lambda a, b: a + b, [x[:, k * 128 : (k + 1) * 128] for k in range(x.shape[1] // 128)])


def net_kernel(
    idx_s, cnt_s, alpha_s, hb3_s, jb3_s, lb3_s,
    buf, seeds,
    aw1, ab1, aw2, ab2, aw3,
    jw1, jb1, jw2, jb2, jw3,
    lw1, lb1, lw2, lb2, lw3,
    packed,
    gw2, gaw1, gcw1, gaw3, gcol, gmisc, tab, xrow, w1all, f2, b2, head, headb, da_w, col, tmp, rowbuf,
    *, cap, width, slots,
):
    T = min(TILE, slots)
    nt = slots // T
    lists = T // cap

    @pl.loop(0, width // 128)
    def _(c):
        blk = buf[:, pl.ds(pl.multiple_of(c * 128, 128), 128)]
        tab[pl.ds(pl.multiple_of(c * 128, 128), 128), 0:42] = blk.T

    rowbuf[...] = jnp.zeros_like(rowbuf)
    for l, (w1, b1, k) in enumerate(((aw1, ab1, None), (jw1, jb1, 0), (jw1, jb1, 1), (lw1, lb1, 0), (lw1, lb1, 1))):
        if k is None:
            tmp[0:6, :] = jnp.zeros((6, HID), F32)
            tmp[6:7, :] = b1[...]
            tmp[7:8, :] = w1[16:17, :]
            tmp[8:24, :] = w1[0:16, :]
        else:
            tmp[0:6, :] = w1[k, 17:23, :]
            tmp[6:7, :] = b1[k : k + 1, :]
            tmp[7:8, :] = w1[k, 16:17, :]
            tmp[8:24, :] = w1[k, 0:16, :]
        hi, lo = split(0.5 * tmp[0:24, :])
        w1all[l * HID : (l + 1) * HID, :] = jnp.concatenate([hi, hi, lo], axis=0).T.astype(BF)
        if l in (1, 2):
            hi, lo = split(tmp[0:8, :])
            da_w[l - 1] = jnp.concatenate([hi, lo], axis=0).astype(BF)
    for l, w in enumerate((aw2[...], jw2[0], jw2[1], lw2[0], lw2[1])):
        hi, lo = split(0.5 * w)
        if l < 3:
            b2[l, 0:HID, :] = hi.astype(BF)
            b2[l, HID:, :] = lo.astype(BF)
        f2[l, 0:HID, :] = hi.T.astype(BF)
        f2[l, HID:, :] = lo.T.astype(BF)
    tmp[0:12, :] = aw3[...].T
    w_mean = tmp[0:8, :]
    w_ls = tmp[6:14, :]
    r8 = lax.broadcasted_iota(jnp.int32, (8, HID), 0)
    w_head = jnp.concatenate([jnp.where(r8 < 6, w_mean, 0.0), jnp.where(r8 < 6, w_ls, 0.0)], axis=0)
    hi, lo = split(w_head)
    head[...] = jnp.concatenate([hi, lo], axis=0).astype(BF)
    headb[...] = (0.5 * jnp.concatenate([hi, lo], axis=0)).T.astype(BF)
    rowbuf[0:1, :] = 0.5 * ab2[...]
    rowbuf[1:3, :] = 0.5 * jb2[...]
    rowbuf[3:5, :] = 0.5 * lb2[...]
    rowbuf[5:7, :] = jw3[...]
    rowbuf[7:9, :] = lw3[...]
    col[:, 0:16] = rowbuf[...].T
    rows16 = lax.broadcasted_iota(jnp.int32, (16, 1), 0)
    hb = jnp.zeros((16, 1), F32)
    for k in range(12):
        hb = jnp.where(rows16 == (k if k < 6 else k + 2), hb3_s[k], hb)

    gw2[...] = jnp.zeros_like(gw2)
    gaw1[...] = jnp.zeros_like(gaw1)
    gcw1[...] = jnp.zeros_like(gcw1)
    gaw3[...] = jnp.zeros_like(gaw3)
    gcol[...] = jnp.zeros_like(gcol)
    gmisc[...] = jnp.zeros_like(gmisc)
    level = alpha_s[0]

    def act(u):
        t = jnp.tanh(u)
        p = 1.0 + t
        h = u * p
        return h, p + h * (2.0 - p)

    def layer2(l, h):
        r = dot(f2[l], h.astype(BF))
        return act(r[:HID] + r[HID:] + col[:, l : l + 1])

    def first(l0, l1, x24):
        hi, lo = split(x24)
        xs = jnp.concatenate([hi, lo, hi], axis=0).astype(BF)
        return dot(w1all[l0 * HID : l1 * HID, :], xs)

    def back2(l, g):
        r = dot(b2[l], g)
        return r[:HID] + r[HID:]

    def head_out(h2):
        r = dot(head[...], h2.astype(BF))
        o = r[0:16] + r[16:32] + hb
        mean = o[0:8]
        t = jnp.tanh(o[8:16])
        ls = -5.0 + 3.5 * (t + 1.0)
        return mean, t, ls

    def sample(mean, ls, e, live):
        sg = jnp.exp(ls)
        u = mean + sg * e
        a = jnp.tanh(u)
        au = jnp.abs(u)
        sq = 2.0 * (math.log(2.0) - au - jnp.log1p(jnp.exp(-2.0 * au)))
        lp = -0.5 * e * e - ls - 0.5 * math.log(2.0 * math.pi) - sq
        return a, sg, jnp.sum(jnp.where(live, lp, 0.0), axis=0, keepdims=True)

    def q_of(h2, wcol, b):
        return jnp.sum(h2 * wcol, axis=0, keepdims=True) + b

    def softmin(q, w):
        a, b = -4.0 * q, -4.0 * w
        m = jnp.maximum(a, b)
        return -0.25 * (m + jnp.log1p(jnp.exp(-jnp.abs(a - b))))

    @pl.loop(0, nt)
    def _(i):
        @pl.loop(0, T, unroll=8)
        def _(j):
            xrow[pl.ds(j, 1), :] = tab[pl.ds(idx_s[i * T + j], 1), :]

        xt = xrow[...].T
        row8 = lax.broadcasted_iota(jnp.int32, (8, T), 0)
        row16 = lax.broadcasted_iota(jnp.int32, (16, T), 0)
        live = row8 < ACT
        eps = noise(seeds[pl.ds(i, 1), :], row16)
        lane = lax.broadcasted_iota(jnp.int32, (1, cap), 1)
        mask = jnp.concatenate(
            [jnp.where(lane < cnt_s[i * lists + k], 1.0, 0.0).astype(F32) for k in range(lists)], axis=1
        )
        alpha = jnp.exp(jnp.full((1, T), level, F32))
        b1 = pltpu.roll(xt[16:24], 7, 0)
        reward = b1[6:7]
        xa = jnp.concatenate([jnp.where(row8 == 6, 1.0, b1), xt[0:16]], axis=0)
        b2_ = pltpu.roll(xt[40:48], 7, 0)
        done = b2_[0:1]
        n_lo = jnp.where(row8 == 7, b2_, jnp.where(row8 == 6, 1.0, 0.0))
        xn = jnp.concatenate([n_lo, xt[24:40]], axis=0)

        h1, _ = act(first(0, 1, xn))
        h2, _ = layer2(0, h1)
        mean, _, ls = head_out(h2)
        a2, _, lp2 = sample(mean, ls, eps[8:16], live)
        xn = jnp.concatenate([jnp.where(live, a2, n_lo), xt[24:40]], axis=0)
        r = first(3, 5, xn)
        qs = []
        for k in range(2):
            h1, _ = act(r[k * HID : (k + 1) * HID])
            h2, _ = layer2(3 + k, h1)
            qs.append(q_of(h2, col[:, 7 + k : 8 + k], lb3_s[k]))
        y = reward + GAMMA * (1.0 - done) * (softmin(qs[0], qs[1]) - alpha * lp2)

        hi, lo = split(xa)
        xs = jnp.concatenate([hi, lo, hi], axis=0).astype(BF)
        xw = jnp.concatenate([hi, lo], axis=0).astype(BF)
        r = dot(w1all[0 : 3 * HID, :], xs)
        closs = jnp.zeros((1, T), F32)
        for k in range(2):
            h1, d1 = act(r[(1 + k) * HID : (2 + k) * HID])
            h1b = h1.astype(BF)
            h2, d2 = layer2(1 + k, h1b)
            w3 = col[:, 5 + k : 6 + k]
            dq = q_of(h2, w3, jb3_s[k]) - y
            mdq = dq * mask
            closs = closs + 0.5 * (mdq * dq)
            gcol[2 + k] += fold(h2 * mdq)
            g2 = (0.5 * w3) * mdq * d2
            gcol[k] += fold(g2)
            g2 = g2.astype(BF)
            gw2[1 + k] += dot_t(h1b, g2)
            g1 = (back2(1 + k, g2) * d1).astype(BF)
            w = dot_t(xw, g1)
            gcw1[k] += w[0:24] + w[24:48]
            gmisc[k : k + 1, :] += fold(mdq)

        h1a, d1a = act(r[0:HID])
        h1ab = h1a.astype(BF)
        h2a, d2a = layer2(0, h1ab)
        h2ab = h2a.astype(BF)
        mean, t, ls = head_out(h2ab)
        e = eps[0:8]
        a1, sg, lp = sample(mean, ls, e, live)
        xq = jnp.concatenate([jnp.where(live, a1, xa[0:8]), xt[0:16]], axis=0)
        r = first(1, 3, xq)
        qs, d1s, d2s = [], [], []
        for k in range(2):
            h1, d1 = act(r[k * HID : (k + 1) * HID])
            h2, d2 = layer2(1 + k, h1)
            qs.append(q_of(h2, col[:, 5 + k : 6 + k], jb3_s[k]))
            d1s.append(d1)
            d2s.append(d2)
        sm = softmin(qs[0], qs[1])
        p0 = 1.0 / (1.0 + jnp.exp(4.0 * (qs[0] - qs[1])))
        da = jnp.zeros((8, T), F32)
        for k, pk in enumerate((p0, 1.0 - p0)):
            g2 = ((0.5 * col[:, 5 + k : 6 + k]) * (-pk * mask) * d2s[k]).astype(BF)
            g1 = (back2(1 + k, g2) * d1s[k]).astype(BF)
            w = dot(da_w[k], g1)
            da = da + w[0:8] + w[8:16]
        ma = mask * alpha
        du = da * (1.0 - a1 * a1) + ma * (2.0 * a1)
        dls = (du * sg * e - ma) * (3.5 * (1.0 - t * t))
        do = jnp.concatenate([jnp.where(live, du, 0.0), jnp.where(live, dls, 0.0)], axis=0)
        gcol[5] += jnp.concatenate([fold(do), jnp.zeros((HID - 16, 128), F32)], axis=0)
        dob = do.astype(BF)
        gaw3[...] += dot_t(dob, h2ab)
        g2 = dot(headb[...], jnp.concatenate([dob, dob], axis=0)) * d2a
        gcol[4] += fold(g2)
        g2 = g2.astype(BF)
        gw2[0] += dot_t(h1ab, g2)
        g1 = (back2(0, g2) * d1a).astype(BF)
        w = dot_t(xw, g1)
        gaw1[...] += w[0:24] + w[24:48]
        gmisc[2:3, :] += fold(closs)
        gmisc[3:4, :] += fold(mask * (alpha * lp - sm))
        gmisc[4:5, :] += fold(mask * (lp - 6.0))
        gmisc[5:6, :] += fold(mask)

    for m in range(3):
        for h in range(2):
            packed[(2 * m + h) * HID : (2 * m + h + 1) * HID, :] = gw2[m, :, h * 128 : (h + 1) * 128]
    lane = lax.broadcasted_iota(jnp.int32, (HID, 128), 1)
    cols = jnp.zeros((HID, 128), F32)
    for k in range(6):
        cols = jnp.where(lane == k, jnp.sum(gcol[k], axis=1, keepdims=True), cols)
    for h in range(2):
        packed[R_AW1 + 24 * h : R_AW1 + 24 * (h + 1), :] = gaw1[:, h * 128 : (h + 1) * 128]
        for k in range(2):
            at = R_CW1 + 48 * k + 24 * h
            packed[at : at + 24, :] = gcw1[k, :, h * 128 : (h + 1) * 128]
        packed[R_AW3 + 16 * h : R_AW3 + 16 * (h + 1), :] = gaw3[:, h * 128 : (h + 1) * 128]
        packed[R_COL + 8 * h : R_COL + 8 * (h + 1), :] = cols[h * 128 : (h + 1) * 128].T[0:8]
    packed[R_MISC : R_MISC + 8, :] = gmisc[...]
    packed[R_END:, :] = jnp.zeros((packed.shape[0] - R_END, 128), F32)


def split_sizes(n):
    sizes = [2]
    n //= 2
    while n > 1:
        f = 4 if n % 4 == 0 else n if n < 4 else 2
        sizes.append(f)
        n //= f
    return sizes


def sum_kernel(sizes, mine, out, full, *rest):
    ns = len(sizes)
    got, part, sems = rest[:ns], rest[ns : 2 * ns], rest[2 * ns]
    me = lax.axis_index("dp")
    digits, strides, st = [], [], 1
    for f in sizes:
        digits.append(lax.rem(me // st, f))
        strides.append(st)
        st *= f

    def member(s, k):
        d = lax.rem(digits[s] + k, sizes[s])
        return d, me + (d - digits[s]) * strides[s]

    barrier = pltpu.get_barrier_semaphore()
    count = 0
    for s in range(ns):
        for k in range(1, sizes[s]):
            pl.semaphore_signal(barrier, inc=1, device_id=(member(s, k)[1],), device_id_type=pl.DeviceIdType.MESH)
            count += 1
    pl.semaphore_wait(barrier, count)

    def send(src, dst, s, k, phase):
        return pltpu.make_async_remote_copy(
            src_ref=src, dst_ref=dst, send_sem=sems.at[phase, s, k, 0], recv_sem=sems.at[phase, s, k, 1],
            device_id=(member(s, k)[1],), device_id_type=pl.DeviceIdType.MESH,
        )

    done = []
    cur, size = mine, mine.shape[0]
    for s in range(ns):
        f = sizes[s]
        blk = size // f
        copies = []
        for k in range(1, f):
            d, _ = member(s, k)
            c = send(cur.at[pl.ds(d * blk, blk)], got[s].at[k - 1], s, k, 0)
            c.start()
            copies.append(c)
        acc = cur[pl.ds(digits[s] * blk, blk)]
        for k in range(1, f):
            copies[k - 1].wait_recv()
            acc = acc + got[s][k - 1]
        part[s][...] = acc
        done += copies
        cur, size = part[s], blk
    at = 0
    span = mine.shape[0]
    for s in range(ns):
        span //= sizes[s]
        at = at + digits[s] * span
    full[pl.ds(at, 1)] = part[ns - 1][...]
    span = 1
    for s in reversed(range(ns)):
        copies = []
        for k in range(1, sizes[s]):
            c = send(full.at[pl.ds(at, span)], full.at[pl.ds(at, span)], s, k, 1)
            c.start()
            copies.append(c)
        for c in copies:
            c.wait_recv()
        done += copies
        at = at - digits[s] * span
        span *= sizes[s]
    out[...] = full[...]
    for c in done:
        c.wait_send()


def sum_over_devices(packed, n):
    sizes = split_sizes(n)
    rows = packed.shape[0] // n
    mine = packed.reshape(n, rows, 128)
    got, part, size = [], [], n
    for f in sizes:
        size //= f
        got.append(pltpu.VMEM((f - 1, size, rows, 128), F32))
        part.append(pltpu.VMEM((size, rows, 128), F32))
    vm = pl.BlockSpec(memory_space=pltpu.VMEM)
    out = pl.pallas_call(
        functools.partial(sum_kernel, sizes),
        out_shape=jax.ShapeDtypeStruct((n, rows, 128), F32),
        in_specs=[vm],
        out_specs=vm,
        scratch_shapes=[pltpu.VMEM((n, rows, 128), F32)] + got + part + [pltpu.SemaphoreType.DMA((2, len(sizes), max(sizes), 2))],
        compiler_params=pltpu.CompilerParams(collective_id=1, has_side_effects=True, vmem_limit_bytes=40 << 20),
        name="sum_over_devices",
    )(mine)
    return out.reshape(packed.shape)


def finish_kernel(level_s, g, aw1, ab1, aw2, ab2, aw3, ab3, cw1, cb1, cw2, cb2, cw3, cb3, da, losses, tmp):
    misc = jnp.sum(g[R_MISC : R_MISC + 8, :], axis=1, keepdims=True)
    n = misc[5:6]
    inv = 1.0 / n

    def rows(at, count):
        return jnp.concatenate([g[at : at + count, :], g[at + count : at + 2 * count, :]], axis=1) * inv

    aw2[...] = rows(0, HID)
    cw2[0] = rows(2 * HID, HID)
    cw2[1] = rows(4 * HID, HID)
    w = rows(R_AW1, 24)
    aw1[0:16, :] = w[8:24]
    aw1[16:17, :] = w[7:8]
    ab1[...] = w[6:7]
    for k in range(2):
        w = rows(R_CW1 + 48 * k, 24)
        cw1[k, 0:16, :] = w[8:24]
        cw1[k, 16:17, :] = w[7:8]
        cw1[k, 17:23, :] = w[0:6]
        cb1[k : k + 1, :] = w[6:7]
    w = rows(R_AW3, 16)
    tmp[0:8, :] = w[0:8]
    tmp[6:12, :] = w[8:14]
    aw3[...] = tmp[...].T[:, 0:12]
    c = rows(R_COL, 8)
    cb2[...] = c[0:2]
    cw3[...] = c[2:4]
    ab2[...] = c[4:5]
    ab3[...] = jnp.concatenate([c[5:6, 0:6], c[5:6, 8:14]], axis=1)
    m = misc * inv
    cb3[...] = jnp.concatenate([m[0:1], m[1:2]], axis=1)
    da[...] = -m[4:5]
    losses[...] = jnp.concatenate([m[2:3], m[3:4], -level_s[0] * m[4:5]], axis=1)


def finish(total, level):
    vm = pl.BlockSpec(memory_space=pltpu.VMEM)
    shapes = [
        (OBS, HID), (1, HID), (HID, HID), (1, HID), (HID, 12), (1, 12),
        (2, 23, HID), (2, HID), (2, HID, HID), (2, HID), (2, HID), (1, 2), (1, 1), (1, 3),
    ]
    outs = pl.pallas_call(
        finish_kernel,
        out_shape=[jax.ShapeDtypeStruct(x, F32) for x in shapes],
        in_specs=[pl.BlockSpec(memory_space=pltpu.SMEM), vm],
        out_specs=[vm] * len(shapes),
        scratch_shapes=[pltpu.VMEM((16, HID), F32)],
        name="finish",
    )(level.reshape(1), total)
    final = [(OBS, HID), (HID,), (HID, HID), (HID,), (HID, 12), (12,), (2, 23, HID), (2, HID), (2, HID, HID), (2, HID), (2, HID), (2,), (), (3,)]
    return tuple(o.reshape(x) for o, x in zip(outs, final))


def local_grads(experience_buffer, idx, counts, seeds, params, packed_rows):
    (aw1, ab1, aw2, ab2, aw3, ab3, jw1, jb1, jw2, jb2, jw3, jb3, lw1, lb1, lw2, lb2, lw3, lb3, level) = params
    feats, width = experience_buffer.shape
    peers, cap = idx.shape
    slots = peers * cap
    T = min(TILE, slots)
    vm = pl.BlockSpec(memory_space=pltpu.VMEM)
    sm = pl.BlockSpec(memory_space=pltpu.SMEM)
    return pl.pallas_call(
        functools.partial(net_kernel, cap=cap, width=width, slots=slots),
        out_shape=jax.ShapeDtypeStruct((packed_rows, 128), F32),
        in_specs=[sm] * 6 + [vm] * 17,
        out_specs=vm,
        scratch_shapes=[
            pltpu.VMEM((3, HID, HID), F32),
            pltpu.VMEM((24, HID), F32),
            pltpu.VMEM((2, 24, HID), F32),
            pltpu.VMEM((16, HID), F32),
            pltpu.VMEM((6, HID, 128), F32),
            pltpu.VMEM((8, 128), F32),
            pltpu.VMEM((width, 128), F32),
            pltpu.VMEM((T, 128), F32),
            pltpu.VMEM((5 * HID, 72), BF),
            pltpu.VMEM((5, 2 * HID, HID), BF),
            pltpu.VMEM((3, 2 * HID, HID), BF),
            pltpu.VMEM((32, HID), BF),
            pltpu.VMEM((HID, 32), BF),
            pltpu.VMEM((2, 16, HID), BF),
            pltpu.VMEM((HID, 128), F32),
            pltpu.VMEM((32, HID), F32),
            pltpu.VMEM((16, HID), F32),
        ],
        compiler_params=pltpu.CompilerParams(vmem_limit_bytes=60 << 20),
        name="networks",
    )(
        idx.reshape(-1), counts, level.reshape(1), ab3, jb3, lb3,
        experience_buffer, seeds.reshape(slots // T, T),
        aw1, ab1.reshape(1, HID), aw2, ab2.reshape(1, HID), aw3,
        jw1, jb1, jw2, jb2, jw3,
        lw1, lb1, lw2, lb2, lw3,
    )


def body(experience_buffer, sampled_indices, filled_lengths, randomizer_numbers, *params):
    peers, cap = sampled_indices.shape[1:]
    level = params[-1]
    message = jnp.concatenate(
        [sampled_indices[0], randomizer_numbers[0], jnp.broadcast_to(filled_lengths[0][:, None], (peers, 128))], axis=1
    )
    got = lax.all_to_all(message, "dp", split_axis=0, concat_axis=0, tiled=True)
    idx, seeds, counts = got[:, :cap], got[:, cap : 2 * cap], got[:, 2 * cap]
    packed = local_grads(experience_buffer, idx, counts, seeds, params, peers * 8 * (-(-R_END // (8 * peers))))
    return finish(sum_over_devices(packed, peers), level)


def solution(mesh):
    in_specs = (P(None, "dp"), P("dp", None, None), P("dp", None), P("dp", None, None)) + (P(),) * 19
    return jax.shard_map(body, mesh=mesh, in_specs=in_specs, out_specs=(P(),) * 14, check_vma=False)
```

```python
import functools
import math

import jax
import jax.numpy as jnp
from jax import lax
from jax.experimental import pallas as pl
from jax.experimental.pallas import tpu as pltpu
from jax.sharding import PartitionSpec as P

OBS = 17
ACT = 6
HID = 256
GAMMA = 0.99
PRIME = 65521
TILE = 1024
R_AW1 = 6 * HID
R_CW1 = R_AW1 + 48
R_AW3 = R_CW1 + 96
R_COL = R_AW3 + 32
R_AB3 = R_COL + 16
R_MISC = R_AB3 + 16
R_END = R_MISC + 8
BF = jnp.bfloat16
F32 = jnp.float32


def dot(a, b):
    return jnp.dot(a, b, preferred_element_type=F32)


def dot_t(a, b):
    return lax.dot_general(a, b, (((1,), (1,)), ((), ())), preferred_element_type=F32)


def split(x):
    hi = x.astype(BF).astype(F32)
    return hi, x - hi


def fold_prime(x):
    return (x >> 16) * 15 + (x & 65535)


def below_prime(x):
    return jnp.where(x >= PRIME, x - PRIME, x)


def noise(seeds, rows):
    comp = jnp.where(rows >= 8, rows - 2, rows)
    z = below_prime(fold_prime(seeds))
    h0 = below_prime(fold_prime(z * 257 + comp * 7919 + 1))
    h1 = below_prime(fold_prime(fold_prime(h0 * 32749 + 12345)))
    h2 = below_prime(fold_prime(fold_prime(h1 * 32749 + 54321)))
    u1 = (h1.astype(F32) + 0.5) * (1.0 / PRIME)
    x = jnp.abs((2 * h2 + (1 - PRIME)).astype(F32)) * (math.pi / PRIME) - 0.5 * math.pi
    x2 = x * x
    p = -1.0 / 39916800.0
    for c in (1.0 / 362880.0, -1.0 / 5040.0, 1.0 / 120.0, -1.0 / 6.0, 1.0):
        p = p * x2 + c
    return jnp.sqrt(-2.0 * jnp.log(u1)) * (p * x)


def fold(x):
    return functools.reduce(lambda a, b: a + b, [x[:, k * 128 : (k + 1) * 128] for k in range(x.shape[1] // 128)])


def message_rows(cap):
    return -(-cap // 128)


def prepare_kernel(
    idx_h, seed_h, cnt_h, buf_h, aw2_h, jw2_h, lw2_h,
    aw1, ab1, ab2, aw3, ab3, jw1, jb1, jb2, jw3, jb3, lw1, lb1, lb2, lw3, lb3, level,
    tab, got, idx_s, w1all, f2, b2, head, headb, da_w, qw, col, scale,
    idx_v, seed_v, cnt_v, buf, w2, msg, land, flat, tmp, rowbuf, in_sems, sems,
    *, n, cap,
):
    me = lax.axis_index("dp")
    rows = message_rows(cap)
    part = min(cap, 128)
    width = buf.shape[1]
    loads = [
        pltpu.make_async_copy(src, dst, in_sems.at[k])
        for k, (src, dst) in enumerate(
            ((idx_h, idx_v), (seed_h, seed_v), (cnt_h, cnt_v), (buf_h, buf), (aw2_h, w2.at[0]), (jw2_h, w2.at[pl.ds(1, 2)]), (lw2_h, w2.at[pl.ds(3, 2)]))
        )
    ]
    for c in loads:
        c.start()
    barrier = pltpu.get_barrier_semaphore()

    @pl.loop(1, n)
    def _(k):
        pl.semaphore_signal(barrier, inc=1, device_id=(lax.rem(me + k, n),), device_id_type=pl.DeviceIdType.MESH)

    for c in loads[:3]:
        c.wait()
    msg[...] = jnp.zeros_like(msg)
    for r in range(rows):
        msg[:, r, 0:part] = idx_v[0, :, r * part : (r + 1) * part]
        msg[:, rows + r, 0:part] = seed_v[0, :, r * part : (r + 1) * part]
    diag = lax.broadcasted_iota(jnp.int32, (n, n), 0) == lax.broadcasted_iota(jnp.int32, (n, n), 1)
    counts = jnp.sum(jnp.where(diag, cnt_v[...].astype(F32), 0.0), axis=1, keepdims=True)
    msg[:, 2 * rows, :] = jnp.broadcast_to(counts, (n, 128)).astype(jnp.int32)
    pl.semaphore_wait(barrier, n - 1)

    def copy(k):
        return pltpu.make_async_remote_copy(
            src_ref=msg.at[lax.rem(me + k, n)], dst_ref=land.at[k], send_sem=sems.at[0, k], recv_sem=sems.at[1, k],
            device_id=(lax.rem(me + k, n),), device_id_type=pl.DeviceIdType.MESH,
        )

    @pl.loop(1, n)
    def _(k):
        copy(k).start()

    loads[3].wait()

    @pl.loop(0, width // 128, unroll=4)
    def _(c):
        blk = buf[:, pl.ds(pl.multiple_of(c * 128, 128), 128)]
        tab[pl.ds(pl.multiple_of(c * 128, 128), 128), 0:42] = blk.T

    for c in loads[4:]:
        c.wait()
    for l, (w1, b1, k) in enumerate(((aw1, ab1, None), (jw1, jb1, 0), (jw1, jb1, 1), (lw1, lb1, 0), (lw1, lb1, 1))):
        if k is None:
            tmp[0:6, :] = jnp.zeros((6, HID), F32)
            tmp[6:7, :] = b1[...]
            tmp[7:8, :] = w1[16:17, :]
            tmp[8:24, :] = w1[0:16, :]
        else:
            tmp[0:6, :] = w1[17:23, k, :]
            tmp[6:7, :] = b1[k : k + 1, :]
            tmp[7:8, :] = w1[16:17, k, :]
            tmp[8:24, :] = w1[0:16, k, :]
        hi, lo = split(0.5 * tmp[0:24, :])
        w1all[l * HID : (l + 1) * HID, :] = jnp.concatenate([hi, hi, lo], axis=0).T.astype(BF)
        if l in (1, 2):
            hi, lo = split(tmp[0:8, :])
            da_w[l - 1] = jnp.concatenate([hi, lo], axis=0).astype(BF)
    for l in range(5):
        w = 0.5 * w2[l]
        hi, lo = split(w)
        f2[l, 0:HID, :] = hi.T.astype(BF)
        f2[l, HID:, :] = lo.T.astype(BF)
        if l < 3:
            if l > 0:
                hi, lo = split(w * (0.5 * jw3[l - 1 : l, :]))
            b2[l, 0:HID, :] = hi.astype(BF)
            b2[l, HID:, :] = lo.astype(BF)
    tmp[0:12, :] = aw3[...]
    r8 = lax.broadcasted_iota(jnp.int32, (8, HID), 0)
    w_head = jnp.concatenate([jnp.where(r8 < 6, tmp[0:8, :], 0.0), jnp.where(r8 < 6, tmp[6:14, :], 0.0)], axis=0)
    hi, lo = split(w_head)
    head[...] = jnp.concatenate([hi, lo], axis=0).astype(BF)
    headb[...] = (0.5 * jnp.concatenate([hi, lo], axis=0)).T.astype(BF)
    for k in range(4):
        w3 = jw3[k : k + 1, :] if k < 2 else lw3[k - 2 : k - 1, :]
        hi, lo = split(w3)
        qw[k] = jnp.concatenate([jnp.where(r8 == 0, hi, 0.0), jnp.where(r8 == 0, lo, 0.0)], axis=0).astype(BF)
    rowbuf[...] = jnp.zeros_like(rowbuf)
    rowbuf[0:1, :] = 0.5 * ab2[...]
    rowbuf[1:3, :] = 0.5 * jb2[...]
    rowbuf[3:5, :] = 0.5 * lb2[...]
    lane12 = lax.broadcasted_iota(jnp.int32, (1, HID), 1)
    hb = jnp.zeros((1, HID), F32)
    for k in range(12):
        hb = jnp.where(lane12 == (k if k < 6 else k + 2), ab3[k], hb)
    rowbuf[5:6, :] = hb
    col[...] = rowbuf[...].T
    scale[...] = jnp.zeros_like(scale)
    scale[0:2, :] = 0.5 * jw3[...]

    land[0] = msg[me]

    @pl.loop(1, n)
    def _(k):
        copy(k).wait()

    @pl.loop(0, n)
    def _(k):
        got[lax.rem(me - k + n, n)] = land[k]

    for r in range(rows):
        flat[:, r, :] = got[:, r, :]
    c = pltpu.make_async_copy(flat, idx_s, in_sems.at[0])
    c.start()
    c.wait()


def prepare(experience_buffer, sampled, seeds, counts, params):
    (aw1, ab1, aw2, ab2, aw3, ab3, jw1, jb1, jw2, jb2, jw3, jb3, lw1, lb1, lw2, lb2, lw3, lb3, level) = params
    feats, width = experience_buffer.shape
    _, n, cap = sampled.shape
    rows = message_rows(cap)
    vm = pl.BlockSpec(memory_space=pltpu.VMEM)
    sm = pl.BlockSpec(memory_space=pltpu.SMEM)
    hbm = pl.BlockSpec(memory_space=pl.ANY)
    out = [
        pltpu.VMEM((width, 128), F32),
        pltpu.VMEM((n, 8, 128), jnp.int32),
        pltpu.SMEM((n, rows, 128), jnp.int32),
        pltpu.VMEM((5 * HID, 72), BF),
        pltpu.VMEM((5, 2 * HID, HID), BF),
        pltpu.VMEM((3, 2 * HID, HID), BF),
        pltpu.VMEM((32, HID), BF),
        pltpu.VMEM((HID, 32), BF),
        pltpu.VMEM((2, 16, HID), BF),
        pltpu.VMEM((4, 16, HID), BF),
        pltpu.VMEM((HID, 8), F32),
        pltpu.VMEM((8, HID), F32),
    ]
    return pl.pallas_call(
        functools.partial(prepare_kernel, n=n, cap=cap),
        out_shape=out,
        in_specs=[hbm] * 7 + [vm] * 4 + [sm] + [vm] * 4 + [sm] + [vm] * 4 + [sm] * 2,
        out_specs=[vm, vm, sm] + [vm] * 9,
        scratch_shapes=[
            pltpu.VMEM((1, n, cap), jnp.int32),
            pltpu.VMEM((1, n, cap), jnp.int32),
            pltpu.VMEM((1, n), jnp.int32),
            pltpu.VMEM((feats, width), F32),
            pltpu.VMEM((5, HID, HID), F32),
            pltpu.VMEM((n, 8, 128), jnp.int32),
            pltpu.VMEM((n, 8, 128), jnp.int32),
            pltpu.VMEM((n, rows, 128), jnp.int32),
            pltpu.VMEM((24, HID), F32),
            pltpu.VMEM((8, HID), F32),
            pltpu.SemaphoreType.DMA((7,)),
            pltpu.SemaphoreType.DMA((2, n)),
        ],
        compiler_params=pltpu.CompilerParams(collective_id=2, has_side_effects=True, vmem_limit_bytes=24 << 20),
        name="exchange_and_prepare",
    )(
        sampled, seeds, counts, experience_buffer, aw2, jw2, lw2,
        aw1, ab1.reshape(1, HID), ab2.reshape(1, HID), aw3.T, ab3,
        jw1.transpose(1, 0, 2), jb1, jb2, jw3, jb3, lw1.transpose(1, 0, 2), lb1, lb2, lw3, lb3, level.reshape(1),
    )


def net_kernel(
    idx_s, level_s, jb3_s, lb3_s,
    tab, got, w1all, f2, b2, head, headb, da_w, qw, col, scale,
    packed,
    xrow, gw2, gw2b, gaw1, gcw1, gaw3, gcw3, gcol, gmisc,
    *, cap, slots,
):
    T = min(TILE, slots)
    nt = slots // T
    lists = T // cap
    rows = message_rows(cap)
    part = min(cap, 128)

    def gather(i):
        for t in range(T):
            r = idx_s[i * lists + t // cap, (t % cap) // 128, t % 128]
            xrow[t : t + 1, :] = tab[pl.ds(r, 1), :]

    gather(0)
    for ref in (gw2, gw2b, gaw1, gcw1, gaw3, gcw3, gcol, gmisc):
        ref[...] = jnp.zeros_like(ref)
    level = level_s[0]

    def act(u):
        t = jnp.tanh(u)
        p = 1.0 + t
        h = u * p
        return h.astype(BF), p + h * (2.0 - p)

    def layer2(l, h):
        r = dot(f2[l], h)
        return act(r[:HID] + r[HID:] + col[:, l : l + 1])

    def first(l0, l1, x24):
        hi, lo = split(x24)
        xs = jnp.concatenate([hi, lo, hi], axis=0).astype(BF)
        return dot(w1all[l0 * HID : l1 * HID, :], xs)

    def back2(l, g):
        r = dot(b2[l], g)
        return r[:HID] + r[HID:]

    def head_out(h2):
        r = dot(head[...], h2)
        o = r[0:16] + r[16:32] + col[0:16, 5:6]
        mean = o[0:8]
        t = jnp.tanh(o[8:16])
        ls = -5.0 + 3.5 * (t + 1.0)
        return mean, t, ls

    def sample(mean, ls, e, live):
        sg = jnp.exp(ls)
        u = mean + sg * e
        a = jnp.tanh(u)
        au = jnp.abs(u)
        sq = 2.0 * (math.log(2.0) - au - jnp.log(1.0 + jnp.exp(-2.0 * au)))
        lp = -0.5 * e * e - ls - 0.5 * math.log(2.0 * math.pi) - sq
        return a, sg, jnp.sum(jnp.where(live, lp, 0.0), axis=0, keepdims=True)

    def q_of(k, h2, b):
        r = dot(qw[k], h2)
        return r[0:1] + r[8:9] + b

    def softmin(q, w):
        a, b = -4.0 * q, -4.0 * w
        return -0.25 * (jnp.maximum(a, b) + jnp.log(1.0 + jnp.exp(-jnp.abs(a - b))))

    ones = jnp.ones((16, T), BF)

    @pl.loop(0, nt)
    def _(i):
        xt = xrow[...].T
        gather(jnp.minimum(i + 1, nt - 1))
        row8 = lax.broadcasted_iota(jnp.int32, (8, T), 0)
        row16 = lax.broadcasted_iota(jnp.int32, (16, T), 0)
        live = row8 < ACT
        seeds = jnp.concatenate([got[i * lists + k, rows + r : rows + r + 1, 0:part] for k in range(lists) for r in range(rows)], axis=1)
        lane = lax.broadcasted_iota(jnp.int32, (1, cap), 1)
        mask = jnp.concatenate(
            [jnp.where(lane < got[i * lists + k, 2 * rows : 2 * rows + 1, 0:1], 1.0, 0.0).astype(F32) for k in range(lists)], axis=1
        )
        alpha = jnp.exp(jnp.full((1, T), level, F32))
        b1 = pltpu.roll(xt[16:24], 7, 0)
        reward = b1[6:7]
        xa = jnp.concatenate([jnp.where(row8 == 6, 1.0, b1), xt[0:16]], axis=0)
        b2_ = pltpu.roll(xt[40:48], 7, 0)
        done = b2_[0:1]
        n_lo = jnp.where(row8 == 7, b2_, jnp.where(row8 == 6, 1.0, 0.0))
        xn = jnp.concatenate([n_lo, xt[24:40]], axis=0)

        un = first(0, 1, xn)
        hi, lo = split(xa)
        xw = jnp.concatenate([hi, lo], axis=0).astype(BF)
        ua = dot(w1all[0 : 3 * HID, :], jnp.concatenate([hi, lo, hi], axis=0).astype(BF))
        eps = noise(seeds, row16)
        e = eps[0:8]
        hn, _ = act(un)
        h1a, d1a = act(ua[0:HID])
        h1c, d1c = zip(*[act(ua[(1 + k) * HID : (2 + k) * HID]) for k in range(2)])
        hn, _ = layer2(0, hn)
        mean, _, ls = head_out(hn)
        a2, _, lp2 = sample(mean, ls, eps[8:16], live)
        h2a, d2a = layer2(0, h1a)
        mean, t, ls = head_out(h2a)
        a1, sg, lp = sample(mean, ls, e, live)
        un = first(3, 5, jnp.concatenate([jnp.where(live, a2, n_lo), xt[24:40]], axis=0))
        h2c, d2c = zip(*[layer2(1 + k, h1c[k]) for k in range(2)])
        qc = [q_of(k, h2c[k], jb3_s[k]) for k in range(2)]
        uq = first(1, 3, jnp.concatenate([jnp.where(live, a1, xa[0:8]), xt[0:16]], axis=0))
        ht = [act(un[k * HID : (k + 1) * HID])[0] for k in range(2)]
        ht = [layer2(3 + k, ht[k])[0] for k in range(2)]
        qt = [q_of(2 + k, ht[k], lb3_s[k]) for k in range(2)]
        h1q, d1q = zip(*[act(uq[k * HID : (k + 1) * HID]) for k in range(2)])
        y = reward + GAMMA * (1.0 - done) * (softmin(qt[0], qt[1]) - alpha * lp2)
        h2q, d2q = zip(*[layer2(1 + k, h1q[k]) for k in range(2)])
        qq = [q_of(k, h2q[k], jb3_s[k]) for k in range(2)]

        closs = jnp.zeros((1, T), F32)
        g2c = []
        for k in range(2):
            dq = qc[k] - y
            mdq = dq * mask
            closs = closs + 0.5 * (mdq * dq)
            g2 = (mdq * d2c[k]).astype(BF)
            g2c.append(g2)
            mhi, mlo = split(mdq)
            m16 = jnp.where(row16 == 0, mhi, jnp.where(row16 == 1, mlo, 0.0)).astype(BF)
            gcw3[k] += dot_t(m16, h2c[k])
            r = dot_t(jnp.concatenate([h1c[k], ones], axis=0), g2)
            gw2[1 + k] += r[0:HID]
            gw2b[1 + k] += r[HID : HID + 8]
            gmisc[k : k + 1, :] += fold(mdq)
        sm = softmin(qq[0], qq[1])
        p0 = 1.0 / (1.0 + jnp.exp(4.0 * (qq[0] - qq[1])))
        da = jnp.zeros((8, T), F32)
        for k, pk in enumerate((p0, 1.0 - p0)):
            g2 = ((-pk * mask) * d2q[k]).astype(BF)
            g1 = (back2(1 + k, g2) * d1q[k]).astype(BF)
            w = dot(da_w[k], g1)
            da = da + w[0:8] + w[8:16]
        for k in range(2):
            g1 = (back2(1 + k, g2c[k]) * d1c[k]).astype(BF)
            w = dot_t(xw, g1)
            gcw1[k] += w[0:24] + w[24:48]
        ma = mask * alpha
        du = da * (1.0 - a1 * a1) + ma * (2.0 * a1)
        dls = (du * sg * e - ma) * (3.5 * (1.0 - t * t))
        do = jnp.concatenate([jnp.where(live, du, 0.0), jnp.where(live, dls, 0.0)], axis=0)
        gcol[...] += fold(do)
        dob = do.astype(BF)
        gaw3[...] += dot_t(dob, h2a)
        g2 = (dot(headb[...], jnp.concatenate([dob, dob], axis=0)) * d2a).astype(BF)
        r = dot_t(jnp.concatenate([h1a, ones], axis=0), g2)
        gw2[0] += r[0:HID]
        gw2b[0] += r[HID : HID + 8]
        g1 = (back2(0, g2) * d1a).astype(BF)
        w = dot_t(xw, g1)
        gaw1[...] += w[0:24] + w[24:48]
        gmisc[2:3, :] += fold(closs)
        gmisc[3:4, :] += fold(mask * (alpha * lp - sm))
        gmisc[4:5, :] += fold(mask * (lp - 6.0))
        gmisc[5:6, :] += fold(mask)

    row8 = lax.broadcasted_iota(jnp.int32, (8, HID), 0)
    cols = jnp.zeros((8, HID), F32)
    for k in range(2):
        s = scale[k : k + 1, :]
        cols = jnp.where(row8 == k, gw2b[1 + k] * s, cols)
        cols = jnp.where(row8 == 2 + k, gcw3[k, 0:1, :] + gcw3[k, 1:2, :], cols)
    cols = jnp.where(row8 == 4, gw2b[0], cols)
    for m in range(3):
        for h in range(2):
            w = gw2[m, :, h * 128 : (h + 1) * 128]
            if m > 0:
                w = w * scale[m - 1 : m, h * 128 : (h + 1) * 128]
            packed[(2 * m + h) * HID : (2 * m + h + 1) * HID, :] = w
    for h in range(2):
        packed[R_AW1 + 24 * h : R_AW1 + 24 * (h + 1), :] = gaw1[:, h * 128 : (h + 1) * 128]
        for k in range(2):
            at = R_CW1 + 48 * k + 24 * h
            packed[at : at + 24, :] = gcw1[k, :, h * 128 : (h + 1) * 128]
        packed[R_AW3 + 16 * h : R_AW3 + 16 * (h + 1), :] = gaw3[:, h * 128 : (h + 1) * 128]
        packed[R_COL + 8 * h : R_COL + 8 * (h + 1), :] = cols[:, h * 128 : (h + 1) * 128]
    packed[R_AB3 : R_AB3 + 16, :] = gcol[...]
    packed[R_MISC : R_MISC + 8, :] = gmisc[...]
    packed[R_END:, :] = jnp.zeros((packed.shape[0] - R_END, 128), F32)


def local_grads(ready, params, n, cap, packed_rows):
    tab, got, idx_s, *weights = ready
    jb3, lb3, level = params[11], params[17], params[18]
    slots = n * cap
    T = min(TILE, slots)
    vm = pl.BlockSpec(memory_space=pltpu.VMEM)
    sm = pl.BlockSpec(memory_space=pltpu.SMEM)
    return pl.pallas_call(
        functools.partial(net_kernel, cap=cap, slots=slots),
        out_shape=pltpu.VMEM((packed_rows, 128), F32),
        in_specs=[sm] * 4 + [vm] * (2 + len(weights)),
        out_specs=vm,
        scratch_shapes=[
            pltpu.VMEM((T, 128), F32),
            pltpu.VMEM((3, HID, HID), F32),
            pltpu.VMEM((3, 8, HID), F32),
            pltpu.VMEM((24, HID), F32),
            pltpu.VMEM((2, 24, HID), F32),
            pltpu.VMEM((16, HID), F32),
            pltpu.VMEM((2, 16, HID), F32),
            pltpu.VMEM((16, 128), F32),
            pltpu.VMEM((8, 128), F32),
        ],
        compiler_params=pltpu.CompilerParams(vmem_limit_bytes=40 << 20),
        name="networks",
    )(idx_s, level.reshape(1), jb3, lb3, tab, got, *weights)


def split_sizes(n):
    sizes = [2]
    n //= 2
    while n > 1:
        f = 4 if n % 4 == 0 else n if n < 4 else 2
        sizes.append(f)
        n //= f
    return sizes


def sum_kernel(sizes, mine, out, full, *rest):
    ns = len(sizes)
    got, part, sems = rest[:ns], rest[ns : 2 * ns], rest[2 * ns]
    me = lax.axis_index("dp")
    digits, strides, st = [], [], 1
    for f in sizes:
        digits.append(lax.rem(me // st, f))
        strides.append(st)
        st *= f

    def member(s, k):
        d = lax.rem(digits[s] + k, sizes[s])
        return d, me + (d - digits[s]) * strides[s]

    barrier = pltpu.get_barrier_semaphore()
    count = 0
    for s in range(ns):
        for k in range(1, sizes[s]):
            pl.semaphore_signal(barrier, inc=1, device_id=(member(s, k)[1],), device_id_type=pl.DeviceIdType.MESH)
            count += 1
    pl.semaphore_wait(barrier, count)

    def send(src, dst, s, k, phase):
        return pltpu.make_async_remote_copy(
            src_ref=src, dst_ref=dst, send_sem=sems.at[phase, s, k, 0], recv_sem=sems.at[phase, s, k, 1],
            device_id=(member(s, k)[1],), device_id_type=pl.DeviceIdType.MESH,
        )

    done = []
    cur, size = mine, mine.shape[0]
    for s in range(ns):
        f = sizes[s]
        blk = size // f
        copies = []
        for k in range(1, f):
            d, _ = member(s, k)
            c = send(cur.at[pl.ds(d * blk, blk)], got[s].at[k - 1], s, k, 0)
            c.start()
            copies.append(c)
        acc = cur[pl.ds(digits[s] * blk, blk)]
        for k in range(1, f):
            copies[k - 1].wait_recv()
            acc = acc + got[s][k - 1]
        part[s][...] = acc
        done += copies
        cur, size = part[s], blk
    at = 0
    span = mine.shape[0]
    for s in range(ns):
        span //= sizes[s]
        at = at + digits[s] * span
    full[pl.ds(at, 1)] = part[ns - 1][...]
    span = 1
    for s in reversed(range(ns)):
        copies = []
        for k in range(1, sizes[s]):
            c = send(full.at[pl.ds(at, span)], full.at[pl.ds(at, span)], s, k, 1)
            c.start()
            copies.append(c)
        for c in copies:
            c.wait_recv()
        done += copies
        at = at - digits[s] * span
        span *= sizes[s]
    out[...] = full[...]
    for c in done:
        c.wait_send()


def sum_over_devices(packed, n):
    sizes = split_sizes(n)
    rows = packed.shape[0] // n
    mine = packed.reshape(n, rows, 128)
    got, part, size = [], [], n
    for f in sizes:
        size //= f
        got.append(pltpu.VMEM((f - 1, size, rows, 128), F32))
        part.append(pltpu.VMEM((size, rows, 128), F32))
    vm = pl.BlockSpec(memory_space=pltpu.VMEM)
    out = pl.pallas_call(
        functools.partial(sum_kernel, sizes),
        out_shape=pltpu.VMEM((n, rows, 128), F32),
        in_specs=[vm],
        out_specs=vm,
        scratch_shapes=[pltpu.VMEM((n, rows, 128), F32)] + got + part + [pltpu.SemaphoreType.DMA((2, len(sizes), max(sizes), 2))],
        compiler_params=pltpu.CompilerParams(collective_id=1, has_side_effects=True, vmem_limit_bytes=24 << 20),
        name="sum_over_devices",
    )(mine)
    return out.reshape(packed.shape)


def finish_kernel(level_s, g, aw1, ab1, aw2, ab2, aw3, ab3, cw1, cb1, cw2, cb2, cw3, cb3, da, losses):
    misc = jnp.sum(g[R_MISC : R_MISC + 8, :], axis=1, keepdims=True)
    n = misc[5:6]
    inv = 1.0 / n

    def rows(at, count):
        return jnp.concatenate([g[at : at + count, :], g[at + count : at + 2 * count, :]], axis=1) * inv

    aw2[...] = rows(0, HID)
    cw2[0] = rows(2 * HID, HID)
    cw2[1] = rows(4 * HID, HID)
    w = rows(R_AW1, 24)
    aw1[0:16, :] = w[8:24]
    aw1[16:17, :] = w[7:8]
    ab1[...] = w[6:7]
    for k in range(2):
        w = rows(R_CW1 + 48 * k, 24)
        cw1[0:16, k, :] = w[8:24]
        cw1[16:17, k, :] = w[7:8]
        cw1[17:23, k, :] = w[0:6]
        cb1[k : k + 1, :] = w[6:7]
    w = rows(R_AW3, 16)
    aw3[0:6, :] = w[0:6]
    aw3[6:12, :] = w[8:14]
    c = rows(R_COL, 8)
    cb2[...] = c[0:2]
    cw3[...] = c[2:4]
    ab2[...] = c[4:5]
    b = jnp.sum(g[R_AB3 : R_AB3 + 16, :], axis=1, keepdims=True) * inv
    diag = lax.broadcasted_iota(jnp.int32, (16, 128), 0) == lax.broadcasted_iota(jnp.int32, (16, 128), 1)
    b = jnp.sum(jnp.where(diag, b, 0.0), axis=0, keepdims=True)
    ab3[...] = jnp.concatenate([b[:, 0:6], b[:, 8:14]], axis=1)
    m = misc * inv
    cb3[...] = jnp.concatenate([m[0:1], m[1:2]], axis=1)
    da[...] = -m[4:5]
    losses[...] = jnp.concatenate([m[2:3], m[3:4], -level_s[0] * m[4:5]], axis=1)


def finish(total, level):
    vm = pl.BlockSpec(memory_space=pltpu.VMEM)
    shapes = [
        (OBS, HID), (1, HID), (HID, HID), (1, HID), (12, HID), (1, 12),
        (23, 2, HID), (2, HID), (2, HID, HID), (2, HID), (2, HID), (1, 2), (1, 1), (1, 3),
    ]
    outs = list(pl.pallas_call(
        finish_kernel,
        out_shape=[jax.ShapeDtypeStruct(x, F32) for x in shapes],
        in_specs=[pl.BlockSpec(memory_space=pltpu.SMEM), vm],
        out_specs=[vm] * len(shapes),
        name="finish",
    )(level.reshape(1), total))
    outs[4] = outs[4].T
    outs[6] = outs[6].transpose(1, 0, 2)
    for k, shape in ((1, (HID,)), (3, (HID,)), (5, (12,)), (11, (2,)), (12, ()), (13, (3,))):
        outs[k] = outs[k].reshape(shape)
    return tuple(outs)


def body(experience_buffer, sampled_indices, filled_lengths, randomizer_numbers, *params):
    n, cap = sampled_indices.shape[1:]
    ready = prepare(experience_buffer, sampled_indices, randomizer_numbers, filled_lengths, params)
    packed = local_grads(ready, params, n, cap, n * 8 * (-(-R_END // (8 * n))))
    return finish(sum_over_devices(packed, n), params[-1])


def solution(mesh):
    in_specs = (P(None, "dp"), P("dp", None, None), P("dp", None), P("dp", None, None)) + (P(),) * 19
    return jax.shard_map(body, mesh=mesh, in_specs=in_specs, out_specs=(P(),) * 14, check_vma=False)
```

```python
import functools
import math

import jax
import jax.numpy as jnp
from jax import lax
from jax.experimental import pallas as pl
from jax.experimental.pallas import tpu as pltpu
from jax.sharding import PartitionSpec as P

OBS = 17
ACT = 6
HID = 256
GAMMA = 0.99
PRIME = 65521
TILE = 1024
CHUNKS = 4
R_AW1 = 6 * HID
R_CW1 = R_AW1 + 48
R_AW3 = R_CW1 + 96
R_COL = R_AW3 + 32
R_AB3 = R_COL + 16
R_MISC = R_AB3 + 16
R_END = R_MISC + 8
BF = jnp.bfloat16
F32 = jnp.float32


def dot(a, b):
    return jnp.dot(a, b, preferred_element_type=F32)


def dot_t(a, b):
    return lax.dot_general(a, b, (((1,), (1,)), ((), ())), preferred_element_type=F32)


def split(x):
    hi = x.astype(BF).astype(F32)
    return hi, x - hi


def fold_prime(x):
    return (x >> 16) * 15 + (x & 65535)


def below_prime(x):
    return jnp.where(x >= PRIME, x - PRIME, x)


def noise(seeds, rows):
    comp = jnp.where(rows >= 8, rows - 2, rows)
    z = below_prime(fold_prime(seeds))
    h0 = below_prime(fold_prime(z * 257 + comp * 7919 + 1))
    h1 = below_prime(fold_prime(fold_prime(h0 * 32749 + 12345)))
    h2 = below_prime(fold_prime(fold_prime(h1 * 32749 + 54321)))
    u1 = (h1.astype(F32) + 0.5) * (1.0 / PRIME)
    x = jnp.abs((2 * h2 + (1 - PRIME)).astype(F32)) * (math.pi / PRIME) - 0.5 * math.pi
    x2 = x * x
    p = -1.0 / 39916800.0
    for c in (1.0 / 362880.0, -1.0 / 5040.0, 1.0 / 120.0, -1.0 / 6.0, 1.0):
        p = p * x2 + c
    return jnp.sqrt(-2.0 * jnp.log(u1)) * (p * x)


def fold(x):
    return functools.reduce(lambda a, b: a + b, [x[:, k * 128 : (k + 1) * 128] for k in range(x.shape[1] // 128)])


def message_rows(cap):
    return -(-cap // 128)


def prepare_kernel(
    idx_h, seed_h, cnt_h, buf_h, aw2_h, jw2_h, lw2_h,
    aw1_h, ab1_h, ab2_h, aw3_h, jw1_h, jb1_h, jb2_h, jw3_h, lw1_h, lb1_h, lb2_h, lw3_h,
    ab3_h, jb3_h, lb3_h, level,
    tab, got, idx_s, w1all, f2, b2, head, headb, da_w, qw, col, scale, scal,
    idx_v, seed_v, cnt_v, buf, w2, aw1, ab1, ab2, aw3, jw1, jb1, jb2, jw3, lw1, lb1, lb2, lw3,
    ab3, jb3, lb3, msg, land, flat, tmp, rowbuf, in_sems, sems,
    *, n, cap,
):
    me = lax.axis_index("dp")
    rows = message_rows(cap)
    part = min(cap, 128)
    width = buf.shape[1]
    pairs = (
        (idx_h, idx_v), (seed_h, seed_v), (cnt_h, cnt_v), (buf_h, buf),
        (aw2_h, w2.at[0]), (jw2_h, w2.at[pl.ds(1, 2)]), (lw2_h, w2.at[pl.ds(3, 2)]),
        (aw1_h, aw1), (ab1_h, ab1), (ab2_h, ab2), (aw3_h, aw3), (jw1_h, jw1), (jb1_h, jb1), (jb2_h, jb2),
        (jw3_h, jw3), (lw1_h, lw1), (lb1_h, lb1), (lb2_h, lb2), (lw3_h, lw3),
        (ab3_h, ab3), (jb3_h, jb3), (lb3_h, lb3),
    )
    loads = [pltpu.make_async_copy(src, dst, in_sems.at[k]) for k, (src, dst) in enumerate(pairs)]
    for c in loads:
        c.start()
    barrier = pltpu.get_barrier_semaphore()

    @pl.loop(1, n)
    def _(k):
        pl.semaphore_signal(barrier, inc=1, device_id=(lax.rem(me + k, n),), device_id_type=pl.DeviceIdType.MESH)

    for c in loads[:3]:
        c.wait()
    msg[...] = jnp.zeros_like(msg)
    for r in range(rows):
        msg[:, r, 0:part] = idx_v[0, :, r * part : (r + 1) * part]
        msg[:, rows + r, 0:part] = seed_v[0, :, r * part : (r + 1) * part]
    diag = lax.broadcasted_iota(jnp.int32, (n, n), 0) == lax.broadcasted_iota(jnp.int32, (n, n), 1)
    counts = jnp.sum(jnp.where(diag, cnt_v[...].astype(F32), 0.0), axis=1, keepdims=True)
    msg[:, 2 * rows, :] = jnp.broadcast_to(counts, (n, 128)).astype(jnp.int32)
    pl.semaphore_wait(barrier, n - 1)

    def copy(k):
        return pltpu.make_async_remote_copy(
            src_ref=msg.at[lax.rem(me + k, n)], dst_ref=land.at[k], send_sem=sems.at[0, k], recv_sem=sems.at[1, k],
            device_id=(lax.rem(me + k, n),), device_id_type=pl.DeviceIdType.MESH,
        )

    @pl.loop(1, n)
    def _(k):
        copy(k).start()

    loads[3].wait()

    @pl.loop(0, width // 128, unroll=4)
    def _(c):
        blk = buf[:, pl.ds(pl.multiple_of(c * 128, 128), 128)]
        tab[pl.ds(pl.multiple_of(c * 128, 128), 128), 0:42] = blk.T

    for c in loads[4:]:
        c.wait()
    for l, (w1, b1, k) in enumerate(((aw1, ab1, None), (jw1, jb1, 0), (jw1, jb1, 1), (lw1, lb1, 0), (lw1, lb1, 1))):
        if k is None:
            tmp[0:6, :] = jnp.zeros((6, HID), F32)
            tmp[6:7, :] = b1[...]
            tmp[7:8, :] = w1[16:17, :]
            tmp[8:24, :] = w1[0:16, :]
        else:
            tmp[0:6, :] = w1[17:23, k, :]
            tmp[6:7, :] = b1[k : k + 1, :]
            tmp[7:8, :] = w1[16:17, k, :]
            tmp[8:24, :] = w1[0:16, k, :]
        hi, lo = split(0.5 * tmp[0:24, :])
        w1all[l * HID : (l + 1) * HID, :] = jnp.concatenate([hi, hi, lo], axis=0).T.astype(BF)
        if l in (1, 2):
            hi, lo = split(tmp[0:8, :])
            da_w[l - 1] = jnp.concatenate([hi, lo], axis=0).astype(BF)
    for l in range(5):
        w = 0.5 * w2[l]
        hi, lo = split(w)
        f2[l, 0:HID, :] = hi.T.astype(BF)
        f2[l, HID:, :] = lo.T.astype(BF)
        if l < 3:
            if l > 0:
                hi, lo = split(w * (0.5 * jw3[l - 1 : l, :]))
            b2[l, 0:HID, :] = hi.astype(BF)
            b2[l, HID:, :] = lo.astype(BF)
    tmp[0:12, :] = aw3[...]
    r8 = lax.broadcasted_iota(jnp.int32, (8, HID), 0)
    w_head = jnp.concatenate([jnp.where(r8 < 6, tmp[0:8, :], 0.0), jnp.where(r8 < 6, tmp[6:14, :], 0.0)], axis=0)
    hi, lo = split(w_head)
    head[...] = jnp.concatenate([hi, lo], axis=0).astype(BF)
    headb[...] = (0.5 * jnp.concatenate([hi, lo], axis=0)).T.astype(BF)
    for k in range(4):
        w3 = jw3[k : k + 1, :] if k < 2 else lw3[k - 2 : k - 1, :]
        hi, lo = split(w3)
        qw[k] = jnp.concatenate([jnp.where(r8 == 0, hi, 0.0), jnp.where(r8 == 0, lo, 0.0)], axis=0).astype(BF)
    rowbuf[...] = jnp.zeros_like(rowbuf)
    rowbuf[0:1, :] = 0.5 * ab2[...]
    rowbuf[1:3, :] = 0.5 * jb2[...]
    rowbuf[3:5, :] = 0.5 * lb2[...]
    lane12 = lax.broadcasted_iota(jnp.int32, (1, HID), 1)
    hb = jnp.zeros((1, HID), F32)
    for k in range(12):
        hb = jnp.where(lane12 == (k if k < 6 else k + 2), ab3[k], hb)
    rowbuf[5:6, :] = hb
    col[...] = rowbuf[...].T
    scale[...] = jnp.zeros_like(scale)
    scale[0:2, :] = 0.5 * jw3[...]
    for k in range(2):
        scal[k] = jb3[k]
        scal[2 + k] = lb3[k]
    scal[4] = level[0]

    land[0] = msg[me]

    @pl.loop(1, n)
    def _(k):
        copy(k).wait()

    @pl.loop(0, n)
    def _(k):
        got[lax.rem(me - k + n, n)] = land[k]

    for r in range(rows):
        flat[:, r, :] = got[:, r, :]
    c = pltpu.make_async_copy(flat, idx_s, in_sems.at[0])
    c.start()
    c.wait()


def prepare(experience_buffer, sampled, seeds, counts, params):
    (aw1, ab1, aw2, ab2, aw3, ab3, jw1, jb1, jw2, jb2, jw3, jb3, lw1, lb1, lw2, lb2, lw3, lb3, level) = params
    feats, width = experience_buffer.shape
    _, n, cap = sampled.shape
    rows = message_rows(cap)
    vm = pl.BlockSpec(memory_space=pltpu.VMEM)
    sm = pl.BlockSpec(memory_space=pltpu.SMEM)
    hbm = pl.BlockSpec(memory_space=pl.ANY)
    out = [
        pltpu.VMEM((width, 128), F32),
        pltpu.VMEM((n, 8, 128), jnp.int32),
        pltpu.SMEM((n, rows, 128), jnp.int32),
        pltpu.VMEM((5 * HID, 72), BF),
        pltpu.VMEM((5, 2 * HID, HID), BF),
        pltpu.VMEM((3, 2 * HID, HID), BF),
        pltpu.VMEM((32, HID), BF),
        pltpu.VMEM((HID, 32), BF),
        pltpu.VMEM((2, 16, HID), BF),
        pltpu.VMEM((4, 16, HID), BF),
        pltpu.VMEM((HID, 8), F32),
        pltpu.VMEM((8, HID), F32),
        pltpu.SMEM((8,), F32),
    ]
    return pl.pallas_call(
        functools.partial(prepare_kernel, n=n, cap=cap),
        out_shape=out,
        in_specs=[hbm] * 22 + [sm],
        out_specs=[vm, vm, sm] + [vm] * 9 + [sm],
        scratch_shapes=[
            pltpu.VMEM((1, n, cap), jnp.int32),
            pltpu.VMEM((1, n, cap), jnp.int32),
            pltpu.VMEM((1, n), jnp.int32),
            pltpu.VMEM((feats, width), F32),
            pltpu.VMEM((5, HID, HID), F32),
            pltpu.VMEM((OBS, HID), F32),
            pltpu.VMEM((1, HID), F32),
            pltpu.VMEM((1, HID), F32),
            pltpu.VMEM((12, HID), F32),
            pltpu.VMEM((23, 2, HID), F32),
            pltpu.VMEM((2, HID), F32),
            pltpu.VMEM((2, HID), F32),
            pltpu.VMEM((2, HID), F32),
            pltpu.VMEM((23, 2, HID), F32),
            pltpu.VMEM((2, HID), F32),
            pltpu.VMEM((2, HID), F32),
            pltpu.VMEM((2, HID), F32),
            pltpu.SMEM((12,), F32),
            pltpu.SMEM((2,), F32),
            pltpu.SMEM((2,), F32),
            pltpu.VMEM((n, 8, 128), jnp.int32),
            pltpu.VMEM((n, 8, 128), jnp.int32),
            pltpu.VMEM((n, rows, 128), jnp.int32),
            pltpu.VMEM((24, HID), F32),
            pltpu.VMEM((8, HID), F32),
            pltpu.SemaphoreType.DMA((22,)),
            pltpu.SemaphoreType.DMA((2, n)),
        ],
        compiler_params=pltpu.CompilerParams(collective_id=2, has_side_effects=True, vmem_limit_bytes=24 << 20),
        name="exchange_and_prepare",
    )(
        *[
            pltpu.with_memory_space_constraint(x, pltpu.HBM)
            for x in (
                sampled, seeds, counts, experience_buffer, aw2, jw2, lw2,
                aw1, ab1.reshape(1, HID), ab2.reshape(1, HID), aw3.T,
                jw1.transpose(1, 0, 2), jb1, jb2, jw3, lw1.transpose(1, 0, 2), lb1, lb2, lw3,
                ab3, jb3, lb3,
            )
        ],
        level.reshape(1),
    )


def net_kernel(
    idx_s, scal, tab, got, w1all, f2, b2, head, headb, da_w, qw, col, scale,
    packed,
    xrow, gw2, gw2b, gaw1, gcw1, gaw3, gcw3, gcol, gmisc,
    *, cap, slots,
):
    T = min(TILE, slots)
    nt = slots // T
    lists = T // cap
    rows = message_rows(cap)
    part = min(cap, 128)

    def gather(i):
        for t in range(T):
            r = idx_s[i * lists + t // cap, (t % cap) // 128, t % 128]
            xrow[t : t + 1, :] = tab[pl.ds(r, 1), :]

    gather(0)
    for ref in (gw2, gw2b, gaw1, gcw1, gaw3, gcw3, gcol, gmisc):
        ref[...] = jnp.zeros_like(ref)
    level = scal[4]
    jb3_s = (scal[0], scal[1])
    lb3_s = (scal[2], scal[3])

    def act(u):
        t = jnp.tanh(u)
        p = 1.0 + t
        h = u * p
        return h.astype(BF), p + h * (2.0 - p)

    def layer2(l, h):
        r = dot(f2[l], h)
        return act(r[:HID] + r[HID:] + col[:, l : l + 1])

    def first(l0, l1, x24):
        hi, lo = split(x24)
        xs = jnp.concatenate([hi, lo, hi], axis=0).astype(BF)
        return dot(w1all[l0 * HID : l1 * HID, :], xs)

    def back2(l, g):
        r = dot(b2[l], g)
        return r[:HID] + r[HID:]

    def head_out(h2):
        r = dot(head[...], h2)
        o = r[0:16] + r[16:32] + col[0:16, 5:6]
        mean = o[0:8]
        t = jnp.tanh(o[8:16])
        ls = -5.0 + 3.5 * (t + 1.0)
        return mean, t, ls

    def sample(mean, ls, e, live):
        sg = jnp.exp(ls)
        u = mean + sg * e
        a = jnp.tanh(u)
        au = jnp.abs(u)
        sq = 2.0 * (math.log(2.0) - au - jnp.log(1.0 + jnp.exp(-2.0 * au)))
        lp = -0.5 * e * e - ls - 0.5 * math.log(2.0 * math.pi) - sq
        return a, sg, jnp.sum(jnp.where(live, lp, 0.0), axis=0, keepdims=True)

    def q_of(k, h2, b):
        r = dot(qw[k], h2)
        return r[0:1] + r[8:9] + b

    def softmin(q, w):
        a, b = -4.0 * q, -4.0 * w
        return -0.25 * (jnp.maximum(a, b) + jnp.log(1.0 + jnp.exp(-jnp.abs(a - b))))

    ones = jnp.ones((16, T), BF)

    @pl.loop(0, nt)
    def _(i):
        xt = xrow[...].T
        gather(jnp.minimum(i + 1, nt - 1))
        row8 = lax.broadcasted_iota(jnp.int32, (8, T), 0)
        row16 = lax.broadcasted_iota(jnp.int32, (16, T), 0)
        live = row8 < ACT
        seeds = jnp.concatenate([got[i * lists + k, rows + r : rows + r + 1, 0:part] for k in range(lists) for r in range(rows)], axis=1)
        lane = lax.broadcasted_iota(jnp.int32, (1, cap), 1)
        mask = jnp.concatenate(
            [jnp.where(lane < got[i * lists + k, 2 * rows : 2 * rows + 1, 0:1], 1.0, 0.0).astype(F32) for k in range(lists)], axis=1
        )
        alpha = jnp.exp(jnp.full((1, T), level, F32))
        b1 = pltpu.roll(xt[16:24], 7, 0)
        reward = b1[6:7]
        xa = jnp.concatenate([jnp.where(row8 == 6, 1.0, b1), xt[0:16]], axis=0)
        b2_ = pltpu.roll(xt[40:48], 7, 0)
        done = b2_[0:1]
        n_lo = jnp.where(row8 == 7, b2_, jnp.where(row8 == 6, 1.0, 0.0))
        xn = jnp.concatenate([n_lo, xt[24:40]], axis=0)

        un = first(0, 1, xn)
        hi, lo = split(xa)
        xw = jnp.concatenate([hi, lo], axis=0).astype(BF)
        ua = dot(w1all[0 : 3 * HID, :], jnp.concatenate([hi, lo, hi], axis=0).astype(BF))
        eps = noise(seeds, row16)
        e = eps[0:8]
        hn, _ = act(un)
        h1a, d1a = act(ua[0:HID])
        h1c, d1c = zip(*[act(ua[(1 + k) * HID : (2 + k) * HID]) for k in range(2)])
        hn, _ = layer2(0, hn)
        mean, _, ls = head_out(hn)
        a2, _, lp2 = sample(mean, ls, eps[8:16], live)
        h2a, d2a = layer2(0, h1a)
        mean, t, ls = head_out(h2a)
        a1, sg, lp = sample(mean, ls, e, live)
        un = first(3, 5, jnp.concatenate([jnp.where(live, a2, n_lo), xt[24:40]], axis=0))
        h2c, d2c = zip(*[layer2(1 + k, h1c[k]) for k in range(2)])
        qc = [q_of(k, h2c[k], jb3_s[k]) for k in range(2)]
        uq = first(1, 3, jnp.concatenate([jnp.where(live, a1, xa[0:8]), xt[0:16]], axis=0))
        ht = [act(un[k * HID : (k + 1) * HID])[0] for k in range(2)]
        ht = [layer2(3 + k, ht[k])[0] for k in range(2)]
        qt = [q_of(2 + k, ht[k], lb3_s[k]) for k in range(2)]
        h1q, d1q = zip(*[act(uq[k * HID : (k + 1) * HID]) for k in range(2)])
        y = reward + GAMMA * (1.0 - done) * (softmin(qt[0], qt[1]) - alpha * lp2)
        h2q, d2q = zip(*[layer2(1 + k, h1q[k]) for k in range(2)])
        qq = [q_of(k, h2q[k], jb3_s[k]) for k in range(2)]

        closs = jnp.zeros((1, T), F32)
        g2c = []
        for k in range(2):
            dq = qc[k] - y
            mdq = dq * mask
            closs = closs + 0.5 * (mdq * dq)
            g2 = (mdq * d2c[k]).astype(BF)
            g2c.append(g2)
            mhi, mlo = split(mdq)
            m16 = jnp.where(row16 == 0, mhi, jnp.where(row16 == 1, mlo, 0.0)).astype(BF)
            gcw3[k] += dot_t(m16, h2c[k])
            r = dot_t(jnp.concatenate([h1c[k], ones], axis=0), g2)
            gw2[1 + k] += r[0:HID]
            gw2b[1 + k] += r[HID : HID + 8]
            gmisc[k : k + 1, :] += fold(mdq)
        sm = softmin(qq[0], qq[1])
        p0 = 1.0 / (1.0 + jnp.exp(4.0 * (qq[0] - qq[1])))
        da = jnp.zeros((8, T), F32)
        for k, pk in enumerate((p0, 1.0 - p0)):
            g2 = ((-pk * mask) * d2q[k]).astype(BF)
            g1 = (back2(1 + k, g2) * d1q[k]).astype(BF)
            w = dot(da_w[k], g1)
            da = da + w[0:8] + w[8:16]
        for k in range(2):
            g1 = (back2(1 + k, g2c[k]) * d1c[k]).astype(BF)
            w = dot_t(xw, g1)
            gcw1[k] += w[0:24] + w[24:48]
        ma = mask * alpha
        du = da * (1.0 - a1 * a1) + ma * (2.0 * a1)
        dls = (du * sg * e - ma) * (3.5 * (1.0 - t * t))
        do = jnp.concatenate([jnp.where(live, du, 0.0), jnp.where(live, dls, 0.0)], axis=0)
        gcol[...] += fold(do)
        dob = do.astype(BF)
        gaw3[...] += dot_t(dob, h2a)
        g2 = (dot(headb[...], jnp.concatenate([dob, dob], axis=0)) * d2a).astype(BF)
        r = dot_t(jnp.concatenate([h1a, ones], axis=0), g2)
        gw2[0] += r[0:HID]
        gw2b[0] += r[HID : HID + 8]
        g1 = (back2(0, g2) * d1a).astype(BF)
        w = dot_t(xw, g1)
        gaw1[...] += w[0:24] + w[24:48]
        gmisc[2:3, :] += fold(closs)
        gmisc[3:4, :] += fold(mask * (alpha * lp - sm))
        gmisc[4:5, :] += fold(mask * (lp - 6.0))
        gmisc[5:6, :] += fold(mask)

    row8 = lax.broadcasted_iota(jnp.int32, (8, HID), 0)
    cols = jnp.zeros((8, HID), F32)
    for k in range(2):
        s = scale[k : k + 1, :]
        cols = jnp.where(row8 == k, gw2b[1 + k] * s, cols)
        cols = jnp.where(row8 == 2 + k, gcw3[k, 0:1, :] + gcw3[k, 1:2, :], cols)
    cols = jnp.where(row8 == 4, gw2b[0], cols)
    for m in range(3):
        for h in range(2):
            w = gw2[m, :, h * 128 : (h + 1) * 128]
            if m > 0:
                w = w * scale[m - 1 : m, h * 128 : (h + 1) * 128]
            packed[(2 * m + h) * HID : (2 * m + h + 1) * HID, :] = w
    for h in range(2):
        packed[R_AW1 + 24 * h : R_AW1 + 24 * (h + 1), :] = gaw1[:, h * 128 : (h + 1) * 128]
        for k in range(2):
            at = R_CW1 + 48 * k + 24 * h
            packed[at : at + 24, :] = gcw1[k, :, h * 128 : (h + 1) * 128]
        packed[R_AW3 + 16 * h : R_AW3 + 16 * (h + 1), :] = gaw3[:, h * 128 : (h + 1) * 128]
        packed[R_COL + 8 * h : R_COL + 8 * (h + 1), :] = cols[:, h * 128 : (h + 1) * 128]
    packed[R_AB3 : R_AB3 + 16, :] = gcol[...]
    packed[R_MISC : R_MISC + 8, :] = gmisc[...]
    packed[R_END:, :] = jnp.zeros((packed.shape[0] - R_END, 128), F32)


def local_grads(ready, n, cap, packed_rows):
    tab, got, idx_s, *weights, scal = ready
    slots = n * cap
    T = min(TILE, slots)
    vm = pl.BlockSpec(memory_space=pltpu.VMEM)
    sm = pl.BlockSpec(memory_space=pltpu.SMEM)
    return pl.pallas_call(
        functools.partial(net_kernel, cap=cap, slots=slots),
        out_shape=pltpu.VMEM((packed_rows, 128), F32),
        in_specs=[sm] * 2 + [vm] * (2 + len(weights)),
        out_specs=vm,
        scratch_shapes=[
            pltpu.VMEM((T, 128), F32),
            pltpu.VMEM((3, HID, HID), F32),
            pltpu.VMEM((3, 8, HID), F32),
            pltpu.VMEM((24, HID), F32),
            pltpu.VMEM((2, 24, HID), F32),
            pltpu.VMEM((16, HID), F32),
            pltpu.VMEM((2, 16, HID), F32),
            pltpu.VMEM((16, 128), F32),
            pltpu.VMEM((8, 128), F32),
        ],
        compiler_params=pltpu.CompilerParams(vmem_limit_bytes=40 << 20),
        name="networks",
    )(idx_s, scal, tab, got, *weights)


def split_sizes(n):
    sizes = [2]
    n //= 2
    while n > 1:
        f = 4 if n % 4 == 0 else n if n < 4 else 2
        sizes.append(f)
        n //= f
    return sizes


def chunk_rows(rows):
    units = rows // 8
    k = min(CHUNKS, units)
    cuts = [8 * (units * j // k) for j in range(k + 1)]
    return list(zip(cuts[:-1], cuts[1:]))


def sum_kernel(sizes, mine, out, *rest):
    ns = len(sizes)
    got, part, sems = rest[:ns], rest[ns : 2 * ns], rest[2 * ns]
    n = mine.shape[0]
    parts = chunk_rows(mine.shape[1])
    me = lax.axis_index("dp")
    digits, strides, st = [], [], 1
    for f in sizes:
        digits.append(lax.rem(me // st, f))
        strides.append(st)
        st *= f

    def member(s, k):
        d = lax.rem(digits[s] + k, sizes[s])
        return d, me + (d - digits[s]) * strides[s]

    barrier = pltpu.get_barrier_semaphore()
    count = 0
    for s in range(ns):
        for k in range(1, sizes[s]):
            pl.semaphore_signal(barrier, inc=1, device_id=(member(s, k)[1],), device_id_type=pl.DeviceIdType.MESH)
            count += 1
    pl.semaphore_wait(barrier, count)

    def send(src, dst, s, k, phase, c):
        copy = pltpu.make_async_remote_copy(
            src_ref=src, dst_ref=dst, send_sem=sems.at[phase, c, s, k, 0], recv_sem=sems.at[phase, c, s, k, 1],
            device_id=(member(s, k)[1],), device_id_type=pl.DeviceIdType.MESH,
        )
        copy.start()
        return copy

    spans, starts = [n], [0]
    for s in range(ns):
        spans.append(spans[s] // sizes[s])
        starts.append(starts[s] + digits[s] * spans[s + 1])
    done, flying = [], {}

    def scatter(s, c):
        lo, hi = parts[c]
        src = mine if s == 0 else part[s - 1]
        flying[0, s, c] = [
            send(src.at[pl.ds(member(s, k)[0] * spans[s + 1], spans[s + 1]), lo:hi], got[s].at[k - 1, :, lo:hi], s, k, 0, c)
            for k in range(1, sizes[s])
        ]

    def add(s, c):
        lo, hi = parts[c]
        src = mine if s == 0 else part[s - 1]
        acc = src[pl.ds(digits[s] * spans[s + 1], spans[s + 1]), lo:hi]
        for k, copy in enumerate(flying[0, s, c]):
            copy.wait_recv()
            acc = acc + got[s][k, :, lo:hi]
            done.append(copy)
        if s == ns - 1:
            out[pl.ds(starts[ns], 1), lo:hi] = acc
        else:
            part[s][:, lo:hi] = acc

    def spread(s, c):
        lo, hi = parts[c]
        at = out.at[pl.ds(starts[s + 1], spans[s + 1]), lo:hi]
        flying[1, s, c] = [send(at, at, s, k, 1, c) for k in range(1, sizes[s])]

    def arrive(s, c):
        for copy in flying[1, s, c]:
            copy.wait_recv()
            done.append(copy)

    def step(j, c):
        if 1 <= j <= ns:
            add(j - 1, c)
        if j > ns:
            arrive(2 * ns - j, c)
        if j < ns:
            scatter(j, c)
        elif j < 2 * ns:
            spread(2 * ns - 1 - j, c)

    for t in range(2 * ns + len(parts)):
        for j in reversed(range(2 * ns + 1)):
            if 0 <= t - j < len(parts):
                step(j, t - j)
    for copy in done:
        copy.wait_send()


def sum_over_devices(packed, n):
    sizes = split_sizes(n)
    rows = packed.shape[0] // n
    mine = packed.reshape(n, rows, 128)
    got, part, size = [], [], n
    for f in sizes:
        size //= f
        got.append(pltpu.VMEM((f - 1, size, rows, 128), F32))
        part.append(pltpu.VMEM((size, rows, 128), F32))
    vm = pl.BlockSpec(memory_space=pltpu.VMEM)
    out = pl.pallas_call(
        functools.partial(sum_kernel, sizes),
        out_shape=pltpu.VMEM((n, rows, 128), F32),
        in_specs=[vm],
        out_specs=vm,
        scratch_shapes=got + part + [pltpu.SemaphoreType.DMA((2, len(chunk_rows(rows)), len(sizes), max(sizes), 2))],
        compiler_params=pltpu.CompilerParams(collective_id=1, has_side_effects=True, vmem_limit_bytes=24 << 20),
        name="sum_over_devices",
    )(mine)
    return out.reshape(packed.shape)


def finish_kernel(scal, g, aw1, ab1, aw2, ab2, aw3, ab3, cw1, cb1, cw2, cb2, cw3, cb3, da, losses):
    misc = jnp.sum(g[R_MISC : R_MISC + 8, :], axis=1, keepdims=True)
    n = misc[5:6]
    inv = 1.0 / n

    def rows(at, count):
        return jnp.concatenate([g[at : at + count, :], g[at + count : at + 2 * count, :]], axis=1) * inv

    aw2[...] = rows(0, HID)
    cw2[0] = rows(2 * HID, HID)
    cw2[1] = rows(4 * HID, HID)
    w = rows(R_AW1, 24)
    aw1[0:16, :] = w[8:24]
    aw1[16:17, :] = w[7:8]
    ab1[...] = w[6:7]
    for k in range(2):
        w = rows(R_CW1 + 48 * k, 24)
        cw1[0:16, k, :] = w[8:24]
        cw1[16:17, k, :] = w[7:8]
        cw1[17:23, k, :] = w[0:6]
        cb1[k : k + 1, :] = w[6:7]
    w = rows(R_AW3, 16)
    aw3[0:6, :] = w[0:6]
    aw3[6:12, :] = w[8:14]
    c = rows(R_COL, 8)
    cb2[...] = c[0:2]
    cw3[...] = c[2:4]
    ab2[...] = c[4:5]
    b = jnp.sum(g[R_AB3 : R_AB3 + 16, :], axis=1, keepdims=True) * inv
    diag = lax.broadcasted_iota(jnp.int32, (16, 128), 0) == lax.broadcasted_iota(jnp.int32, (16, 128), 1)
    b = jnp.sum(jnp.where(diag, b, 0.0), axis=0, keepdims=True)
    ab3[...] = jnp.concatenate([b[:, 0:6], b[:, 8:14]], axis=1)
    m = misc * inv
    cb3[...] = jnp.concatenate([m[0:1], m[1:2]], axis=1)
    da[...] = -m[4:5]
    losses[...] = jnp.concatenate([m[2:3], m[3:4], -scal[4] * m[4:5]], axis=1)


def finish(total, scal):
    vm = pl.BlockSpec(memory_space=pltpu.VMEM)
    shapes = [
        (OBS, HID), (1, HID), (HID, HID), (1, HID), (12, HID), (1, 12),
        (23, 2, HID), (2, HID), (2, HID, HID), (2, HID), (2, HID), (1, 2), (1, 1), (1, 3),
    ]
    outs = list(pl.pallas_call(
        finish_kernel,
        out_shape=[jax.ShapeDtypeStruct(x, F32) for x in shapes],
        in_specs=[pl.BlockSpec(memory_space=pltpu.SMEM), vm],
        out_specs=[vm] * len(shapes),
        name="finish",
    )(scal, total))
    outs[4] = outs[4].T
    outs[6] = outs[6].transpose(1, 0, 2)
    for k, shape in ((1, (HID,)), (3, (HID,)), (5, (12,)), (11, (2,)), (12, ()), (13, (3,))):
        outs[k] = outs[k].reshape(shape)
    return tuple(outs)


def body(experience_buffer, sampled_indices, filled_lengths, randomizer_numbers, *params):
    n, cap = sampled_indices.shape[1:]
    ready = prepare(experience_buffer, sampled_indices, randomizer_numbers, filled_lengths, params)
    packed = local_grads(ready, n, cap, n * 8 * (-(-R_END // (8 * n))))
    return finish(sum_over_devices(packed, n), ready[-1])


def solution(mesh):
    in_specs = (P(None, "dp"), P("dp", None, None), P("dp", None), P("dp", None, None)) + (P(),) * 19
    return jax.shard_map(body, mesh=mesh, in_specs=in_specs, out_specs=(P(),) * 14, check_vma=False)
```

```python
import functools
import math

import jax
import jax.numpy as jnp
from jax import lax
from jax.experimental import pallas as pl
from jax.experimental.pallas import tpu as pltpu
from jax.sharding import PartitionSpec as P

OBS = 17
ACT = 6
HID = 256
GAMMA = 0.99
PRIME = 65521
TILE = 1024
CHUNKS = 4
VARIANTS = 8
R_AW1 = 6 * HID
R_CW1 = R_AW1 + 48
R_AW3 = R_CW1 + 96
R_COL = R_AW3 + 32
R_AB3 = R_COL + 16
R_MISC = R_AB3 + 16
R_END = R_MISC + 8
BF = jnp.bfloat16
F32 = jnp.float32


def dot(a, b):
    return jnp.dot(a, b, preferred_element_type=F32)


def dot_t(a, b):
    return lax.dot_general(a, b, (((1,), (1,)), ((), ())), preferred_element_type=F32)


def split(x):
    hi = x.astype(BF).astype(F32)
    return hi, x - hi


def fold_prime(x):
    return (x >> 16) * 15 + (x & 65535)


def below_prime(x):
    return jnp.where(x >= PRIME, x - PRIME, x)


def noise(seeds, rows):
    comp = jnp.where(rows >= 8, rows - 2, rows)
    z = below_prime(fold_prime(seeds))
    h0 = below_prime(fold_prime(z * 257 + comp * 7919 + 1))
    h1 = below_prime(fold_prime(fold_prime(h0 * 32749 + 12345)))
    h2 = below_prime(fold_prime(fold_prime(h1 * 32749 + 54321)))
    u1 = (h1.astype(F32) + 0.5) * (1.0 / PRIME)
    x = jnp.abs((2 * h2 + (1 - PRIME)).astype(F32)) * (math.pi / PRIME) - 0.5 * math.pi
    x2 = x * x
    p = -1.0 / 39916800.0
    for c in (1.0 / 362880.0, -1.0 / 5040.0, 1.0 / 120.0, -1.0 / 6.0, 1.0):
        p = p * x2 + c
    return jnp.sqrt(-2.0 * jnp.log(u1)) * (p * x)


def fold(x):
    return functools.reduce(lambda a, b: a + b, [x[:, k * 128 : (k + 1) * 128] for k in range(x.shape[1] // 128)])


def message_rows(cap):
    return -(-cap // 128)


def prepare_kernel(
    idx_h, seed_h, cnt_h, buf_h, aw2_h, jw2_h, lw2_h,
    aw1_h, ab1_h, ab2_h, aw3_h, jw1_h, jb1_h, jb2_h, jw3_h, lw1_h, lb1_h, lb2_h, lw3_h,
    ab3_h, jb3_h, lb3_h, level,
    tab, got, idx_s, w1all, f2, b2, head, headb, da_w, qw, col, scale, scal,
    idx_v, seed_v, cnt_v, buf, w2, aw1, ab1, ab2, aw3, jw1, jb1, jb2, jw3, lw1, lb1, lb2, lw3,
    ab3, jb3, lb3, msg, land, flat, tmp, rowbuf, in_sems, sems,
    *, n, cap,
):
    me = lax.axis_index("dp")
    rows = message_rows(cap)
    part = min(cap, 128)
    width = buf.shape[1]
    pairs = (
        (idx_h, idx_v), (seed_h, seed_v), (cnt_h, cnt_v), (buf_h, buf),
        (aw2_h, w2.at[0]), (jw2_h, w2.at[pl.ds(1, 2)]), (lw2_h, w2.at[pl.ds(3, 2)]),
        (aw1_h, aw1), (ab1_h, ab1), (ab2_h, ab2), (aw3_h, aw3), (jw1_h, jw1), (jb1_h, jb1), (jb2_h, jb2),
        (jw3_h, jw3), (lw1_h, lw1), (lb1_h, lb1), (lb2_h, lb2), (lw3_h, lw3),
        (ab3_h, ab3), (jb3_h, jb3), (lb3_h, lb3),
    )
    loads = [pltpu.make_async_copy(src, dst, in_sems.at[k]) for k, (src, dst) in enumerate(pairs)]
    for c in loads:
        c.start()
    barrier = pltpu.get_barrier_semaphore()

    @pl.loop(1, n)
    def _(k):
        pl.semaphore_signal(barrier, inc=1, device_id=(lax.rem(me + k, n),), device_id_type=pl.DeviceIdType.MESH)

    for c in loads[:3]:
        c.wait()
    msg[...] = jnp.zeros_like(msg)
    for r in range(rows):
        msg[:, r, 0:part] = idx_v[0, :, r * part : (r + 1) * part]
        msg[:, rows + r, 0:part] = seed_v[0, :, r * part : (r + 1) * part]
    diag = lax.broadcasted_iota(jnp.int32, (n, n), 0) == lax.broadcasted_iota(jnp.int32, (n, n), 1)
    counts = jnp.sum(jnp.where(diag, cnt_v[...].astype(F32), 0.0), axis=1, keepdims=True)
    msg[:, 2 * rows, :] = jnp.broadcast_to(counts, (n, 128)).astype(jnp.int32)
    for c in loads[4:]:
        c.wait()
    for l, (w1, b1, k) in enumerate(((aw1, ab1, None), (jw1, jb1, 0), (jw1, jb1, 1), (lw1, lb1, 0), (lw1, lb1, 1))):
        if k is None:
            tmp[0:6, :] = jnp.zeros((6, HID), F32)
            tmp[6:7, :] = b1[...]
            tmp[7:8, :] = w1[16:17, :]
            tmp[8:24, :] = w1[0:16, :]
        else:
            tmp[0:6, :] = w1[17:23, k, :]
            tmp[6:7, :] = b1[k : k + 1, :]
            tmp[7:8, :] = w1[16:17, k, :]
            tmp[8:24, :] = w1[0:16, k, :]
        hi, lo = split(0.5 * tmp[0:24, :])
        w1all[l * HID : (l + 1) * HID, :] = jnp.concatenate([hi, hi, lo], axis=0).T.astype(BF)
        if l in (1, 2):
            hi, lo = split(tmp[0:8, :])
            da_w[l - 1] = jnp.concatenate([hi, lo], axis=0).astype(BF)
    start = ((2 * me + 1).astype(F32) / n - 1.0) * 2.0**-8

    def roundings(ref, l, w):
        left = w.astype(BF).astype(F32) * start
        for v in range(VARIANTS):
            want = w + left
            got_ = want.astype(BF)
            ref[l, v] = got_
            left = want - got_.astype(F32)

    for l in range(5):
        w = 0.5 * w2[l]
        roundings(f2, l, w.T)
        if l == 0:
            roundings(b2, l, w)
        elif l < 3:
            roundings(b2, l, w * (0.5 * jw3[l - 1 : l, :]))
    tmp[0:12, :] = aw3[...]
    r8 = lax.broadcasted_iota(jnp.int32, (8, HID), 0)
    w_head = jnp.concatenate([jnp.where(r8 < 6, tmp[0:8, :], 0.0), jnp.where(r8 < 6, tmp[6:14, :], 0.0)], axis=0)
    hi, lo = split(w_head)
    head[...] = jnp.concatenate([hi, lo], axis=0).astype(BF)
    headb[...] = (0.5 * jnp.concatenate([hi, lo], axis=0)).T.astype(BF)
    for k in range(4):
        w3 = jw3[k : k + 1, :] if k < 2 else lw3[k - 2 : k - 1, :]
        hi, lo = split(w3)
        qw[k] = jnp.concatenate([jnp.where(r8 == 0, hi, 0.0), jnp.where(r8 == 0, lo, 0.0)], axis=0).astype(BF)
    rowbuf[...] = jnp.zeros_like(rowbuf)
    rowbuf[0:1, :] = 0.5 * ab2[...]
    rowbuf[1:3, :] = 0.5 * jb2[...]
    rowbuf[3:5, :] = 0.5 * lb2[...]
    lane12 = lax.broadcasted_iota(jnp.int32, (1, HID), 1)
    hb = jnp.zeros((1, HID), F32)
    for k in range(12):
        hb = jnp.where(lane12 == (k if k < 6 else k + 2), ab3[k], hb)
    rowbuf[5:6, :] = hb
    col[...] = rowbuf[...].T
    scale[...] = jnp.zeros_like(scale)
    scale[0:2, :] = 0.5 * jw3[...]
    for k in range(2):
        scal[k] = jb3[k]
        scal[2 + k] = lb3[k]
    scal[4] = level[0]

    pl.semaphore_wait(barrier, n - 1)

    def copy(k):
        return pltpu.make_async_remote_copy(
            src_ref=msg.at[lax.rem(me + k, n)], dst_ref=land.at[k], send_sem=sems.at[0, k], recv_sem=sems.at[1, k],
            device_id=(lax.rem(me + k, n),), device_id_type=pl.DeviceIdType.MESH,
        )

    @pl.loop(1, n)
    def _(k):
        copy(k).start()

    loads[3].wait()

    @pl.loop(0, width // 128, unroll=4)
    def _(c):
        blk = buf[:, pl.ds(pl.multiple_of(c * 128, 128), 128)]
        tab[pl.ds(pl.multiple_of(c * 128, 128), 128), 0:42] = blk.T

    land[0] = msg[me]

    @pl.loop(1, n)
    def _(k):
        copy(k).wait()

    @pl.loop(0, n)
    def _(k):
        got[lax.rem(me - k + n, n)] = land[k]

    for r in range(rows):
        flat[:, r, :] = got[:, r, :]
    c = pltpu.make_async_copy(flat, idx_s, in_sems.at[0])
    c.start()
    c.wait()


def prepare(experience_buffer, sampled, seeds, counts, params):
    (aw1, ab1, aw2, ab2, aw3, ab3, jw1, jb1, jw2, jb2, jw3, jb3, lw1, lb1, lw2, lb2, lw3, lb3, level) = params
    feats, width = experience_buffer.shape
    _, n, cap = sampled.shape
    rows = message_rows(cap)
    vm = pl.BlockSpec(memory_space=pltpu.VMEM)
    sm = pl.BlockSpec(memory_space=pltpu.SMEM)
    hbm = pl.BlockSpec(memory_space=pl.ANY)
    out = [
        pltpu.VMEM((width, 128), F32),
        pltpu.VMEM((n, 8, 128), jnp.int32),
        pltpu.SMEM((n, rows, 128), jnp.int32),
        pltpu.VMEM((5 * HID, 72), BF),
        pltpu.VMEM((5, VARIANTS, HID, HID), BF),
        pltpu.VMEM((3, VARIANTS, HID, HID), BF),
        pltpu.VMEM((32, HID), BF),
        pltpu.VMEM((HID, 32), BF),
        pltpu.VMEM((2, 16, HID), BF),
        pltpu.VMEM((4, 16, HID), BF),
        pltpu.VMEM((HID, 8), F32),
        pltpu.VMEM((8, HID), F32),
        pltpu.SMEM((8,), F32),
    ]
    return pl.pallas_call(
        functools.partial(prepare_kernel, n=n, cap=cap),
        out_shape=out,
        in_specs=[hbm] * 22 + [sm],
        out_specs=[vm, vm, sm] + [vm] * 9 + [sm],
        scratch_shapes=[
            pltpu.VMEM((1, n, cap), jnp.int32),
            pltpu.VMEM((1, n, cap), jnp.int32),
            pltpu.VMEM((1, n), jnp.int32),
            pltpu.VMEM((feats, width), F32),
            pltpu.VMEM((5, HID, HID), F32),
            pltpu.VMEM((OBS, HID), F32),
            pltpu.VMEM((1, HID), F32),
            pltpu.VMEM((1, HID), F32),
            pltpu.VMEM((12, HID), F32),
            pltpu.VMEM((23, 2, HID), F32),
            pltpu.VMEM((2, HID), F32),
            pltpu.VMEM((2, HID), F32),
            pltpu.VMEM((2, HID), F32),
            pltpu.VMEM((23, 2, HID), F32),
            pltpu.VMEM((2, HID), F32),
            pltpu.VMEM((2, HID), F32),
            pltpu.VMEM((2, HID), F32),
            pltpu.SMEM((12,), F32),
            pltpu.SMEM((2,), F32),
            pltpu.SMEM((2,), F32),
            pltpu.VMEM((n, 8, 128), jnp.int32),
            pltpu.VMEM((n, 8, 128), jnp.int32),
            pltpu.VMEM((n, rows, 128), jnp.int32),
            pltpu.VMEM((24, HID), F32),
            pltpu.VMEM((8, HID), F32),
            pltpu.SemaphoreType.DMA((22,)),
            pltpu.SemaphoreType.DMA((2, n)),
        ],
        compiler_params=pltpu.CompilerParams(collective_id=2, has_side_effects=True, vmem_limit_bytes=24 << 20),
        name="exchange_and_prepare",
    )(
        *[
            pltpu.with_memory_space_constraint(x, pltpu.HBM)
            for x in (
                sampled, seeds, counts, experience_buffer, aw2, jw2, lw2,
                aw1, ab1.reshape(1, HID), ab2.reshape(1, HID), aw3.T,
                jw1.transpose(1, 0, 2), jb1, jb2, jw3, lw1.transpose(1, 0, 2), lb1, lb2, lw3,
                ab3, jb3, lb3,
            )
        ],
        level.reshape(1),
    )


def net_kernel(
    idx_s, scal, tab, got, w1all, f2, b2, head, headb, da_w, qw, col, scale,
    packed,
    xrow, gw2, gw2b, gaw1, gcw1, gaw3, gcw3, gcol, gmisc,
    *, cap, slots,
):
    T = min(TILE, slots)
    nt = slots // T
    lists = T // cap
    rows = message_rows(cap)
    part = min(cap, 128)

    def gather(i):
        for t in range(T):
            r = idx_s[i * lists + t // cap, (t % cap) // 128, t % 128]
            xrow[t : t + 1, :] = tab[pl.ds(r, 1), :]

    gather(0)
    for ref in (gw2, gw2b, gaw1, gcw1, gaw3, gcw3, gcol, gmisc):
        ref[...] = jnp.zeros_like(ref)
    level = scal[4]
    jb3_s = (scal[0], scal[1])
    lb3_s = (scal[2], scal[3])

    def act(u):
        t = jnp.tanh(u)
        p = 1.0 + t
        h = u * p
        return h.astype(BF), p + h * (2.0 - p)

    def layer2(i, l, h):
        return act(by_chunk(f2, l, i, h) + col[:, l : l + 1])

    def first(l0, l1, x24):
        hi, lo = split(x24)
        xs = jnp.concatenate([hi, lo, hi], axis=0).astype(BF)
        return dot(w1all[l0 * HID : l1 * HID, :], xs)

    def by_chunk(w, l, i, x):
        nq = T // HID
        return jnp.concatenate(
            [dot(w[l, lax.rem(i * nq + q, VARIANTS)], x[:, q * HID : (q + 1) * HID]) for q in range(nq)], axis=1
        )

    def head_out(h2):
        r = dot(head[...], h2)
        o = r[0:16] + r[16:32] + col[0:16, 5:6]
        mean = o[0:8]
        t = jnp.tanh(o[8:16])
        ls = -5.0 + 3.5 * (t + 1.0)
        return mean, t, ls

    def sample(mean, ls, e, live):
        sg = jnp.exp(ls)
        u = mean + sg * e
        a = jnp.tanh(u)
        au = jnp.abs(u)
        sq = 2.0 * (math.log(2.0) - au - jnp.log(1.0 + jnp.exp(-2.0 * au)))
        lp = -0.5 * e * e - ls - 0.5 * math.log(2.0 * math.pi) - sq
        return a, sg, jnp.sum(jnp.where(live, lp, 0.0), axis=0, keepdims=True)

    def q_of(k, h2, b):
        r = dot(qw[k], h2)
        return r[0:1] + r[8:9] + b

    def softmin(q, w):
        a, b = -4.0 * q, -4.0 * w
        return -0.25 * (jnp.maximum(a, b) + jnp.log(1.0 + jnp.exp(-jnp.abs(a - b))))

    ones = jnp.ones((16, T), BF)

    @pl.loop(0, nt)
    def _(i):
        xt = xrow[...].T
        gather(jnp.minimum(i + 1, nt - 1))
        row8 = lax.broadcasted_iota(jnp.int32, (8, T), 0)
        row16 = lax.broadcasted_iota(jnp.int32, (16, T), 0)
        live = row8 < ACT
        seeds = jnp.concatenate([got[i * lists + k, rows + r : rows + r + 1, 0:part] for k in range(lists) for r in range(rows)], axis=1)
        lane = lax.broadcasted_iota(jnp.int32, (1, cap), 1)
        mask = jnp.concatenate(
            [jnp.where(lane < got[i * lists + k, 2 * rows : 2 * rows + 1, 0:1], 1.0, 0.0).astype(F32) for k in range(lists)], axis=1
        )
        alpha = jnp.exp(jnp.full((1, T), level, F32))
        b1 = pltpu.roll(xt[16:24], 7, 0)
        reward = b1[6:7]
        xa = jnp.concatenate([jnp.where(row8 == 6, 1.0, b1), xt[0:16]], axis=0)
        b2_ = pltpu.roll(xt[40:48], 7, 0)
        done = b2_[0:1]
        n_lo = jnp.where(row8 == 7, b2_, jnp.where(row8 == 6, 1.0, 0.0))
        xn = jnp.concatenate([n_lo, xt[24:40]], axis=0)

        un = first(0, 1, xn)
        hi, lo = split(xa)
        xw = jnp.concatenate([hi, lo], axis=0).astype(BF)
        ua = dot(w1all[0 : 3 * HID, :], jnp.concatenate([hi, lo, hi], axis=0).astype(BF))
        eps = noise(seeds, row16)
        e = eps[0:8]
        hn, _ = act(un)
        h1a, d1a = act(ua[0:HID])
        h1c, d1c = zip(*[act(ua[(1 + k) * HID : (2 + k) * HID]) for k in range(2)])
        hn, _ = layer2(i, 0, hn)
        mean, _, ls = head_out(hn)
        a2, _, lp2 = sample(mean, ls, eps[8:16], live)
        h2a, d2a = layer2(i, 0, h1a)
        mean, t, ls = head_out(h2a)
        a1, sg, lp = sample(mean, ls, e, live)
        un = first(3, 5, jnp.concatenate([jnp.where(live, a2, n_lo), xt[24:40]], axis=0))
        h2c, d2c = zip(*[layer2(i, 1 + k, h1c[k]) for k in range(2)])
        qc = [q_of(k, h2c[k], jb3_s[k]) for k in range(2)]
        uq = first(1, 3, jnp.concatenate([jnp.where(live, a1, xa[0:8]), xt[0:16]], axis=0))
        ht = [act(un[k * HID : (k + 1) * HID])[0] for k in range(2)]
        ht = [layer2(i, 3 + k, ht[k])[0] for k in range(2)]
        qt = [q_of(2 + k, ht[k], lb3_s[k]) for k in range(2)]
        h1q, d1q = zip(*[act(uq[k * HID : (k + 1) * HID]) for k in range(2)])
        y = reward + GAMMA * (1.0 - done) * (softmin(qt[0], qt[1]) - alpha * lp2)
        h2q, d2q = zip(*[layer2(i, 1 + k, h1q[k]) for k in range(2)])
        qq = [q_of(k, h2q[k], jb3_s[k]) for k in range(2)]

        closs = jnp.zeros((1, T), F32)
        g2c = []
        for k in range(2):
            dq = qc[k] - y
            mdq = dq * mask
            closs = closs + 0.5 * (mdq * dq)
            g2 = (mdq * d2c[k]).astype(BF)
            g2c.append(g2)
            mhi, mlo = split(mdq)
            m16 = jnp.where(row16 == 0, mhi, jnp.where(row16 == 1, mlo, 0.0)).astype(BF)
            gcw3[k] += dot_t(m16, h2c[k])
            r = dot_t(jnp.concatenate([h1c[k], ones], axis=0), g2)
            gw2[1 + k] += r[0:HID]
            gw2b[1 + k] += r[HID : HID + 8]
            gmisc[k : k + 1, :] += fold(mdq)
        sm = softmin(qq[0], qq[1])
        p0 = 1.0 / (1.0 + jnp.exp(4.0 * (qq[0] - qq[1])))
        da = jnp.zeros((8, T), F32)
        for k, pk in enumerate((p0, 1.0 - p0)):
            g2 = ((-pk * mask) * d2q[k]).astype(BF)
            g1 = (by_chunk(b2, 1 + k, i, g2) * d1q[k]).astype(BF)
            w = dot(da_w[k], g1)
            da = da + w[0:8] + w[8:16]
        for k in range(2):
            g1 = (by_chunk(b2, 1 + k, i, g2c[k]) * d1c[k]).astype(BF)
            w = dot_t(xw, g1)
            gcw1[k] += w[0:24] + w[24:48]
        ma = mask * alpha
        du = da * (1.0 - a1 * a1) + ma * (2.0 * a1)
        dls = (du * sg * e - ma) * (3.5 * (1.0 - t * t))
        do = jnp.concatenate([jnp.where(live, du, 0.0), jnp.where(live, dls, 0.0)], axis=0)
        gcol[...] += fold(do)
        dob = do.astype(BF)
        gaw3[...] += dot_t(dob, h2a)
        g2 = (dot(headb[...], jnp.concatenate([dob, dob], axis=0)) * d2a).astype(BF)
        r = dot_t(jnp.concatenate([h1a, ones], axis=0), g2)
        gw2[0] += r[0:HID]
        gw2b[0] += r[HID : HID + 8]
        g1 = (by_chunk(b2, 0, i, g2) * d1a).astype(BF)
        w = dot_t(xw, g1)
        gaw1[...] += w[0:24] + w[24:48]
        gmisc[2:3, :] += fold(closs)
        gmisc[3:4, :] += fold(mask * (alpha * lp - sm))
        gmisc[4:5, :] += fold(mask * (lp - 6.0))
        gmisc[5:6, :] += fold(mask)

    row8 = lax.broadcasted_iota(jnp.int32, (8, HID), 0)
    cols = jnp.zeros((8, HID), F32)
    for k in range(2):
        s = scale[k : k + 1, :]
        cols = jnp.where(row8 == k, gw2b[1 + k] * s, cols)
        cols = jnp.where(row8 == 2 + k, gcw3[k, 0:1, :] + gcw3[k, 1:2, :], cols)
    cols = jnp.where(row8 == 4, gw2b[0], cols)
    for m in range(3):
        for h in range(2):
            w = gw2[m, :, h * 128 : (h + 1) * 128]
            if m > 0:
                w = w * scale[m - 1 : m, h * 128 : (h + 1) * 128]
            packed[(2 * m + h) * HID : (2 * m + h + 1) * HID, :] = w
    for h in range(2):
        packed[R_AW1 + 24 * h : R_AW1 + 24 * (h + 1), :] = gaw1[:, h * 128 : (h + 1) * 128]
        for k in range(2):
            at = R_CW1 + 48 * k + 24 * h
            packed[at : at + 24, :] = gcw1[k, :, h * 128 : (h + 1) * 128]
        packed[R_AW3 + 16 * h : R_AW3 + 16 * (h + 1), :] = gaw3[:, h * 128 : (h + 1) * 128]
        packed[R_COL + 8 * h : R_COL + 8 * (h + 1), :] = cols[:, h * 128 : (h + 1) * 128]
    packed[R_AB3 : R_AB3 + 16, :] = gcol[...]
    packed[R_MISC : R_MISC + 8, :] = gmisc[...]
    packed[R_END:, :] = jnp.zeros((packed.shape[0] - R_END, 128), F32)


def local_grads(ready, n, cap, packed_rows):
    tab, got, idx_s, *weights, scal = ready
    slots = n * cap
    T = min(TILE, slots)
    vm = pl.BlockSpec(memory_space=pltpu.VMEM)
    sm = pl.BlockSpec(memory_space=pltpu.SMEM)
    return pl.pallas_call(
        functools.partial(net_kernel, cap=cap, slots=slots),
        out_shape=pltpu.VMEM((packed_rows, 128), F32),
        in_specs=[sm] * 2 + [vm] * (2 + len(weights)),
        out_specs=vm,
        scratch_shapes=[
            pltpu.VMEM((T, 128), F32),
            pltpu.VMEM((3, HID, HID), F32),
            pltpu.VMEM((3, 8, HID), F32),
            pltpu.VMEM((24, HID), F32),
            pltpu.VMEM((2, 24, HID), F32),
            pltpu.VMEM((16, HID), F32),
            pltpu.VMEM((2, 16, HID), F32),
            pltpu.VMEM((16, 128), F32),
            pltpu.VMEM((8, 128), F32),
        ],
        compiler_params=pltpu.CompilerParams(vmem_limit_bytes=40 << 20),
        name="networks",
    )(idx_s, scal, tab, got, *weights)


def split_sizes(n):
    sizes = [2]
    n //= 2
    while n > 1:
        f = 4 if n % 4 == 0 else n if n < 4 else 2
        sizes.append(f)
        n //= f
    return sizes


def chunk_rows(rows):
    units = rows // 8
    k = min(CHUNKS, units)
    cuts = [8 * (units * j // k) for j in range(k + 1)]
    return list(zip(cuts[:-1], cuts[1:]))


def sum_kernel(sizes, mine, out, *rest):
    ns = len(sizes)
    got, part, sems = rest[:ns], rest[ns : 2 * ns], rest[2 * ns]
    n = mine.shape[0]
    parts = chunk_rows(mine.shape[1])
    me = lax.axis_index("dp")
    digits, strides, st = [], [], 1
    for f in sizes:
        digits.append(lax.rem(me // st, f))
        strides.append(st)
        st *= f

    def member(s, k):
        d = lax.rem(digits[s] + k, sizes[s])
        return d, me + (d - digits[s]) * strides[s]

    barrier = pltpu.get_barrier_semaphore()
    count = 0
    for s in range(ns):
        for k in range(1, sizes[s]):
            pl.semaphore_signal(barrier, inc=1, device_id=(member(s, k)[1],), device_id_type=pl.DeviceIdType.MESH)
            count += 1
    pl.semaphore_wait(barrier, count)

    def send(src, dst, s, k, phase, c):
        copy = pltpu.make_async_remote_copy(
            src_ref=src, dst_ref=dst, send_sem=sems.at[phase, c, s, k, 0], recv_sem=sems.at[phase, c, s, k, 1],
            device_id=(member(s, k)[1],), device_id_type=pl.DeviceIdType.MESH,
        )
        copy.start()
        return copy

    spans, starts = [n], [0]
    for s in range(ns):
        spans.append(spans[s] // sizes[s])
        starts.append(starts[s] + digits[s] * spans[s + 1])
    done, flying = [], {}

    def scatter(s, c):
        lo, hi = parts[c]
        src = mine if s == 0 else part[s - 1]
        flying[0, s, c] = [
            send(src.at[pl.ds(member(s, k)[0] * spans[s + 1], spans[s + 1]), lo:hi], got[s].at[k - 1, :, lo:hi], s, k, 0, c)
            for k in range(1, sizes[s])
        ]

    def add(s, c):
        lo, hi = parts[c]
        src = mine if s == 0 else part[s - 1]
        acc = src[pl.ds(digits[s] * spans[s + 1], spans[s + 1]), lo:hi]
        for k, copy in enumerate(flying[0, s, c]):
            copy.wait_recv()
            acc = acc + got[s][k, :, lo:hi]
            done.append(copy)
        if s == ns - 1:
            out[pl.ds(starts[ns], 1), lo:hi] = acc
        else:
            part[s][:, lo:hi] = acc

    def spread(s, c):
        lo, hi = parts[c]
        at = out.at[pl.ds(starts[s + 1], spans[s + 1]), lo:hi]
        flying[1, s, c] = [send(at, at, s, k, 1, c) for k in range(1, sizes[s])]

    def arrive(s, c):
        for copy in flying[1, s, c]:
            copy.wait_recv()
            done.append(copy)

    chunks = range(len(parts))
    for c in chunks:
        scatter(0, c)
    for s in range(ns):
        for c in chunks:
            add(s, c)
            if s < ns - 1:
                scatter(s + 1, c)
            else:
                spread(ns - 1, c)
    for s in reversed(range(ns)):
        for c in chunks:
            arrive(s, c)
            if s > 0:
                spread(s - 1, c)
    for copy in done:
        copy.wait_send()


def sum_over_devices(packed, n):
    sizes = split_sizes(n)
    rows = packed.shape[0] // n
    mine = packed.reshape(n, rows, 128)
    got, part, size = [], [], n
    for f in sizes:
        size //= f
        got.append(pltpu.VMEM((f - 1, size, rows, 128), F32))
        part.append(pltpu.VMEM((size, rows, 128), F32))
    vm = pl.BlockSpec(memory_space=pltpu.VMEM)
    out = pl.pallas_call(
        functools.partial(sum_kernel, sizes),
        out_shape=pltpu.VMEM((n, rows, 128), F32),
        in_specs=[vm],
        out_specs=vm,
        scratch_shapes=got + part + [pltpu.SemaphoreType.DMA((2, len(chunk_rows(rows)), len(sizes), max(sizes), 2))],
        compiler_params=pltpu.CompilerParams(collective_id=1, has_side_effects=True, vmem_limit_bytes=24 << 20),
        name="sum_over_devices",
    )(mine)
    return out.reshape(packed.shape)


def finish_kernel(scal, g, aw1, ab1, aw2, ab2, aw3, ab3, cw1, cb1, cw2, cb2, cw3, cb3, da, losses):
    misc = jnp.sum(g[R_MISC : R_MISC + 8, :], axis=1, keepdims=True)
    n = misc[5:6]
    inv = 1.0 / n

    def rows(at, count):
        return jnp.concatenate([g[at : at + count, :], g[at + count : at + 2 * count, :]], axis=1) * inv

    aw2[...] = rows(0, HID)
    cw2[0] = rows(2 * HID, HID)
    cw2[1] = rows(4 * HID, HID)
    w = rows(R_AW1, 24)
    aw1[0:16, :] = w[8:24]
    aw1[16:17, :] = w[7:8]
    ab1[...] = w[6:7]
    for k in range(2):
        w = rows(R_CW1 + 48 * k, 24)
        cw1[0:16, k, :] = w[8:24]
        cw1[16:17, k, :] = w[7:8]
        cw1[17:23, k, :] = w[0:6]
        cb1[k : k + 1, :] = w[6:7]
    w = rows(R_AW3, 16)
    aw3[0:6, :] = w[0:6]
    aw3[6:12, :] = w[8:14]
    c = rows(R_COL, 8)
    cb2[...] = c[0:2]
    cw3[...] = c[2:4]
    ab2[...] = c[4:5]
    b = jnp.sum(g[R_AB3 : R_AB3 + 16, :], axis=1, keepdims=True) * inv
    diag = lax.broadcasted_iota(jnp.int32, (16, 128), 0) == lax.broadcasted_iota(jnp.int32, (16, 128), 1)
    b = jnp.sum(jnp.where(diag, b, 0.0), axis=0, keepdims=True)
    ab3[...] = jnp.concatenate([b[:, 0:6], b[:, 8:14]], axis=1)
    m = misc * inv
    cb3[...] = jnp.concatenate([m[0:1], m[1:2]], axis=1)
    da[...] = -m[4:5]
    losses[...] = jnp.concatenate([m[2:3], m[3:4], -scal[4] * m[4:5]], axis=1)


def finish(total, scal):
    vm = pl.BlockSpec(memory_space=pltpu.VMEM)
    shapes = [
        (OBS, HID), (1, HID), (HID, HID), (1, HID), (12, HID), (1, 12),
        (23, 2, HID), (2, HID), (2, HID, HID), (2, HID), (2, HID), (1, 2), (1, 1), (1, 3),
    ]
    outs = list(pl.pallas_call(
        finish_kernel,
        out_shape=[jax.ShapeDtypeStruct(x, F32) for x in shapes],
        in_specs=[pl.BlockSpec(memory_space=pltpu.SMEM), vm],
        out_specs=[vm] * len(shapes),
        name="finish",
    )(scal, total))
    outs[4] = outs[4].T
    outs[6] = outs[6].transpose(1, 0, 2)
    for k, shape in ((1, (HID,)), (3, (HID,)), (5, (12,)), (11, (2,)), (12, ()), (13, (3,))):
        outs[k] = outs[k].reshape(shape)
    return tuple(outs)


def body(experience_buffer, sampled_indices, filled_lengths, randomizer_numbers, *params):
    n, cap = sampled_indices.shape[1:]
    ready = prepare(experience_buffer, sampled_indices, randomizer_numbers, filled_lengths, params)
    packed = local_grads(ready, n, cap, n * 8 * (-(-R_END // (8 * n))))
    return finish(sum_over_devices(packed, n), ready[-1])


def solution(mesh):
    in_specs = (P(None, "dp"), P("dp", None, None), P("dp", None), P("dp", None, None)) + (P(),) * 19
    return jax.shard_map(body, mesh=mesh, in_specs=in_specs, out_specs=(P(),) * 14, check_vma=False)
```

```python
import functools
import math

import jax
import jax.numpy as jnp
from jax import lax
from jax.experimental import pallas as pl
from jax.experimental.pallas import tpu as pltpu
from jax.sharding import PartitionSpec as P

OBS = 17
ACT = 6
HID = 256
GAMMA = 0.99
PRIME = 65521
TILE = 1024
CHUNKS = 4
VARIANTS = 8
R_AW1 = 6 * HID
R_CW1 = R_AW1 + 48
R_AW3 = R_CW1 + 96
R_COL = R_AW3 + 32
R_AB3 = R_COL + 16
R_MISC = R_AB3 + 16
R_END = R_MISC + 8
BF = jnp.bfloat16
F32 = jnp.float32


def dot(a, b):
    return jnp.dot(a, b, preferred_element_type=F32)


def dot_t(a, b):
    return lax.dot_general(a, b, (((1,), (1,)), ((), ())), preferred_element_type=F32)


def split(x):
    hi = x.astype(BF).astype(F32)
    return hi, x - hi


def fold_prime(x):
    return (x >> 16) * 15 + (x & 65535)


def below_prime(x):
    return jnp.where(x >= PRIME, x - PRIME, x)


def noise(seeds, rows):
    comp = jnp.where(rows >= 8, rows - 2, rows)
    z = below_prime(fold_prime(seeds))
    h0 = below_prime(fold_prime(z * 257 + comp * 7919 + 1))
    h1 = below_prime(fold_prime(fold_prime(h0 * 32749 + 12345)))
    h2 = below_prime(fold_prime(fold_prime(h1 * 32749 + 54321)))
    u1 = (h1.astype(F32) + 0.5) * (1.0 / PRIME)
    x = jnp.abs((2 * h2 + (1 - PRIME)).astype(F32)) * (math.pi / PRIME) - 0.5 * math.pi
    x2 = x * x
    p = -1.0 / 39916800.0
    for c in (1.0 / 362880.0, -1.0 / 5040.0, 1.0 / 120.0, -1.0 / 6.0, 1.0):
        p = p * x2 + c
    return jnp.sqrt(-2.0 * jnp.log(u1)) * (p * x)


def fold(x):
    return functools.reduce(lambda a, b: a + b, [x[:, k * 128 : (k + 1) * 128] for k in range(x.shape[1] // 128)])


def message_rows(cap):
    return -(-cap // 128)


def prepare_kernel(
    idx_h, seed_h, cnt_h, buf_h, aw2_h, jw2_h, lw2_h,
    aw1_h, ab1_h, ab2_h, aw3_h, jw1_h, jb1_h, jb2_h, jw3_h, lw1_h, lb1_h, lb2_h, lw3_h,
    ab3_h, jb3_h, lb3_h, level,
    tab, got, idx_s, w1all, fa, f2, b2, head, headb, da_w, qw, col, scale, scal,
    idx_v, seed_v, cnt_v, buf, w2, aw1, ab1, ab2, aw3, jw1, jb1, jb2, jw3, lw1, lb1, lb2, lw3,
    ab3, jb3, lb3, msg, land, flat, tmp, rowbuf, in_sems, sems,
    *, n, cap,
):
    me = lax.axis_index("dp")
    rows = message_rows(cap)
    part = min(cap, 128)
    width = buf.shape[1]
    pairs = (
        (idx_h, idx_v), (seed_h, seed_v), (cnt_h, cnt_v), (buf_h, buf),
        (aw2_h, w2.at[0]), (jw2_h, w2.at[pl.ds(1, 2)]), (lw2_h, w2.at[pl.ds(3, 2)]),
        (aw1_h, aw1), (ab1_h, ab1), (ab2_h, ab2), (aw3_h, aw3), (jw1_h, jw1), (jb1_h, jb1), (jb2_h, jb2),
        (jw3_h, jw3), (lw1_h, lw1), (lb1_h, lb1), (lb2_h, lb2), (lw3_h, lw3),
        (ab3_h, ab3), (jb3_h, jb3), (lb3_h, lb3),
    )
    loads = [pltpu.make_async_copy(src, dst, in_sems.at[k]) for k, (src, dst) in enumerate(pairs)]
    for c in loads:
        c.start()
    barrier = pltpu.get_barrier_semaphore()

    @pl.loop(1, n)
    def _(k):
        pl.semaphore_signal(barrier, inc=1, device_id=(lax.rem(me + k, n),), device_id_type=pl.DeviceIdType.MESH)

    for c in loads[:3]:
        c.wait()
    msg[...] = jnp.zeros_like(msg)
    for r in range(rows):
        msg[:, r, 0:part] = idx_v[0, :, r * part : (r + 1) * part]
        msg[:, rows + r, 0:part] = seed_v[0, :, r * part : (r + 1) * part]
    diag = lax.broadcasted_iota(jnp.int32, (n, n), 0) == lax.broadcasted_iota(jnp.int32, (n, n), 1)
    counts = jnp.sum(jnp.where(diag, cnt_v[...].astype(F32), 0.0), axis=1, keepdims=True)
    msg[:, 2 * rows, :] = jnp.broadcast_to(counts, (n, 128)).astype(jnp.int32)
    for c in loads[4:]:
        c.wait()
    for l, (w1, b1, k) in enumerate(((aw1, ab1, None), (jw1, jb1, 0), (jw1, jb1, 1), (lw1, lb1, 0), (lw1, lb1, 1))):
        if k is None:
            tmp[0:6, :] = jnp.zeros((6, HID), F32)
            tmp[6:7, :] = b1[...]
            tmp[7:8, :] = w1[16:17, :]
            tmp[8:24, :] = w1[0:16, :]
        else:
            tmp[0:6, :] = w1[17:23, k, :]
            tmp[6:7, :] = b1[k : k + 1, :]
            tmp[7:8, :] = w1[16:17, k, :]
            tmp[8:24, :] = w1[0:16, k, :]
        hi, lo = split(0.5 * tmp[0:24, :])
        w1all[l * HID : (l + 1) * HID, :] = jnp.concatenate([hi, hi, lo], axis=0).T.astype(BF)
        if l in (1, 2):
            hi, lo = split(tmp[0:8, :])
            da_w[l - 1] = jnp.concatenate([hi, lo], axis=0).astype(BF)
    start = ((2 * me + 1).astype(F32) / n - 1.0) * 2.0**-8

    def roundings(ref, l, w):
        left = w.astype(BF).astype(F32) * start
        for v in range(VARIANTS):
            want = w + left
            got_ = want.astype(BF)
            ref[l, v] = got_
            left = want - got_.astype(F32)

    for l in range(5):
        w = 0.5 * w2[l]
        wt = w.T
        roundings(f2, l, wt)
        if l == 0:
            hi, lo = split(wt)
            fa[0:HID, :] = hi.astype(BF)
            fa[HID:, :] = lo.astype(BF)
        if l == 0:
            roundings(b2, l, w)
        elif l < 3:
            roundings(b2, l, w * (0.5 * jw3[l - 1 : l, :]))
    tmp[0:12, :] = aw3[...]
    r8 = lax.broadcasted_iota(jnp.int32, (8, HID), 0)
    w_head = jnp.concatenate([jnp.where(r8 < 6, tmp[0:8, :], 0.0), jnp.where(r8 < 6, tmp[6:14, :], 0.0)], axis=0)
    hi, lo = split(w_head)
    head[...] = jnp.concatenate([hi, lo], axis=0).astype(BF)
    headb[...] = (0.5 * jnp.concatenate([hi, lo], axis=0)).T.astype(BF)
    for k in range(4):
        w3 = jw3[k : k + 1, :] if k < 2 else lw3[k - 2 : k - 1, :]
        hi, lo = split(w3)
        qw[k] = jnp.concatenate([jnp.where(r8 == 0, hi, 0.0), jnp.where(r8 == 0, lo, 0.0)], axis=0).astype(BF)
    rowbuf[...] = jnp.zeros_like(rowbuf)
    rowbuf[0:1, :] = 0.5 * ab2[...]
    rowbuf[1:3, :] = 0.5 * jb2[...]
    rowbuf[3:5, :] = 0.5 * lb2[...]
    lane12 = lax.broadcasted_iota(jnp.int32, (1, HID), 1)
    hb = jnp.zeros((1, HID), F32)
    for k in range(12):
        hb = jnp.where(lane12 == (k if k < 6 else k + 2), ab3[k], hb)
    rowbuf[5:6, :] = hb
    col[...] = rowbuf[...].T
    scale[...] = jnp.zeros_like(scale)
    scale[0:2, :] = 0.5 * jw3[...]
    for k in range(2):
        scal[k] = jb3[k]
        scal[2 + k] = lb3[k]
    scal[4] = level[0]

    pl.semaphore_wait(barrier, n - 1)

    def copy(k):
        return pltpu.make_async_remote_copy(
            src_ref=msg.at[lax.rem(me + k, n)], dst_ref=land.at[k], send_sem=sems.at[0, k], recv_sem=sems.at[1, k],
            device_id=(lax.rem(me + k, n),), device_id_type=pl.DeviceIdType.MESH,
        )

    @pl.loop(1, n)
    def _(k):
        copy(k).start()

    loads[3].wait()

    @pl.loop(0, width // 128, unroll=4)
    def _(c):
        blk = buf[:, pl.ds(pl.multiple_of(c * 128, 128), 128)]
        tab[pl.ds(pl.multiple_of(c * 128, 128), 128), 0:42] = blk.T

    land[0] = msg[me]

    @pl.loop(1, n)
    def _(k):
        copy(k).wait()

    @pl.loop(0, n)
    def _(k):
        got[lax.rem(me - k + n, n)] = land[k]

    for r in range(rows):
        flat[:, r, :] = got[:, r, :]
    c = pltpu.make_async_copy(flat, idx_s, in_sems.at[0])
    c.start()
    c.wait()


def prepare(experience_buffer, sampled, seeds, counts, params):
    (aw1, ab1, aw2, ab2, aw3, ab3, jw1, jb1, jw2, jb2, jw3, jb3, lw1, lb1, lw2, lb2, lw3, lb3, level) = params
    feats, width = experience_buffer.shape
    _, n, cap = sampled.shape
    rows = message_rows(cap)
    vm = pl.BlockSpec(memory_space=pltpu.VMEM)
    sm = pl.BlockSpec(memory_space=pltpu.SMEM)
    hbm = pl.BlockSpec(memory_space=pl.ANY)
    out = [
        pltpu.VMEM((width, 128), F32),
        pltpu.VMEM((n, 8, 128), jnp.int32),
        pltpu.SMEM((n, rows, 128), jnp.int32),
        pltpu.VMEM((5 * HID, 72), BF),
        pltpu.VMEM((2 * HID, HID), BF),
        pltpu.VMEM((5, VARIANTS, HID, HID), BF),
        pltpu.VMEM((3, VARIANTS, HID, HID), BF),
        pltpu.VMEM((32, HID), BF),
        pltpu.VMEM((HID, 32), BF),
        pltpu.VMEM((2, 16, HID), BF),
        pltpu.VMEM((4, 16, HID), BF),
        pltpu.VMEM((HID, 8), F32),
        pltpu.VMEM((8, HID), F32),
        pltpu.SMEM((8,), F32),
    ]
    return pl.pallas_call(
        functools.partial(prepare_kernel, n=n, cap=cap),
        out_shape=out,
        in_specs=[hbm] * 22 + [sm],
        out_specs=[vm, vm, sm] + [vm] * 10 + [sm],
        scratch_shapes=[
            pltpu.VMEM((1, n, cap), jnp.int32),
            pltpu.VMEM((1, n, cap), jnp.int32),
            pltpu.VMEM((1, n), jnp.int32),
            pltpu.VMEM((feats, width), F32),
            pltpu.VMEM((5, HID, HID), F32),
            pltpu.VMEM((OBS, HID), F32),
            pltpu.VMEM((1, HID), F32),
            pltpu.VMEM((1, HID), F32),
            pltpu.VMEM((12, HID), F32),
            pltpu.VMEM((23, 2, HID), F32),
            pltpu.VMEM((2, HID), F32),
            pltpu.VMEM((2, HID), F32),
            pltpu.VMEM((2, HID), F32),
            pltpu.VMEM((23, 2, HID), F32),
            pltpu.VMEM((2, HID), F32),
            pltpu.VMEM((2, HID), F32),
            pltpu.VMEM((2, HID), F32),
            pltpu.SMEM((12,), F32),
            pltpu.SMEM((2,), F32),
            pltpu.SMEM((2,), F32),
            pltpu.VMEM((n, 8, 128), jnp.int32),
            pltpu.VMEM((n, 8, 128), jnp.int32),
            pltpu.VMEM((n, rows, 128), jnp.int32),
            pltpu.VMEM((24, HID), F32),
            pltpu.VMEM((8, HID), F32),
            pltpu.SemaphoreType.DMA((22,)),
            pltpu.SemaphoreType.DMA((2, n)),
        ],
        compiler_params=pltpu.CompilerParams(collective_id=2, has_side_effects=True, vmem_limit_bytes=24 << 20),
        name="exchange_and_prepare",
    )(
        *[
            pltpu.with_memory_space_constraint(x, pltpu.HBM)
            for x in (
                sampled, seeds, counts, experience_buffer, aw2, jw2, lw2,
                aw1, ab1.reshape(1, HID), ab2.reshape(1, HID), aw3.T,
                jw1.transpose(1, 0, 2), jb1, jb2, jw3, lw1.transpose(1, 0, 2), lb1, lb2, lw3,
                ab3, jb3, lb3,
            )
        ],
        level.reshape(1),
    )


def net_kernel(
    idx_s, scal, tab, got, w1all, fa, f2, b2, head, headb, da_w, qw, col, scale,
    packed,
    xrow, gw2, gw2b, gaw1, gcw1, gaw3, gcw3, gcol, gmisc,
    *, cap, slots,
):
    T = min(TILE, slots)
    nt = slots // T
    lists = T // cap
    rows = message_rows(cap)
    part = min(cap, 128)

    def gather(i):
        for t in range(T):
            r = idx_s[i * lists + t // cap, (t % cap) // 128, t % 128]
            xrow[t : t + 1, :] = tab[pl.ds(r, 1), :]

    gather(0)
    for ref in (gw2, gw2b, gaw1, gcw1, gaw3, gcw3, gcol, gmisc):
        ref[...] = jnp.zeros_like(ref)
    level = scal[4]
    jb3_s = (scal[0], scal[1])
    lb3_s = (scal[2], scal[3])

    def act32(u):
        t = jnp.tanh(u)
        p = 1.0 + t
        h = u * p
        return h, p + h * (2.0 - p)

    def act(u):
        h, d = act32(u)
        return h.astype(BF), d

    def layer2(i, l, h):
        return act(by_chunk(f2, l, i, h) + col[:, l : l + 1])

    def first(l0, l1, x24):
        hi, lo = split(x24)
        xs = jnp.concatenate([hi, lo, hi], axis=0).astype(BF)
        return dot(w1all[l0 * HID : l1 * HID, :], xs)

    def by_chunk(w, l, i, x):
        nq = T // HID
        return jnp.concatenate(
            [dot(w[l, lax.rem(i * nq + q, VARIANTS)], x[:, q * HID : (q + 1) * HID]) for q in range(nq)], axis=1
        )

    def exact(w, h):
        hb = h.astype(BF)
        r = dot(w[...], hb)
        half = r.shape[0] // 2
        lo = dot(w[0:half, :], (h - hb.astype(F32)).astype(BF))
        return hb, r[:half] + (r[half:] + lo)

    def head_out(o):
        o = o + col[0:16, 5:6]
        mean = o[0:8]
        t = jnp.tanh(o[8:16])
        ls = -5.0 + 3.5 * (t + 1.0)
        return mean, t, ls

    def sample(mean, ls, e, live):
        sg = jnp.exp(ls)
        u = mean + sg * e
        a = jnp.tanh(u)
        au = jnp.abs(u)
        sq = 2.0 * (math.log(2.0) - au - jnp.log(1.0 + jnp.exp(-2.0 * au)))
        lp = -0.5 * e * e - ls - 0.5 * math.log(2.0 * math.pi) - sq
        return a, sg, jnp.sum(jnp.where(live, lp, 0.0), axis=0, keepdims=True)

    def q_of(k, h2, b):
        r = dot(qw[k], h2)
        return r[0:1] + r[8:9] + b

    def softmin(q, w):
        a, b = -4.0 * q, -4.0 * w
        return -0.25 * (jnp.maximum(a, b) + jnp.log(1.0 + jnp.exp(-jnp.abs(a - b))))

    ones = jnp.ones((16, T), BF)

    @pl.loop(0, nt)
    def _(i):
        xt = xrow[...].T
        gather(jnp.minimum(i + 1, nt - 1))
        row8 = lax.broadcasted_iota(jnp.int32, (8, T), 0)
        row16 = lax.broadcasted_iota(jnp.int32, (16, T), 0)
        live = row8 < ACT
        seeds = jnp.concatenate([got[i * lists + k, rows + r : rows + r + 1, 0:part] for k in range(lists) for r in range(rows)], axis=1)
        lane = lax.broadcasted_iota(jnp.int32, (1, cap), 1)
        mask = jnp.concatenate(
            [jnp.where(lane < got[i * lists + k, 2 * rows : 2 * rows + 1, 0:1], 1.0, 0.0).astype(F32) for k in range(lists)], axis=1
        )
        alpha = jnp.exp(jnp.full((1, T), level, F32))
        b1 = pltpu.roll(xt[16:24], 7, 0)
        reward = b1[6:7]
        xa = jnp.concatenate([jnp.where(row8 == 6, 1.0, b1), xt[0:16]], axis=0)
        b2_ = pltpu.roll(xt[40:48], 7, 0)
        done = b2_[0:1]
        n_lo = jnp.where(row8 == 7, b2_, jnp.where(row8 == 6, 1.0, 0.0))
        xn = jnp.concatenate([n_lo, xt[24:40]], axis=0)

        un = first(0, 1, xn)
        hi, lo = split(xa)
        xw = jnp.concatenate([hi, lo], axis=0).astype(BF)
        ua = dot(w1all[0 : 3 * HID, :], jnp.concatenate([hi, lo, hi], axis=0).astype(BF))
        eps = noise(seeds, row16)
        e = eps[0:8]
        hn, _ = act(un)
        h1a, d1a = act32(ua[0:HID])
        h1c, d1c = zip(*[act(ua[(1 + k) * HID : (2 + k) * HID]) for k in range(2)])
        hn, _ = layer2(i, 0, hn)
        r = dot(head[...], hn)
        mean, _, ls = head_out(r[0:16] + r[16:32])
        a2, _, lp2 = sample(mean, ls, eps[8:16], live)
        h1a, r = exact(fa, h1a)
        h2a, d2a = act32(r + col[:, 0:1])
        h2a, r = exact(head, h2a)
        mean, t, ls = head_out(r)
        a1, sg, lp = sample(mean, ls, e, live)
        un = first(3, 5, jnp.concatenate([jnp.where(live, a2, n_lo), xt[24:40]], axis=0))
        h2c, d2c = zip(*[layer2(i, 1 + k, h1c[k]) for k in range(2)])
        qc = [q_of(k, h2c[k], jb3_s[k]) for k in range(2)]
        uq = first(1, 3, jnp.concatenate([jnp.where(live, a1, xa[0:8]), xt[0:16]], axis=0))
        ht = [act(un[k * HID : (k + 1) * HID])[0] for k in range(2)]
        ht = [layer2(i, 3 + k, ht[k])[0] for k in range(2)]
        qt = [q_of(2 + k, ht[k], lb3_s[k]) for k in range(2)]
        h1q, d1q = zip(*[act(uq[k * HID : (k + 1) * HID]) for k in range(2)])
        y = reward + GAMMA * (1.0 - done) * (softmin(qt[0], qt[1]) - alpha * lp2)
        h2q, d2q = zip(*[layer2(i, 1 + k, h1q[k]) for k in range(2)])
        qq = [q_of(k, h2q[k], jb3_s[k]) for k in range(2)]

        closs = jnp.zeros((1, T), F32)
        g2c = []
        for k in range(2):
            dq = qc[k] - y
            mdq = dq * mask
            closs = closs + 0.5 * (mdq * dq)
            g2 = (mdq * d2c[k]).astype(BF)
            g2c.append(g2)
            mhi, mlo = split(mdq)
            m16 = jnp.where(row16 == 0, mhi, jnp.where(row16 == 1, mlo, 0.0)).astype(BF)
            gcw3[k] += dot_t(m16, h2c[k])
            r = dot_t(jnp.concatenate([h1c[k], ones], axis=0), g2)
            gw2[1 + k] += r[0:HID]
            gw2b[1 + k] += r[HID : HID + 8]
            gmisc[k : k + 1, :] += fold(mdq)
        sm = softmin(qq[0], qq[1])
        p0 = 1.0 / (1.0 + jnp.exp(4.0 * (qq[0] - qq[1])))
        da = jnp.zeros((8, T), F32)
        for k, pk in enumerate((p0, 1.0 - p0)):
            g1 = (by_chunk(b2, 1 + k, i, d2q[k].astype(BF)) * d1q[k]).astype(BF)
            w = dot(da_w[k], g1)
            da = da - (pk * mask) * (w[0:8] + w[8:16])
        for k in range(2):
            g1 = (by_chunk(b2, 1 + k, i, g2c[k]) * d1c[k]).astype(BF)
            w = dot_t(xw, g1)
            gcw1[k] += w[0:24] + w[24:48]
        ma = mask * alpha
        du = da * (1.0 - a1 * a1) + ma * (2.0 * a1)
        dls = (du * sg * e - ma) * (3.5 * (1.0 - t * t))
        do = jnp.concatenate([jnp.where(live, du, 0.0), jnp.where(live, dls, 0.0)], axis=0)
        gcol[...] += fold(do)
        dob = do.astype(BF)
        gaw3[...] += dot_t(dob, h2a)
        g2 = (dot(headb[...], jnp.concatenate([dob, dob], axis=0)) * d2a).astype(BF)
        r = dot_t(jnp.concatenate([h1a, ones], axis=0), g2)
        gw2[0] += r[0:HID]
        gw2b[0] += r[HID : HID + 8]
        g1 = (by_chunk(b2, 0, i, g2) * d1a).astype(BF)
        w = dot_t(xw, g1)
        gaw1[...] += w[0:24] + w[24:48]
        gmisc[2:3, :] += fold(closs)
        gmisc[3:4, :] += fold(mask * (alpha * lp - sm))
        gmisc[4:5, :] += fold(mask * (lp - 6.0))
        gmisc[5:6, :] += fold(mask)

    row8 = lax.broadcasted_iota(jnp.int32, (8, HID), 0)
    cols = jnp.zeros((8, HID), F32)
    for k in range(2):
        s = scale[k : k + 1, :]
        cols = jnp.where(row8 == k, gw2b[1 + k] * s, cols)
        cols = jnp.where(row8 == 2 + k, gcw3[k, 0:1, :] + gcw3[k, 1:2, :], cols)
    cols = jnp.where(row8 == 4, gw2b[0], cols)
    for m in range(3):
        for h in range(2):
            w = gw2[m, :, h * 128 : (h + 1) * 128]
            if m > 0:
                w = w * scale[m - 1 : m, h * 128 : (h + 1) * 128]
            packed[(2 * m + h) * HID : (2 * m + h + 1) * HID, :] = w
    for h in range(2):
        packed[R_AW1 + 24 * h : R_AW1 + 24 * (h + 1), :] = gaw1[:, h * 128 : (h + 1) * 128]
        for k in range(2):
            at = R_CW1 + 48 * k + 24 * h
            packed[at : at + 24, :] = gcw1[k, :, h * 128 : (h + 1) * 128]
        packed[R_AW3 + 16 * h : R_AW3 + 16 * (h + 1), :] = gaw3[:, h * 128 : (h + 1) * 128]
        packed[R_COL + 8 * h : R_COL + 8 * (h + 1), :] = cols[:, h * 128 : (h + 1) * 128]
    packed[R_AB3 : R_AB3 + 16, :] = gcol[...]
    packed[R_MISC : R_MISC + 8, :] = gmisc[...]
    packed[R_END:, :] = jnp.zeros((packed.shape[0] - R_END, 128), F32)


def local_grads(ready, n, cap, packed_rows):
    tab, got, idx_s, *weights, scal = ready
    slots = n * cap
    T = min(TILE, slots)
    vm = pl.BlockSpec(memory_space=pltpu.VMEM)
    sm = pl.BlockSpec(memory_space=pltpu.SMEM)
    return pl.pallas_call(
        functools.partial(net_kernel, cap=cap, slots=slots),
        out_shape=pltpu.VMEM((packed_rows, 128), F32),
        in_specs=[sm] * 2 + [vm] * (2 + len(weights)),
        out_specs=vm,
        scratch_shapes=[
            pltpu.VMEM((T, 128), F32),
            pltpu.VMEM((3, HID, HID), F32),
            pltpu.VMEM((3, 8, HID), F32),
            pltpu.VMEM((24, HID), F32),
            pltpu.VMEM((2, 24, HID), F32),
            pltpu.VMEM((16, HID), F32),
            pltpu.VMEM((2, 16, HID), F32),
            pltpu.VMEM((16, 128), F32),
            pltpu.VMEM((8, 128), F32),
        ],
        compiler_params=pltpu.CompilerParams(vmem_limit_bytes=34 << 20),
        name="networks",
    )(idx_s, scal, tab, got, *weights)


def split_sizes(n):
    sizes = [2]
    n //= 2
    while n > 1:
        f = 4 if n % 4 == 0 else n if n < 4 else 2
        sizes.append(f)
        n //= f
    return sizes


def chunk_rows(rows):
    units = rows // 8
    k = min(CHUNKS, units)
    cuts = [8 * (units * j // k) for j in range(k + 1)]
    return list(zip(cuts[:-1], cuts[1:]))


def sum_kernel(sizes, mine, out, *rest):
    ns = len(sizes)
    got, part, sems = rest[:ns], rest[ns : 2 * ns], rest[2 * ns]
    n = mine.shape[0]
    parts = chunk_rows(mine.shape[1])
    me = lax.axis_index("dp")
    digits, strides, st = [], [], 1
    for f in sizes:
        digits.append(lax.rem(me // st, f))
        strides.append(st)
        st *= f

    def member(s, k):
        d = lax.rem(digits[s] + k, sizes[s])
        return d, me + (d - digits[s]) * strides[s]

    barrier = pltpu.get_barrier_semaphore()
    count = 0
    for s in range(ns):
        for k in range(1, sizes[s]):
            pl.semaphore_signal(barrier, inc=1, device_id=(member(s, k)[1],), device_id_type=pl.DeviceIdType.MESH)
            count += 1
    pl.semaphore_wait(barrier, count)

    def send(src, dst, s, k, phase, c):
        copy = pltpu.make_async_remote_copy(
            src_ref=src, dst_ref=dst, send_sem=sems.at[phase, c, s, k, 0], recv_sem=sems.at[phase, c, s, k, 1],
            device_id=(member(s, k)[1],), device_id_type=pl.DeviceIdType.MESH,
        )
        copy.start()
        return copy

    spans, starts = [n], [0]
    for s in range(ns):
        spans.append(spans[s] // sizes[s])
        starts.append(starts[s] + digits[s] * spans[s + 1])
    done, flying = [], {}

    def scatter(s, c):
        lo, hi = parts[c]
        src = mine if s == 0 else part[s - 1]
        flying[0, s, c] = [
            send(src.at[pl.ds(member(s, k)[0] * spans[s + 1], spans[s + 1]), lo:hi], got[s].at[k - 1, :, lo:hi], s, k, 0, c)
            for k in range(1, sizes[s])
        ]

    def add(s, c):
        lo, hi = parts[c]
        src = mine if s == 0 else part[s - 1]
        acc = src[pl.ds(digits[s] * spans[s + 1], spans[s + 1]), lo:hi]
        for k, copy in enumerate(flying[0, s, c]):
            copy.wait_recv()
            acc = acc + got[s][k, :, lo:hi]
            done.append(copy)
        if s == ns - 1:
            out[pl.ds(starts[ns], 1), lo:hi] = acc
        else:
            part[s][:, lo:hi] = acc

    def spread(s, c):
        lo, hi = parts[c]
        at = out.at[pl.ds(starts[s + 1], spans[s + 1]), lo:hi]
        flying[1, s, c] = [send(at, at, s, k, 1, c) for k in range(1, sizes[s])]

    def arrive(s, c):
        for copy in flying[1, s, c]:
            copy.wait_recv()
            done.append(copy)

    chunks = range(len(parts))
    for c in chunks:
        scatter(0, c)
    for s in range(ns):
        for c in chunks:
            add(s, c)
            if s < ns - 1:
                scatter(s + 1, c)
            else:
                spread(ns - 1, c)
    for s in reversed(range(ns)):
        for c in chunks:
            arrive(s, c)
            if s > 0:
                spread(s - 1, c)
    for copy in done:
        copy.wait_send()


def sum_over_devices(packed, n):
    sizes = split_sizes(n)
    rows = packed.shape[0] // n
    mine = packed.reshape(n, rows, 128)
    got, part, size = [], [], n
    for f in sizes:
        size //= f
        got.append(pltpu.VMEM((f - 1, size, rows, 128), F32))
        part.append(pltpu.VMEM((size, rows, 128), F32))
    vm = pl.BlockSpec(memory_space=pltpu.VMEM)
    out = pl.pallas_call(
        functools.partial(sum_kernel, sizes),
        out_shape=pltpu.VMEM((n, rows, 128), F32),
        in_specs=[vm],
        out_specs=vm,
        scratch_shapes=got + part + [pltpu.SemaphoreType.DMA((2, len(chunk_rows(rows)), len(sizes), max(sizes), 2))],
        compiler_params=pltpu.CompilerParams(collective_id=1, has_side_effects=True, vmem_limit_bytes=24 << 20),
        name="sum_over_devices",
    )(mine)
    return out.reshape(packed.shape)


def finish_kernel(scal, g, aw1, ab1, aw2, ab2, aw3, ab3, cw1, cb1, cw2, cb2, cw3, cb3, da, losses):
    misc = jnp.sum(g[R_MISC : R_MISC + 8, :], axis=1, keepdims=True)
    n = misc[5:6]
    inv = 1.0 / n

    def rows(at, count):
        return jnp.concatenate([g[at : at + count, :], g[at + count : at + 2 * count, :]], axis=1) * inv

    aw2[...] = rows(0, HID)
    cw2[0] = rows(2 * HID, HID)
    cw2[1] = rows(4 * HID, HID)
    w = rows(R_AW1, 24)
    aw1[0:16, :] = w[8:24]
    aw1[16:17, :] = w[7:8]
    ab1[...] = w[6:7]
    for k in range(2):
        w = rows(R_CW1 + 48 * k, 24)
        cw1[0:16, k, :] = w[8:24]
        cw1[16:17, k, :] = w[7:8]
        cw1[17:23, k, :] = w[0:6]
        cb1[k : k + 1, :] = w[6:7]
    w = rows(R_AW3, 16)
    aw3[0:6, :] = w[0:6]
    aw3[6:12, :] = w[8:14]
    c = rows(R_COL, 8)
    cb2[...] = c[0:2]
    cw3[...] = c[2:4]
    ab2[...] = c[4:5]
    b = jnp.sum(g[R_AB3 : R_AB3 + 16, :], axis=1, keepdims=True) * inv
    diag = lax.broadcasted_iota(jnp.int32, (16, 128), 0) == lax.broadcasted_iota(jnp.int32, (16, 128), 1)
    b = jnp.sum(jnp.where(diag, b, 0.0), axis=0, keepdims=True)
    ab3[...] = jnp.concatenate([b[:, 0:6], b[:, 8:14]], axis=1)
    m = misc * inv
    cb3[...] = jnp.concatenate([m[0:1], m[1:2]], axis=1)
    da[...] = -m[4:5]
    losses[...] = jnp.concatenate([m[2:3], m[3:4], -scal[4] * m[4:5]], axis=1)


def finish(total, scal):
    vm = pl.BlockSpec(memory_space=pltpu.VMEM)
    shapes = [
        (OBS, HID), (1, HID), (HID, HID), (1, HID), (12, HID), (1, 12),
        (23, 2, HID), (2, HID), (2, HID, HID), (2, HID), (2, HID), (1, 2), (1, 1), (1, 3),
    ]
    outs = list(pl.pallas_call(
        finish_kernel,
        out_shape=[jax.ShapeDtypeStruct(x, F32) for x in shapes],
        in_specs=[pl.BlockSpec(memory_space=pltpu.SMEM), vm],
        out_specs=[vm] * len(shapes),
        name="finish",
    )(scal, total))
    outs[4] = outs[4].T
    outs[6] = outs[6].transpose(1, 0, 2)
    for k, shape in ((1, (HID,)), (3, (HID,)), (5, (12,)), (11, (2,)), (12, ()), (13, (3,))):
        outs[k] = outs[k].reshape(shape)
    return tuple(outs)


def body(experience_buffer, sampled_indices, filled_lengths, randomizer_numbers, *params):
    n, cap = sampled_indices.shape[1:]
    ready = prepare(experience_buffer, sampled_indices, randomizer_numbers, filled_lengths, params)
    packed = local_grads(ready, n, cap, n * 8 * (-(-R_END // (8 * n))))
    return finish(sum_over_devices(packed, n), ready[-1])


def solution(mesh):
    in_specs = (P(None, "dp"), P("dp", None, None), P("dp", None), P("dp", None, None)) + (P(),) * 19
    return jax.shard_map(body, mesh=mesh, in_specs=in_specs, out_specs=(P(),) * 14, check_vma=False)
```

```python
import functools
import math

import jax
import jax.numpy as jnp
from jax import lax
from jax.experimental import pallas as pl
from jax.experimental.pallas import tpu as pltpu
from jax.sharding import PartitionSpec as P

OBS = 17
ACT = 6
HID = 256
GAMMA = 0.99
PRIME = 65521
TILE = 1024
CHUNKS = 4
VARIANTS = 8
R_CW1 = 4 * HID
R_CCOL = R_CW1 + 96
R_CEND = R_CCOL + 16
R_AW1 = 2 * HID
R_AW3 = R_AW1 + 48
R_ACOL = R_AW3 + 32
R_AB3 = R_ACOL + 16
R_MISC = R_AB3 + 16
R_AEND = R_MISC + 8
BF = jnp.bfloat16
F32 = jnp.float32


def dot(a, b):
    return jnp.dot(a, b, preferred_element_type=F32)


def dot_t(a, b):
    return lax.dot_general(a, b, (((1,), (1,)), ((), ())), preferred_element_type=F32)


def split(x):
    hi = x.astype(BF).astype(F32)
    return hi, x - hi


def fold_prime(x):
    return (x >> 16) * 15 + (x & 65535)


def below_prime(x):
    return jnp.where(x >= PRIME, x - PRIME, x)


def noise(seeds, rows):
    comp = jnp.where(rows >= 8, rows - 2, rows)
    z = below_prime(fold_prime(seeds))
    h0 = below_prime(fold_prime(z * 257 + comp * 7919 + 1))
    h1 = below_prime(fold_prime(fold_prime(h0 * 32749 + 12345)))
    h2 = below_prime(fold_prime(fold_prime(h1 * 32749 + 54321)))
    u1 = (h1.astype(F32) + 0.5) * (1.0 / PRIME)
    x = jnp.abs((2 * h2 + (1 - PRIME)).astype(F32)) * (math.pi / PRIME) - 0.5 * math.pi
    x2 = x * x
    p = -1.0 / 39916800.0
    for c in (1.0 / 362880.0, -1.0 / 5040.0, 1.0 / 120.0, -1.0 / 6.0, 1.0):
        p = p * x2 + c
    return jnp.sqrt(-2.0 * jnp.log(u1)) * (p * x)


def fold(x):
    return functools.reduce(lambda a, b: a + b, [x[:, k * 128 : (k + 1) * 128] for k in range(x.shape[1] // 128)])


def message_rows(cap):
    return -(-cap // 128)


def prepare_kernel(
    idx_h, seed_h, cnt_h, buf_h, aw2_h, jw2_h, lw2_h,
    aw1_h, ab1_h, ab2_h, aw3_h, jw1_h, jb1_h, jb2_h, jw3_h, lw1_h, lb1_h, lb2_h, lw3_h,
    ab3_h, jb3_h, lb3_h, level,
    tab, got, idx_s, w1all, fa, f2, b2, head, headb, da_w, qw, col, scale, scal,
    idx_v, seed_v, cnt_v, buf, w2, aw1, ab1, ab2, aw3, jw1, jb1, jb2, jw3, lw1, lb1, lb2, lw3,
    ab3, jb3, lb3, msg, land, flat, tmp, rowbuf, in_sems, sems,
    *, n, cap,
):
    me = lax.axis_index("dp")
    rows = message_rows(cap)
    part = min(cap, 128)
    width = buf.shape[1]
    pairs = (
        (idx_h, idx_v), (seed_h, seed_v), (cnt_h, cnt_v), (buf_h, buf),
        (aw2_h, w2.at[0]), (jw2_h, w2.at[pl.ds(1, 2)]), (lw2_h, w2.at[pl.ds(3, 2)]),
        (aw1_h, aw1), (ab1_h, ab1), (ab2_h, ab2), (aw3_h, aw3), (jw1_h, jw1), (jb1_h, jb1), (jb2_h, jb2),
        (jw3_h, jw3), (lw1_h, lw1), (lb1_h, lb1), (lb2_h, lb2), (lw3_h, lw3),
        (ab3_h, ab3), (jb3_h, jb3), (lb3_h, lb3),
    )
    loads = [pltpu.make_async_copy(src, dst, in_sems.at[k]) for k, (src, dst) in enumerate(pairs)]
    for c in loads:
        c.start()
    barrier = pltpu.get_barrier_semaphore()

    @pl.loop(1, n)
    def _(k):
        pl.semaphore_signal(barrier, inc=1, device_id=(lax.rem(me + k, n),), device_id_type=pl.DeviceIdType.MESH)

    for c in loads[:3]:
        c.wait()
    msg[...] = jnp.zeros_like(msg)
    for r in range(rows):
        msg[:, r, 0:part] = idx_v[0, :, r * part : (r + 1) * part]
        msg[:, rows + r, 0:part] = seed_v[0, :, r * part : (r + 1) * part]
    diag = lax.broadcasted_iota(jnp.int32, (n, n), 0) == lax.broadcasted_iota(jnp.int32, (n, n), 1)
    counts = jnp.sum(jnp.where(diag, cnt_v[...].astype(F32), 0.0), axis=1, keepdims=True)
    msg[:, 2 * rows, :] = jnp.broadcast_to(counts, (n, 128)).astype(jnp.int32)
    for c in loads[4:]:
        c.wait()
    for l, (w1, b1, k) in enumerate(((aw1, ab1, None), (jw1, jb1, 0), (jw1, jb1, 1), (lw1, lb1, 0), (lw1, lb1, 1))):
        if k is None:
            tmp[0:6, :] = jnp.zeros((6, HID), F32)
            tmp[6:7, :] = b1[...]
            tmp[7:8, :] = w1[16:17, :]
            tmp[8:24, :] = w1[0:16, :]
        else:
            tmp[0:6, :] = w1[17:23, k, :]
            tmp[6:7, :] = b1[k : k + 1, :]
            tmp[7:8, :] = w1[16:17, k, :]
            tmp[8:24, :] = w1[0:16, k, :]
        hi, lo = split(0.5 * tmp[0:24, :])
        w1all[l * HID : (l + 1) * HID, :] = jnp.concatenate([hi, hi, lo], axis=0).T.astype(BF)
        if l in (1, 2):
            hi, lo = split(tmp[0:8, :])
            da_w[l - 1] = jnp.concatenate([hi, lo], axis=0).astype(BF)
    start = ((2 * me + 1).astype(F32) / n - 1.0) * 2.0**-8

    def roundings(ref, l, w):
        left = w.astype(BF).astype(F32) * start
        for v in range(VARIANTS):
            want = w + left
            got_ = want.astype(BF)
            ref[l, v] = got_
            left = want - got_.astype(F32)

    for l in range(5):
        w = 0.5 * w2[l]
        wt = w.T
        roundings(f2, l, wt)
        if l == 0:
            hi, lo = split(wt)
            fa[0:HID, :] = hi.astype(BF)
            fa[HID:, :] = lo.astype(BF)
        if l == 0:
            roundings(b2, l, w)
        elif l < 3:
            roundings(b2, l, w * (0.5 * jw3[l - 1 : l, :]))
    tmp[0:12, :] = aw3[...]
    r8 = lax.broadcasted_iota(jnp.int32, (8, HID), 0)
    w_head = jnp.concatenate([jnp.where(r8 < 6, tmp[0:8, :], 0.0), jnp.where(r8 < 6, tmp[6:14, :], 0.0)], axis=0)
    hi, lo = split(w_head)
    head[...] = jnp.concatenate([hi, lo], axis=0).astype(BF)
    headb[...] = (0.5 * jnp.concatenate([hi, lo], axis=0)).T.astype(BF)
    for k in range(4):
        w3 = jw3[k : k + 1, :] if k < 2 else lw3[k - 2 : k - 1, :]
        hi, lo = split(w3)
        qw[k] = jnp.concatenate([jnp.where(r8 == 0, hi, 0.0), jnp.where(r8 == 0, lo, 0.0)], axis=0).astype(BF)
    rowbuf[...] = jnp.zeros_like(rowbuf)
    rowbuf[0:1, :] = 0.5 * ab2[...]
    rowbuf[1:3, :] = 0.5 * jb2[...]
    rowbuf[3:5, :] = 0.5 * lb2[...]
    lane12 = lax.broadcasted_iota(jnp.int32, (1, HID), 1)
    hb = jnp.zeros((1, HID), F32)
    for k in range(12):
        hb = jnp.where(lane12 == (k if k < 6 else k + 2), ab3[k], hb)
    rowbuf[5:6, :] = hb
    col[...] = rowbuf[...].T
    scale[...] = jnp.zeros_like(scale)
    scale[0:2, :] = 0.5 * jw3[...]
    for k in range(2):
        scal[k] = jb3[k]
        scal[2 + k] = lb3[k]
    scal[4] = level[0]

    pl.semaphore_wait(barrier, n - 1)

    def copy(k):
        return pltpu.make_async_remote_copy(
            src_ref=msg.at[lax.rem(me + k, n)], dst_ref=land.at[k], send_sem=sems.at[0, k], recv_sem=sems.at[1, k],
            device_id=(lax.rem(me + k, n),), device_id_type=pl.DeviceIdType.MESH,
        )

    @pl.loop(1, n)
    def _(k):
        copy(k).start()

    loads[3].wait()

    @pl.loop(0, width // 128, unroll=4)
    def _(c):
        blk = buf[:, pl.ds(pl.multiple_of(c * 128, 128), 128)]
        tab[pl.ds(pl.multiple_of(c * 128, 128), 128), 0:42] = blk.T

    land[0] = msg[me]

    @pl.loop(1, n)
    def _(k):
        copy(k).wait()

    @pl.loop(0, n)
    def _(k):
        got[lax.rem(me - k + n, n)] = land[k]

    for r in range(rows):
        flat[:, r, :] = got[:, r, :]
    c = pltpu.make_async_copy(flat, idx_s, in_sems.at[0])
    c.start()
    c.wait()


def prepare(experience_buffer, sampled, seeds, counts, params):
    (aw1, ab1, aw2, ab2, aw3, ab3, jw1, jb1, jw2, jb2, jw3, jb3, lw1, lb1, lw2, lb2, lw3, lb3, level) = params
    feats, width = experience_buffer.shape
    _, n, cap = sampled.shape
    rows = message_rows(cap)
    vm = pl.BlockSpec(memory_space=pltpu.VMEM)
    sm = pl.BlockSpec(memory_space=pltpu.SMEM)
    hbm = pl.BlockSpec(memory_space=pl.ANY)
    out = [
        pltpu.VMEM((width, 128), F32),
        pltpu.VMEM((n, 8, 128), jnp.int32),
        pltpu.SMEM((n, rows, 128), jnp.int32),
        pltpu.VMEM((5 * HID, 72), BF),
        pltpu.VMEM((2 * HID, HID), BF),
        pltpu.VMEM((5, VARIANTS, HID, HID), BF),
        pltpu.VMEM((3, VARIANTS, HID, HID), BF),
        pltpu.VMEM((32, HID), BF),
        pltpu.VMEM((HID, 32), BF),
        pltpu.VMEM((2, 16, HID), BF),
        pltpu.VMEM((4, 16, HID), BF),
        pltpu.VMEM((HID, 8), F32),
        pltpu.VMEM((8, HID), F32),
        pltpu.SMEM((8,), F32),
    ]
    return pl.pallas_call(
        functools.partial(prepare_kernel, n=n, cap=cap),
        out_shape=out,
        in_specs=[hbm] * 22 + [sm],
        out_specs=[vm, vm, sm] + [vm] * 10 + [sm],
        scratch_shapes=[
            pltpu.VMEM((1, n, cap), jnp.int32),
            pltpu.VMEM((1, n, cap), jnp.int32),
            pltpu.VMEM((1, n), jnp.int32),
            pltpu.VMEM((feats, width), F32),
            pltpu.VMEM((5, HID, HID), F32),
            pltpu.VMEM((OBS, HID), F32),
            pltpu.VMEM((1, HID), F32),
            pltpu.VMEM((1, HID), F32),
            pltpu.VMEM((12, HID), F32),
            pltpu.VMEM((23, 2, HID), F32),
            pltpu.VMEM((2, HID), F32),
            pltpu.VMEM((2, HID), F32),
            pltpu.VMEM((2, HID), F32),
            pltpu.VMEM((23, 2, HID), F32),
            pltpu.VMEM((2, HID), F32),
            pltpu.VMEM((2, HID), F32),
            pltpu.VMEM((2, HID), F32),
            pltpu.SMEM((12,), F32),
            pltpu.SMEM((2,), F32),
            pltpu.SMEM((2,), F32),
            pltpu.VMEM((n, 8, 128), jnp.int32),
            pltpu.VMEM((n, 8, 128), jnp.int32),
            pltpu.VMEM((n, rows, 128), jnp.int32),
            pltpu.VMEM((24, HID), F32),
            pltpu.VMEM((8, HID), F32),
            pltpu.SemaphoreType.DMA((22,)),
            pltpu.SemaphoreType.DMA((2, n)),
        ],
        compiler_params=pltpu.CompilerParams(collective_id=2, has_side_effects=True, vmem_limit_bytes=24 << 20),
        name="exchange_and_prepare",
    )(
        *[
            pltpu.with_memory_space_constraint(x, pltpu.HBM)
            for x in (
                sampled, seeds, counts, experience_buffer, aw2, jw2, lw2,
                aw1, ab1.reshape(1, HID), ab2.reshape(1, HID), aw3.T,
                jw1.transpose(1, 0, 2), jb1, jb2, jw3, lw1.transpose(1, 0, 2), lb1, lb2, lw3,
                ab3, jb3, lb3,
            )
        ],
        level.reshape(1),
    )


def split_sizes(n):
    sizes = [2]
    n //= 2
    while n > 1:
        f = 4 if n % 4 == 0 else n if n < 4 else 2
        sizes.append(f)
        n //= f
    return sizes


def chunk_rows(rows, chunks):
    units = rows // 8
    k = min(chunks, units)
    cuts = [8 * (units * j // k) for j in range(k + 1)]
    return list(zip(cuts[:-1], cuts[1:]))


def piece_rows(end, n):
    return 8 * (-(-end // (8 * n)))


class DeviceSum:
    def __init__(self, sizes, parts, mine, out, got, part, sems):
        self.sizes, self.parts, self.mine, self.out, self.got, self.part, self.sems = sizes, parts, mine, out, got, part, sems
        self.me = lax.axis_index("dp")
        self.digits, self.strides, st = [], [], 1
        for f in sizes:
            self.digits.append(lax.rem(self.me // st, f))
            self.strides.append(st)
            st *= f
        self.spans, self.starts = [mine.shape[0]], [0]
        for s, f in enumerate(sizes):
            self.spans.append(self.spans[s] // f)
            self.starts.append(self.starts[s] + self.digits[s] * self.spans[s + 1])

    def member(self, s, k):
        d = lax.rem(self.digits[s] + k, self.sizes[s])
        return d, self.me + (d - self.digits[s]) * self.strides[s]

    def partners(self):
        return [self.member(s, k)[1] for s in range(len(self.sizes)) for k in range(1, self.sizes[s])]

    def copy(self, phase, s, k, c):
        lo, hi = self.parts[c]
        d, to = self.member(s, k)
        if phase == 0:
            src = self.source(s).at[pl.ds(d * self.spans[s + 1], self.spans[s + 1]), lo:hi]
            dst = self.got[s].at[k - 1, :, lo:hi]
        else:
            src = dst = self.out.at[pl.ds(self.starts[s + 1], self.spans[s + 1]), lo:hi]
        return pltpu.make_async_remote_copy(
            src_ref=src, dst_ref=dst, send_sem=self.sems.at[phase, c, s, k, 0], recv_sem=self.sems.at[phase, c, s, k, 1],
            device_id=(to,), device_id_type=pl.DeviceIdType.MESH,
        )

    def source(self, s):
        return self.mine if s == 0 else self.part[s - 1]

    def start(self, phase, s, c):
        for k in range(1, self.sizes[s]):
            self.copy(phase, s, k, c).start()

    def add(self, s, c):
        lo, hi = self.parts[c]
        span = self.spans[s + 1]
        acc = self.source(s)[pl.ds(self.digits[s] * span, span), lo:hi]
        for k in range(1, self.sizes[s]):
            self.copy(0, s, k, c).wait_recv()
            acc = acc + self.got[s][k - 1, :, lo:hi]
        if s == len(self.sizes) - 1:
            self.out[pl.ds(self.starts[s + 1], 1), lo:hi] = acc
        else:
            self.part[s][:, lo:hi] = acc

    def step(self, j, c):
        ns = len(self.sizes)
        if 1 <= j <= ns:
            self.add(j - 1, c)
        if j > ns:
            for k in range(1, self.sizes[2 * ns - j]):
                self.copy(1, 2 * ns - j, k, c).wait_recv()
        if j < ns:
            self.start(0, j, c)
        elif j < 2 * ns:
            self.start(1, 2 * ns - 1 - j, c)

    def steps(self):
        return 2 * len(self.sizes)

    def all_sent(self):
        for phase in range(2):
            for s in range(len(self.sizes)):
                for k in range(1, self.sizes[s]):
                    for c in range(len(self.parts)):
                        self.copy(phase, s, k, c).wait_send()


def sum_scratch(n, rows, chunks):
    sizes = split_sizes(n)
    got, part, size = [], [], n
    for f in sizes:
        size //= f
        got.append(pltpu.VMEM((f - 1, size, rows, 128), F32))
        part.append(pltpu.VMEM((size, rows, 128), F32))
    sems = pltpu.SemaphoreType.DMA((2, len(chunk_rows(rows, chunks)), len(sizes), max(sizes), 2))
    return [pltpu.VMEM((n, rows, 128), F32)] + got + part + [sems]


def put(dst, at, value):
    rows = dst.shape[1]
    r = 0
    while r < value.shape[0]:
        p, o = divmod(at + r, rows)
        k = min(rows - o, value.shape[0] - r)
        dst[p, o : o + k, :] = value[r : r + k]
        r += k


def net_kernel(
    idx_s, scal, tab, got, w1all, fa, f2, b2, head, headb, da_w, qw, col, scale,
    sum_c, sum_a,
    xrow, xkeep, ekeep, gw2, gw2b, gaw1, gcw1, gaw3, gcw3, gcol, gmisc, *rest,
    n, cap, slots,
):
    T = min(TILE, slots)
    nt = slots // T
    lists = T // cap
    rows = message_rows(cap)
    part = min(cap, 128)
    sizes = split_sizes(n)
    ns = len(sizes)
    per = 2 * ns + 2
    critic_sum, actor_sum = (
        DeviceSum(sizes, chunk_rows(r[0].shape[1], k), r[0], out, r[1 : 1 + ns], r[1 + ns : 1 + 2 * ns], r[1 + 2 * ns])
        for r, out, k in ((rest[:per], sum_c, 1), (rest[per:], sum_a, CHUNKS))
    )
    barrier = pltpu.get_barrier_semaphore()
    partners = critic_sum.partners()
    for to in partners:
        pl.semaphore_signal(barrier, inc=1, device_id=(to,), device_id_type=pl.DeviceIdType.MESH)

    def gather(i):
        for t in range(T):
            r = idx_s[i * lists + t // cap, (t % cap) // 128, t % 128]
            xrow[t : t + 1, :] = tab[pl.ds(r, 1), :]

    gather(0)
    for ref in (gw2, gw2b, gaw1, gcw1, gaw3, gcw3, gcol, gmisc):
        ref[...] = jnp.zeros_like(ref)
    level = scal[4]
    jb3_s = (scal[0], scal[1])
    lb3_s = (scal[2], scal[3])

    def act32(u):
        t = jnp.tanh(u)
        p = 1.0 + t
        h = u * p
        return h, p + h * (2.0 - p)

    def act(u):
        h, d = act32(u)
        return h.astype(BF), d

    def layer2(i, l, h):
        return act(by_chunk(f2, l, i, h) + col[:, l : l + 1])

    def first(l0, l1, x24):
        hi, lo = split(x24)
        xs = jnp.concatenate([hi, lo, hi], axis=0).astype(BF)
        return dot(w1all[l0 * HID : l1 * HID, :], xs)

    def by_chunk(w, l, i, x):
        nq = T // HID
        return jnp.concatenate(
            [dot(w[l, lax.rem(i * nq + q, VARIANTS)], x[:, q * HID : (q + 1) * HID]) for q in range(nq)], axis=1
        )

    def exact(w, h):
        hb = h.astype(BF)
        r = dot(w[...], hb)
        half = r.shape[0] // 2
        lo = dot(w[0:half, :], (h - hb.astype(F32)).astype(BF))
        return hb, r[:half] + (r[half:] + lo)

    def head_out(o):
        o = o + col[0:16, 5:6]
        mean = o[0:8]
        t = jnp.tanh(o[8:16])
        ls = -5.0 + 3.5 * (t + 1.0)
        return mean, t, ls

    def sample(mean, ls, e, live):
        sg = jnp.exp(ls)
        u = mean + sg * e
        a = jnp.tanh(u)
        au = jnp.abs(u)
        sq = 2.0 * (math.log(2.0) - au - jnp.log(1.0 + jnp.exp(-2.0 * au)))
        lp = -0.5 * e * e - ls - 0.5 * math.log(2.0 * math.pi) - sq
        return a, sg, jnp.sum(jnp.where(live, lp, 0.0), axis=0, keepdims=True)

    def q_of(k, h2, b):
        r = dot(qw[k], h2)
        return r[0:1] + r[8:9] + b

    def softmin(q, w):
        a, b = -4.0 * q, -4.0 * w
        return -0.25 * (jnp.maximum(a, b) + jnp.log(1.0 + jnp.exp(-jnp.abs(a - b))))

    ones = jnp.ones((16, T), BF)

    row8 = lax.broadcasted_iota(jnp.int32, (8, T), 0)
    row16 = lax.broadcasted_iota(jnp.int32, (16, T), 0)
    live = row8 < ACT

    def mask_of(i):
        lane = lax.broadcasted_iota(jnp.int32, (1, cap), 1)
        return jnp.concatenate(
            [jnp.where(lane < got[i * lists + k, 2 * rows : 2 * rows + 1, 0:1], 1.0, 0.0).astype(F32) for k in range(lists)], axis=1
        )

    @pl.loop(0, nt)
    def _(i):
        xt = xrow[...].T
        gather(jnp.minimum(i + 1, nt - 1))
        seeds = jnp.concatenate([got[i * lists + k, rows + r : rows + r + 1, 0:part] for k in range(lists) for r in range(rows)], axis=1)
        mask = mask_of(i)
        alpha = jnp.exp(jnp.full((1, T), level, F32))
        b1 = pltpu.roll(xt[16:24], 7, 0)
        reward = b1[6:7]
        xa = jnp.concatenate([jnp.where(row8 == 6, 1.0, b1), xt[0:16]], axis=0)
        b2_ = pltpu.roll(xt[40:48], 7, 0)
        done = b2_[0:1]
        n_lo = jnp.where(row8 == 7, b2_, jnp.where(row8 == 6, 1.0, 0.0))
        xn = jnp.concatenate([n_lo, xt[24:40]], axis=0)
        eps = noise(seeds, row16)
        xkeep[i] = xa
        ekeep[i] = eps[0:8]

        un = first(0, 1, xn)
        hi, lo = split(xa)
        xw = jnp.concatenate([hi, lo], axis=0).astype(BF)
        ua = dot(w1all[HID : 3 * HID, :], jnp.concatenate([hi, lo, hi], axis=0).astype(BF))
        hn, _ = act(un)
        h1c, d1c = zip(*[act(ua[k * HID : (1 + k) * HID]) for k in range(2)])
        hn, _ = layer2(i, 0, hn)
        r = dot(head[...], hn)
        mean, _, ls = head_out(r[0:16] + r[16:32])
        a2, _, lp2 = sample(mean, ls, eps[8:16], live)
        un = first(3, 5, jnp.concatenate([jnp.where(live, a2, n_lo), xt[24:40]], axis=0))
        h2c, d2c = zip(*[layer2(i, 1 + k, h1c[k]) for k in range(2)])
        qc = [q_of(k, h2c[k], jb3_s[k]) for k in range(2)]
        ht = [act(un[k * HID : (k + 1) * HID])[0] for k in range(2)]
        ht = [layer2(i, 3 + k, ht[k])[0] for k in range(2)]
        qt = [q_of(2 + k, ht[k], lb3_s[k]) for k in range(2)]
        y = reward + GAMMA * (1.0 - done) * (softmin(qt[0], qt[1]) - alpha * lp2)
        closs = jnp.zeros((1, T), F32)
        for k in range(2):
            dq = qc[k] - y
            mdq = dq * mask
            closs = closs + 0.5 * (mdq * dq)
            g2 = (mdq * d2c[k]).astype(BF)
            mhi, mlo = split(mdq)
            m16 = jnp.where(row16 == 0, mhi, jnp.where(row16 == 1, mlo, 0.0)).astype(BF)
            gcw3[k] += dot_t(m16, h2c[k])
            r = dot_t(jnp.concatenate([h1c[k], ones], axis=0), g2)
            gw2[1 + k] += r[0:HID]
            gw2b[1 + k] += r[HID : HID + 8]
            g1 = (by_chunk(b2, 1 + k, i, g2) * d1c[k]).astype(BF)
            w = dot_t(xw, g1)
            gcw1[k] += w[0:24] + w[24:48]
            gmisc[k : k + 1, :] += fold(mdq)
        gmisc[2:3, :] += fold(closs)

    mine = critic_sum.mine
    mine[...] = jnp.zeros_like(mine)
    row8h = lax.broadcasted_iota(jnp.int32, (8, HID), 0)
    cols = jnp.zeros((8, HID), F32)
    for k in range(2):
        s = scale[k : k + 1, :]
        cols = jnp.where(row8h == k, gw2b[1 + k] * s, cols)
        cols = jnp.where(row8h == 2 + k, gcw3[k, 0:1, :] + gcw3[k, 1:2, :], cols)
        for h in range(2):
            at = slice(h * 128, (h + 1) * 128)
            put(mine, (2 * k + h) * HID, gw2[1 + k, :, at] * s[:, at])
            put(mine, R_CW1 + 48 * k + 24 * h, gcw1[k, :, at])
    for h in range(2):
        put(mine, R_CCOL + 8 * h, cols[:, h * 128 : (h + 1) * 128])
    pl.semaphore_wait(barrier, len(partners))
    critic_sum.step(0, 0)
    last = critic_sum.steps()
    when = (0, 1, 3, 4, 5, 7, 8) if (last, nt) == (6, 8) else tuple(j * nt // last for j in range(last + 1))

    @pl.loop(0, nt)
    def _(i):
        for j in range(1, last + 1):
            if when[j] < nt:
                pl.when(i == when[j])(functools.partial(critic_sum.step, j, 0))
        mask = mask_of(i)
        alpha = jnp.exp(jnp.full((1, T), level, F32))
        xa = xkeep[i]
        e = ekeep[i]
        hi, lo = split(xa)
        xw = jnp.concatenate([hi, lo], axis=0).astype(BF)
        h1a, d1a = act32(dot(w1all[0:HID, :], jnp.concatenate([hi, lo, hi], axis=0).astype(BF)))
        h1a, r = exact(fa, h1a)
        h2a, d2a = act32(r + col[:, 0:1])
        h2a, r = exact(head, h2a)
        mean, t, ls = head_out(r)
        a1, sg, lp = sample(mean, ls, e, live)
        uq = first(1, 3, jnp.concatenate([jnp.where(live, a1, xa[0:8]), xa[8:24]], axis=0))
        h1q, d1q = zip(*[act(uq[k * HID : (k + 1) * HID]) for k in range(2)])
        h2q, d2q = zip(*[layer2(i, 1 + k, h1q[k]) for k in range(2)])
        qq = [q_of(k, h2q[k], jb3_s[k]) for k in range(2)]
        sm = softmin(qq[0], qq[1])
        p0 = 1.0 / (1.0 + jnp.exp(4.0 * (qq[0] - qq[1])))
        da = jnp.zeros((8, T), F32)
        for k, pk in enumerate((p0, 1.0 - p0)):
            g1 = (by_chunk(b2, 1 + k, i, d2q[k].astype(BF)) * d1q[k]).astype(BF)
            w = dot(da_w[k], g1)
            da = da - (pk * mask) * (w[0:8] + w[8:16])
        ma = mask * alpha
        du = da * (1.0 - a1 * a1) + ma * (2.0 * a1)
        dls = (du * sg * e - ma) * (3.5 * (1.0 - t * t))
        do = jnp.concatenate([jnp.where(live, du, 0.0), jnp.where(live, dls, 0.0)], axis=0)
        gcol[...] += fold(do)
        dob = do.astype(BF)
        gaw3[...] += dot_t(dob, h2a)
        g2 = (dot(headb[...], jnp.concatenate([dob, dob], axis=0)) * d2a).astype(BF)
        r = dot_t(jnp.concatenate([h1a, ones], axis=0), g2)
        gw2[0] += r[0:HID]
        gw2b[0] += r[HID : HID + 8]
        g1 = (by_chunk(b2, 0, i, g2) * d1a).astype(BF)
        w = dot_t(xw, g1)
        gaw1[...] += w[0:24] + w[24:48]
        gmisc[3:4, :] += fold(mask * (alpha * lp - sm))
        gmisc[4:5, :] += fold(mask * (lp - 6.0))
        gmisc[5:6, :] += fold(mask)

    mine = actor_sum.mine
    mine[...] = jnp.zeros_like(mine)
    for h in range(2):
        at = slice(h * 128, (h + 1) * 128)
        put(mine, h * HID, gw2[0, :, at])
        put(mine, R_AW1 + 24 * h, gaw1[:, at])
        put(mine, R_AW3 + 16 * h, gaw3[:, at])
        put(mine, R_ACOL + 8 * h, gw2b[0, :, at])
    put(mine, R_AB3, gcol[...])
    put(mine, R_MISC, gmisc[...])
    for c in range(len(actor_sum.parts)):
        actor_sum.step(0, c)
    for j in range(1, last + 1):
        if when[j] >= nt:
            critic_sum.step(j, 0)
    for j in range(1, last + 1):
        for c in range(len(actor_sum.parts)):
            actor_sum.step(j, c)
    critic_sum.all_sent()
    actor_sum.all_sent()


def summed_grads(ready, n, cap):
    tab, got, idx_s, *weights, scal = ready
    slots = n * cap
    T = min(TILE, slots)
    rows_c, rows_a = piece_rows(R_CEND, n), piece_rows(R_AEND, n)
    vm = pl.BlockSpec(memory_space=pltpu.VMEM)
    sm = pl.BlockSpec(memory_space=pltpu.SMEM)
    return pl.pallas_call(
        functools.partial(net_kernel, n=n, cap=cap, slots=slots),
        out_shape=[pltpu.VMEM((n, rows_c, 128), F32), pltpu.VMEM((n, rows_a, 128), F32)],
        in_specs=[sm] * 2 + [vm] * (2 + len(weights)),
        out_specs=[vm, vm],
        scratch_shapes=[
            pltpu.VMEM((T, 128), F32),
            pltpu.VMEM((slots // T, 24, T), F32),
            pltpu.VMEM((slots // T, 8, T), F32),
            pltpu.VMEM((3, HID, HID), F32),
            pltpu.VMEM((3, 8, HID), F32),
            pltpu.VMEM((24, HID), F32),
            pltpu.VMEM((2, 24, HID), F32),
            pltpu.VMEM((16, HID), F32),
            pltpu.VMEM((2, 16, HID), F32),
            pltpu.VMEM((16, 128), F32),
            pltpu.VMEM((8, 128), F32),
        ]
        + sum_scratch(n, rows_c, 1)
        + sum_scratch(n, rows_a, CHUNKS),
        compiler_params=pltpu.CompilerParams(collective_id=1, has_side_effects=True, vmem_limit_bytes=34 << 20),
        name="networks",
    )(idx_s, scal, tab, got, *weights)


def finish_kernel(scal, gc, ga, aw1, ab1, aw2, ab2, aw3, ab3, cw1, cb1, cw2, cb2, cw3, cb3, da, losses):
    misc = jnp.sum(ga[R_MISC : R_MISC + 8, :], axis=1, keepdims=True)
    inv = 1.0 / misc[5:6]

    def rows(g, at, count):
        return jnp.concatenate([g[at : at + count, :], g[at + count : at + 2 * count, :]], axis=1) * inv

    aw2[...] = rows(ga, 0, HID)
    cw2[0] = rows(gc, 0, HID)
    cw2[1] = rows(gc, 2 * HID, HID)
    w = rows(ga, R_AW1, 24)
    aw1[0:16, :] = w[8:24]
    aw1[16:17, :] = w[7:8]
    ab1[...] = w[6:7]
    for k in range(2):
        w = rows(gc, R_CW1 + 48 * k, 24)
        cw1[0:16, k, :] = w[8:24]
        cw1[16:17, k, :] = w[7:8]
        cw1[17:23, k, :] = w[0:6]
        cb1[k : k + 1, :] = w[6:7]
    w = rows(ga, R_AW3, 16)
    aw3[0:6, :] = w[0:6]
    aw3[6:12, :] = w[8:14]
    c = rows(gc, R_CCOL, 8)
    cb2[...] = c[0:2]
    cw3[...] = c[2:4]
    ab2[...] = rows(ga, R_ACOL, 8)[0:1]
    b = jnp.sum(ga[R_AB3 : R_AB3 + 16, :], axis=1, keepdims=True) * inv
    diag = lax.broadcasted_iota(jnp.int32, (16, 128), 0) == lax.broadcasted_iota(jnp.int32, (16, 128), 1)
    b = jnp.sum(jnp.where(diag, b, 0.0), axis=0, keepdims=True)
    ab3[...] = jnp.concatenate([b[:, 0:6], b[:, 8:14]], axis=1)
    m = misc * inv
    cb3[...] = jnp.concatenate([m[0:1], m[1:2]], axis=1)
    da[...] = -m[4:5]
    losses[...] = jnp.concatenate([m[2:3], m[3:4], -scal[4] * m[4:5]], axis=1)


def finish(critics, others, scal):
    vm = pl.BlockSpec(memory_space=pltpu.VMEM)
    shapes = [
        (OBS, HID), (1, HID), (HID, HID), (1, HID), (12, HID), (1, 12),
        (23, 2, HID), (2, HID), (2, HID, HID), (2, HID), (2, HID), (1, 2), (1, 1), (1, 3),
    ]
    outs = list(pl.pallas_call(
        finish_kernel,
        out_shape=[jax.ShapeDtypeStruct(x, F32) for x in shapes],
        in_specs=[pl.BlockSpec(memory_space=pltpu.SMEM), vm, vm],
        out_specs=[vm] * len(shapes),
        compiler_params=pltpu.CompilerParams(vmem_limit_bytes=16 << 20),
        name="finish",
    )(scal, critics.reshape(-1, 128), others.reshape(-1, 128)))
    outs[4] = outs[4].T
    outs[6] = outs[6].transpose(1, 0, 2)
    for k, shape in ((1, (HID,)), (3, (HID,)), (5, (12,)), (11, (2,)), (12, ()), (13, (3,))):
        outs[k] = outs[k].reshape(shape)
    return tuple(outs)


def body(experience_buffer, sampled_indices, filled_lengths, randomizer_numbers, *params):
    n, cap = sampled_indices.shape[1:]
    ready = prepare(experience_buffer, sampled_indices, randomizer_numbers, filled_lengths, params)
    return finish(*summed_grads(ready, n, cap), ready[-1])


def solution(mesh):
    in_specs = (P(None, "dp"), P("dp", None, None), P("dp", None), P("dp", None, None)) + (P(),) * 19
    return jax.shard_map(body, mesh=mesh, in_specs=in_specs, out_specs=(P(),) * 14, check_vma=False)
```

```python
import functools
import math

import jax
import jax.numpy as jnp
from jax import lax
from jax.experimental import pallas as pl
from jax.experimental.pallas import tpu as pltpu
from jax.sharding import PartitionSpec as P

OBS = 17
ACT = 6
HID = 256
GAMMA = 0.99
PRIME = 65521
TILE = 1024
CHUNKS = (2, 1)
VARIANTS = 8
R_AW1 = 6 * HID
R_CW1 = R_AW1 + 48
R_AW3 = R_CW1 + 96
R_COL = R_AW3 + 32
R_AB3 = R_COL + 16
R_MISC = R_AB3 + 16
R_END = R_MISC + 8
R_CUT = 5 * HID
BF = jnp.bfloat16
F32 = jnp.float32


def dot(a, b):
    return jnp.dot(a, b, preferred_element_type=F32)


def dot_t(a, b):
    return lax.dot_general(a, b, (((1,), (1,)), ((), ())), preferred_element_type=F32)


def split(x):
    hi = x.astype(BF).astype(F32)
    return hi, x - hi


def fold_prime(x):
    return (x >> 16) * 15 + (x & 65535)


def below_prime(x):
    return jnp.where(x >= PRIME, x - PRIME, x)


def noise(seeds, rows):
    comp = jnp.where(rows >= 8, rows - 2, rows)
    z = below_prime(fold_prime(seeds))
    h0 = below_prime(fold_prime(z * 257 + comp * 7919 + 1))
    h1 = below_prime(fold_prime(fold_prime(h0 * 32749 + 12345)))
    h2 = below_prime(fold_prime(fold_prime(h1 * 32749 + 54321)))
    u1 = (h1.astype(F32) + 0.5) * (1.0 / PRIME)
    x = jnp.abs((2 * h2 + (1 - PRIME)).astype(F32)) * (math.pi / PRIME) - 0.5 * math.pi
    x2 = x * x
    p = -1.0 / 39916800.0
    for c in (1.0 / 362880.0, -1.0 / 5040.0, 1.0 / 120.0, -1.0 / 6.0, 1.0):
        p = p * x2 + c
    return jnp.sqrt(-2.0 * jnp.log(u1)) * (p * x)


def fold(x):
    return functools.reduce(lambda a, b: a + b, [x[:, k * 128 : (k + 1) * 128] for k in range(x.shape[1] // 128)])


def message_rows(cap):
    return -(-cap // 128)


def prepare_kernel(
    idx_h, seed_h, cnt_h, buf_h, aw2_h, jw2_h, lw2_h,
    aw1_h, ab1_h, ab2_h, aw3_h, jw1_h, jb1_h, jb2_h, jw3_h, lw1_h, lb1_h, lb2_h, lw3_h,
    ab3_h, jb3_h, lb3_h, level,
    tab, got, idx_s, w1all, fa, f2, b2, head, headb, da_w, qw, col, scale, scal,
    idx_v, seed_v, cnt_v, buf, w2, aw1, ab1, ab2, aw3, jw1, jb1, jb2, jw3, lw1, lb1, lb2, lw3,
    ab3, jb3, lb3, msg, land, flat, tmp, rowbuf, in_sems, sems,
    *, n, cap,
):
    me = lax.axis_index("dp")
    rows = message_rows(cap)
    part = min(cap, 128)
    width = buf.shape[1]
    pairs = (
        (idx_h, idx_v), (seed_h, seed_v), (cnt_h, cnt_v), (buf_h, buf),
        (aw2_h, w2.at[0]), (jw2_h, w2.at[pl.ds(1, 2)]), (lw2_h, w2.at[pl.ds(3, 2)]),
        (aw1_h, aw1), (ab1_h, ab1), (ab2_h, ab2), (aw3_h, aw3), (jw1_h, jw1), (jb1_h, jb1), (jb2_h, jb2),
        (jw3_h, jw3), (lw1_h, lw1), (lb1_h, lb1), (lb2_h, lb2), (lw3_h, lw3),
        (ab3_h, ab3), (jb3_h, jb3), (lb3_h, lb3),
    )
    loads = [pltpu.make_async_copy(src, dst, in_sems.at[k]) for k, (src, dst) in enumerate(pairs)]
    for c in loads:
        c.start()
    barrier = pltpu.get_barrier_semaphore()

    @pl.loop(1, n)
    def _(k):
        pl.semaphore_signal(barrier, inc=1, device_id=(lax.rem(me + k, n),), device_id_type=pl.DeviceIdType.MESH)

    for c in loads[:3]:
        c.wait()
    msg[...] = jnp.zeros_like(msg)
    for r in range(rows):
        msg[:, r, 0:part] = idx_v[0, :, r * part : (r + 1) * part]
        msg[:, rows + r, 0:part] = seed_v[0, :, r * part : (r + 1) * part]
    diag = lax.broadcasted_iota(jnp.int32, (n, n), 0) == lax.broadcasted_iota(jnp.int32, (n, n), 1)
    counts = jnp.sum(jnp.where(diag, cnt_v[...].astype(F32), 0.0), axis=1, keepdims=True)
    msg[:, 2 * rows, :] = jnp.broadcast_to(counts, (n, 128)).astype(jnp.int32)
    for c in loads[4:]:
        c.wait()
    for l, (w1, b1, k) in enumerate(((aw1, ab1, None), (jw1, jb1, 0), (jw1, jb1, 1), (lw1, lb1, 0), (lw1, lb1, 1))):
        if k is None:
            tmp[0:6, :] = jnp.zeros((6, HID), F32)
            tmp[6:7, :] = b1[...]
            tmp[7:8, :] = w1[16:17, :]
            tmp[8:24, :] = w1[0:16, :]
        else:
            tmp[0:6, :] = w1[17:23, k, :]
            tmp[6:7, :] = b1[k : k + 1, :]
            tmp[7:8, :] = w1[16:17, k, :]
            tmp[8:24, :] = w1[0:16, k, :]
        hi, lo = split(0.5 * tmp[0:24, :])
        w1all[l * HID : (l + 1) * HID, :] = jnp.concatenate([hi, hi, lo], axis=0).T.astype(BF)
        if l in (1, 2):
            hi, lo = split(tmp[0:8, :])
            da_w[l - 1] = jnp.concatenate([hi, lo], axis=0).astype(BF)
    start = ((2 * me + 1).astype(F32) / n - 1.0) * 2.0**-8

    def roundings(ref, l, w):
        left = w.astype(BF).astype(F32) * start
        for v in range(VARIANTS):
            want = w + left
            got_ = want.astype(BF)
            ref[l, v] = got_
            left = want - got_.astype(F32)

    for l in range(5):
        w = 0.5 * w2[l]
        wt = w.T
        roundings(f2, l, wt)
        if l == 0:
            hi, lo = split(wt)
            fa[0:HID, :] = hi.astype(BF)
            fa[HID:, :] = lo.astype(BF)
        if l == 0:
            roundings(b2, l, w)
        elif l < 3:
            roundings(b2, l, w * (0.5 * jw3[l - 1 : l, :]))
    tmp[0:12, :] = aw3[...]
    r8 = lax.broadcasted_iota(jnp.int32, (8, HID), 0)
    w_head = jnp.concatenate([jnp.where(r8 < 6, tmp[0:8, :], 0.0), jnp.where(r8 < 6, tmp[6:14, :], 0.0)], axis=0)
    hi, lo = split(w_head)
    head[...] = jnp.concatenate([hi, lo], axis=0).astype(BF)
    headb[...] = (0.5 * jnp.concatenate([hi, lo], axis=0)).T.astype(BF)
    for k in range(4):
        w3 = jw3[k : k + 1, :] if k < 2 else lw3[k - 2 : k - 1, :]
        hi, lo = split(w3)
        qw[k] = jnp.concatenate([jnp.where(r8 == 0, hi, 0.0), jnp.where(r8 == 0, lo, 0.0)], axis=0).astype(BF)
    rowbuf[...] = jnp.zeros_like(rowbuf)
    rowbuf[0:1, :] = 0.5 * ab2[...]
    rowbuf[1:3, :] = 0.5 * jb2[...]
    rowbuf[3:5, :] = 0.5 * lb2[...]
    lane12 = lax.broadcasted_iota(jnp.int32, (1, HID), 1)
    hb = jnp.zeros((1, HID), F32)
    for k in range(12):
        hb = jnp.where(lane12 == (k if k < 6 else k + 2), ab3[k], hb)
    rowbuf[5:6, :] = hb
    col[...] = rowbuf[...].T
    scale[...] = jnp.zeros_like(scale)
    scale[0:2, :] = 0.5 * jw3[...]
    for k in range(2):
        scal[k] = jb3[k]
        scal[2 + k] = lb3[k]
    scal[4] = level[0]

    pl.semaphore_wait(barrier, n - 1)

    def copy(k):
        return pltpu.make_async_remote_copy(
            src_ref=msg.at[lax.rem(me + k, n)], dst_ref=land.at[k], send_sem=sems.at[0, k], recv_sem=sems.at[1, k],
            device_id=(lax.rem(me + k, n),), device_id_type=pl.DeviceIdType.MESH,
        )

    @pl.loop(1, n)
    def _(k):
        copy(k).start()

    loads[3].wait()

    @pl.loop(0, width // 128, unroll=4)
    def _(c):
        blk = buf[:, pl.ds(pl.multiple_of(c * 128, 128), 128)]
        tab[pl.ds(pl.multiple_of(c * 128, 128), 128), 0:42] = blk.T

    land[0] = msg[me]

    @pl.loop(1, n)
    def _(k):
        copy(k).wait()

    @pl.loop(0, n)
    def _(k):
        got[lax.rem(me - k + n, n)] = land[k]

    for r in range(rows):
        flat[:, r, :] = got[:, r, :]
    c = pltpu.make_async_copy(flat, idx_s, in_sems.at[0])
    c.start()
    c.wait()


def prepare(experience_buffer, sampled, seeds, counts, params):
    (aw1, ab1, aw2, ab2, aw3, ab3, jw1, jb1, jw2, jb2, jw3, jb3, lw1, lb1, lw2, lb2, lw3, lb3, level) = params
    feats, width = experience_buffer.shape
    _, n, cap = sampled.shape
    rows = message_rows(cap)
    vm = pl.BlockSpec(memory_space=pltpu.VMEM)
    sm = pl.BlockSpec(memory_space=pltpu.SMEM)
    hbm = pl.BlockSpec(memory_space=pl.ANY)
    out = [
        pltpu.VMEM((width, 128), F32),
        pltpu.VMEM((n, 8, 128), jnp.int32),
        pltpu.SMEM((n, rows, 128), jnp.int32),
        pltpu.VMEM((5 * HID, 72), BF),
        pltpu.VMEM((2 * HID, HID), BF),
        pltpu.VMEM((5, VARIANTS, HID, HID), BF),
        pltpu.VMEM((3, VARIANTS, HID, HID), BF),
        pltpu.VMEM((32, HID), BF),
        pltpu.VMEM((HID, 32), BF),
        pltpu.VMEM((2, 16, HID), BF),
        pltpu.VMEM((4, 16, HID), BF),
        pltpu.VMEM((HID, 8), F32),
        pltpu.VMEM((8, HID), F32),
        pltpu.SMEM((8,), F32),
    ]
    return pl.pallas_call(
        functools.partial(prepare_kernel, n=n, cap=cap),
        out_shape=out,
        in_specs=[hbm] * 22 + [sm],
        out_specs=[vm, vm, sm] + [vm] * 10 + [sm],
        scratch_shapes=[
            pltpu.VMEM((1, n, cap), jnp.int32),
            pltpu.VMEM((1, n, cap), jnp.int32),
            pltpu.VMEM((1, n), jnp.int32),
            pltpu.VMEM((feats, width), F32),
            pltpu.VMEM((5, HID, HID), F32),
            pltpu.VMEM((OBS, HID), F32),
            pltpu.VMEM((1, HID), F32),
            pltpu.VMEM((1, HID), F32),
            pltpu.VMEM((12, HID), F32),
            pltpu.VMEM((23, 2, HID), F32),
            pltpu.VMEM((2, HID), F32),
            pltpu.VMEM((2, HID), F32),
            pltpu.VMEM((2, HID), F32),
            pltpu.VMEM((23, 2, HID), F32),
            pltpu.VMEM((2, HID), F32),
            pltpu.VMEM((2, HID), F32),
            pltpu.VMEM((2, HID), F32),
            pltpu.SMEM((12,), F32),
            pltpu.SMEM((2,), F32),
            pltpu.SMEM((2,), F32),
            pltpu.VMEM((n, 8, 128), jnp.int32),
            pltpu.VMEM((n, 8, 128), jnp.int32),
            pltpu.VMEM((n, rows, 128), jnp.int32),
            pltpu.VMEM((24, HID), F32),
            pltpu.VMEM((8, HID), F32),
            pltpu.SemaphoreType.DMA((22,)),
            pltpu.SemaphoreType.DMA((2, n)),
        ],
        compiler_params=pltpu.CompilerParams(collective_id=2, has_side_effects=True, vmem_limit_bytes=24 << 20),
        name="exchange_and_prepare",
    )(
        *[
            pltpu.with_memory_space_constraint(x, pltpu.HBM)
            for x in (
                sampled, seeds, counts, experience_buffer, aw2, jw2, lw2,
                aw1, ab1.reshape(1, HID), ab2.reshape(1, HID), aw3.T,
                jw1.transpose(1, 0, 2), jb1, jb2, jw3, lw1.transpose(1, 0, 2), lb1, lb2, lw3,
                ab3, jb3, lb3,
            )
        ],
        level.reshape(1),
    )


def stage_groups(n):
    groups, st = [(2, 1)], 2
    while st < n:
        f = 4 if (n // st) % 4 == 0 else 2
        groups.append((f, st))
        st *= f
    return groups, groups[:1] + groups[:0:-1]


def chunk_rows(rows, chunks):
    units = rows // 8
    k = min(chunks, units)
    cuts = [8 * (units * j // k) for j in range(k + 1)]
    return list(zip(cuts[:-1], cuts[1:]))


def piece_rows(end, n):
    return 8 * (-(-end // (8 * n)))


class DeviceSum:
    def __init__(self, groups, parts, mine, out, got, part, sems):
        self.sizes, self.strides = [f for f, _ in groups], [st for _, st in groups]
        self.parts, self.mine, self.out, self.got, self.part, self.sems = parts, mine, out, got, part, sems
        self.me = lax.axis_index("dp")
        self.digits = [lax.rem(self.me // st, f) for f, st in groups]
        self.spans, self.starts = [mine.shape[0]], [0]
        for s, f in enumerate(self.sizes):
            self.spans.append(self.spans[s] // f)
            self.starts.append(self.starts[s] + self.digits[s] * self.spans[s + 1])

    def member(self, s, k):
        d = lax.rem(self.digits[s] + k, self.sizes[s])
        return d, self.me + (d - self.digits[s]) * self.strides[s]

    def partners(self):
        return [self.member(s, k)[1] for s in range(len(self.sizes)) for k in range(1, self.sizes[s])]

    def copy(self, phase, s, k, c):
        lo, hi = self.parts[c]
        d, to = self.member(s, k)
        if phase == 0:
            src = self.source(s).at[pl.ds(d * self.spans[s + 1], self.spans[s + 1]), lo:hi]
            dst = self.got[s].at[k - 1, :, lo:hi]
        else:
            src = dst = self.out.at[pl.ds(self.starts[s + 1], self.spans[s + 1]), lo:hi]
        return pltpu.make_async_remote_copy(
            src_ref=src, dst_ref=dst, send_sem=self.sems.at[phase, c, s, k, 0], recv_sem=self.sems.at[phase, c, s, k, 1],
            device_id=(to,), device_id_type=pl.DeviceIdType.MESH,
        )

    def source(self, s):
        return self.mine if s == 0 else self.part[s - 1]

    def start(self, phase, s, c):
        for k in range(1, self.sizes[s]):
            self.copy(phase, s, k, c).start()

    def add(self, s, c):
        lo, hi = self.parts[c]
        span = self.spans[s + 1]
        acc = self.source(s)[pl.ds(self.digits[s] * span, span), lo:hi]
        for k in range(1, self.sizes[s]):
            self.copy(0, s, k, c).wait_recv()
            acc = acc + self.got[s][k - 1, :, lo:hi]
        if s == len(self.sizes) - 1:
            self.out[pl.ds(self.starts[s + 1], 1), lo:hi] = acc
        else:
            self.part[s][:, lo:hi] = acc

    def step(self, j, c):
        ns = len(self.sizes)
        if 1 <= j <= ns:
            self.add(j - 1, c)
        if j > ns:
            for k in range(1, self.sizes[2 * ns - j]):
                self.copy(1, 2 * ns - j, k, c).wait_recv()
        if j < ns:
            self.start(0, j, c)
        elif j < 2 * ns:
            self.start(1, 2 * ns - 1 - j, c)

    def steps(self):
        return 2 * len(self.sizes)

    def all_sent(self):
        for phase in range(2):
            for s in range(len(self.sizes)):
                for k in range(1, self.sizes[s]):
                    for c in range(len(self.parts)):
                        self.copy(phase, s, k, c).wait_send()


def sum_scratch(groups, n, rows, chunks):
    got, part, size = [], [], n
    sizes = [f for f, _ in groups]
    for f in sizes:
        size //= f
        got.append(pltpu.VMEM((f - 1, size, rows, 128), F32))
        part.append(pltpu.VMEM((size, rows, 128), F32))
    sems = pltpu.SemaphoreType.DMA((2, len(chunk_rows(rows, chunks)), len(sizes), max(sizes), 2))
    return [pltpu.VMEM((n, rows, 128), F32)] + got + part + [sems]


def put(dst, at, value):
    rows = dst.shape[1]
    r = 0
    while r < value.shape[0]:
        p, o = divmod(at + r, rows)
        k = min(rows - o, value.shape[0] - r)
        dst[p, o : o + k, :] = value[r : r + k]
        r += k


def net_kernel(
    idx_s, scal, tab, got, w1all, fa, f2, b2, head, headb, da_w, qw, col, scale,
    sum_q, sum_p,
    xrow, gw2, gw2b, gaw1, gcw1, gaw3, gcw3, gcol, gmisc, *rest,
    n, cap, slots,
):
    T = min(TILE, slots)
    nt = slots // T
    lists = T // cap
    rows = message_rows(cap)
    part = min(cap, 128)
    per = len(rest) // 2
    ns = (per - 2) // 2
    sums = [
        DeviceSum(groups, chunk_rows(r[0].shape[1], k), r[0], out, r[1 : 1 + ns], r[1 + ns : 1 + 2 * ns], r[1 + 2 * ns])
        for groups, r, out, k in zip(stage_groups(n), (rest[:per], rest[per:]), (sum_q, sum_p), CHUNKS)
    ]
    barrier = pltpu.get_barrier_semaphore()
    partners = sums[0].partners()
    for to in partners:
        pl.semaphore_signal(barrier, inc=1, device_id=(to,), device_id_type=pl.DeviceIdType.MESH)

    def gather(i):
        for t in range(T):
            r = idx_s[i * lists + t // cap, (t % cap) // 128, t % 128]
            xrow[t : t + 1, :] = tab[pl.ds(r, 1), :]

    gather(0)
    for ref in (gw2, gw2b, gaw1, gcw1, gaw3, gcw3, gcol, gmisc):
        ref[...] = jnp.zeros_like(ref)
    level = scal[4]
    jb3_s = (scal[0], scal[1])
    lb3_s = (scal[2], scal[3])

    def act32(u):
        t = jnp.tanh(u)
        p = 1.0 + t
        h = u * p
        return h, p + h * (2.0 - p)

    def act(u):
        h, d = act32(u)
        return h.astype(BF), d

    def layer2(i, l, h):
        return act(by_chunk(f2, l, i, h) + col[:, l : l + 1])

    def first(l0, l1, x24):
        hi, lo = split(x24)
        xs = jnp.concatenate([hi, lo, hi], axis=0).astype(BF)
        return dot(w1all[l0 * HID : l1 * HID, :], xs)

    def by_chunk(w, l, i, x):
        nq = T // HID
        return jnp.concatenate(
            [dot(w[l, lax.rem(i * nq + q, VARIANTS)], x[:, q * HID : (q + 1) * HID]) for q in range(nq)], axis=1
        )

    def exact(w, h):
        hb = h.astype(BF)
        r = dot(w[...], hb)
        half = r.shape[0] // 2
        lo = dot(w[0:half, :], (h - hb.astype(F32)).astype(BF))
        return hb, r[:half] + (r[half:] + lo)

    def head_out(o):
        o = o + col[0:16, 5:6]
        mean = o[0:8]
        t = jnp.tanh(o[8:16])
        ls = -5.0 + 3.5 * (t + 1.0)
        return mean, t, ls

    def sample(mean, ls, e, live):
        sg = jnp.exp(ls)
        u = mean + sg * e
        a = jnp.tanh(u)
        au = jnp.abs(u)
        sq = 2.0 * (math.log(2.0) - au - jnp.log(1.0 + jnp.exp(-2.0 * au)))
        lp = -0.5 * e * e - ls - 0.5 * math.log(2.0 * math.pi) - sq
        return a, sg, jnp.sum(jnp.where(live, lp, 0.0), axis=0, keepdims=True)

    def q_of(k, h2, b):
        r = dot(qw[k], h2)
        return r[0:1] + r[8:9] + b

    def softmin(q, w):
        a, b = -4.0 * q, -4.0 * w
        return -0.25 * (jnp.maximum(a, b) + jnp.log(1.0 + jnp.exp(-jnp.abs(a - b))))

    ones = jnp.ones((16, T), BF)

    @pl.loop(0, nt)
    def _(i):
        xt = xrow[...].T
        gather(jnp.minimum(i + 1, nt - 1))
        row8 = lax.broadcasted_iota(jnp.int32, (8, T), 0)
        row16 = lax.broadcasted_iota(jnp.int32, (16, T), 0)
        live = row8 < ACT
        seeds = jnp.concatenate([got[i * lists + k, rows + r : rows + r + 1, 0:part] for k in range(lists) for r in range(rows)], axis=1)
        lane = lax.broadcasted_iota(jnp.int32, (1, cap), 1)
        mask = jnp.concatenate(
            [jnp.where(lane < got[i * lists + k, 2 * rows : 2 * rows + 1, 0:1], 1.0, 0.0).astype(F32) for k in range(lists)], axis=1
        )
        alpha = jnp.exp(jnp.full((1, T), level, F32))
        b1 = pltpu.roll(xt[16:24], 7, 0)
        reward = b1[6:7]
        xa = jnp.concatenate([jnp.where(row8 == 6, 1.0, b1), xt[0:16]], axis=0)
        b2_ = pltpu.roll(xt[40:48], 7, 0)
        done = b2_[0:1]
        n_lo = jnp.where(row8 == 7, b2_, jnp.where(row8 == 6, 1.0, 0.0))
        xn = jnp.concatenate([n_lo, xt[24:40]], axis=0)

        un = first(0, 1, xn)
        hi, lo = split(xa)
        xw = jnp.concatenate([hi, lo], axis=0).astype(BF)
        ua = dot(w1all[0 : 3 * HID, :], jnp.concatenate([hi, lo, hi], axis=0).astype(BF))
        eps = noise(seeds, row16)
        e = eps[0:8]
        hn, _ = act(un)
        h1a, d1a = act32(ua[0:HID])
        h1c, d1c = zip(*[act(ua[(1 + k) * HID : (2 + k) * HID]) for k in range(2)])
        hn, _ = layer2(i, 0, hn)
        r = dot(head[...], hn)
        mean, _, ls = head_out(r[0:16] + r[16:32])
        a2, _, lp2 = sample(mean, ls, eps[8:16], live)
        h1a, r = exact(fa, h1a)
        h2a, d2a = act32(r + col[:, 0:1])
        h2a, r = exact(head, h2a)
        mean, t, ls = head_out(r)
        a1, sg, lp = sample(mean, ls, e, live)
        un = first(3, 5, jnp.concatenate([jnp.where(live, a2, n_lo), xt[24:40]], axis=0))
        h2c, d2c = zip(*[layer2(i, 1 + k, h1c[k]) for k in range(2)])
        qc = [q_of(k, h2c[k], jb3_s[k]) for k in range(2)]
        uq = first(1, 3, jnp.concatenate([jnp.where(live, a1, xa[0:8]), xt[0:16]], axis=0))
        ht = [act(un[k * HID : (k + 1) * HID])[0] for k in range(2)]
        ht = [layer2(i, 3 + k, ht[k])[0] for k in range(2)]
        qt = [q_of(2 + k, ht[k], lb3_s[k]) for k in range(2)]
        h1q, d1q = zip(*[act(uq[k * HID : (k + 1) * HID]) for k in range(2)])
        y = reward + GAMMA * (1.0 - done) * (softmin(qt[0], qt[1]) - alpha * lp2)
        h2q, d2q = zip(*[layer2(i, 1 + k, h1q[k]) for k in range(2)])
        qq = [q_of(k, h2q[k], jb3_s[k]) for k in range(2)]

        closs = jnp.zeros((1, T), F32)
        g2c = []
        for k in range(2):
            dq = qc[k] - y
            mdq = dq * mask
            closs = closs + 0.5 * (mdq * dq)
            g2 = (mdq * d2c[k]).astype(BF)
            g2c.append(g2)
            mhi, mlo = split(mdq)
            m16 = jnp.where(row16 == 0, mhi, jnp.where(row16 == 1, mlo, 0.0)).astype(BF)
            gcw3[k] += dot_t(m16, h2c[k])
            r = dot_t(jnp.concatenate([h1c[k], ones], axis=0), g2)
            gw2[1 + k] += r[0:HID]
            gw2b[1 + k] += r[HID : HID + 8]
            gmisc[k : k + 1, :] += fold(mdq)
        sm = softmin(qq[0], qq[1])
        p0 = 1.0 / (1.0 + jnp.exp(4.0 * (qq[0] - qq[1])))
        da = jnp.zeros((8, T), F32)
        for k, pk in enumerate((p0, 1.0 - p0)):
            g1 = (by_chunk(b2, 1 + k, i, d2q[k].astype(BF)) * d1q[k]).astype(BF)
            w = dot(da_w[k], g1)
            da = da - (pk * mask) * (w[0:8] + w[8:16])
        for k in range(2):
            g1 = (by_chunk(b2, 1 + k, i, g2c[k]) * d1c[k]).astype(BF)
            w = dot_t(xw, g1)
            gcw1[k] += w[0:24] + w[24:48]
        ma = mask * alpha
        du = da * (1.0 - a1 * a1) + ma * (2.0 * a1)
        dls = (du * sg * e - ma) * (3.5 * (1.0 - t * t))
        do = jnp.concatenate([jnp.where(live, du, 0.0), jnp.where(live, dls, 0.0)], axis=0)
        gcol[...] += fold(do)
        dob = do.astype(BF)
        gaw3[...] += dot_t(dob, h2a)
        g2 = (dot(headb[...], jnp.concatenate([dob, dob], axis=0)) * d2a).astype(BF)
        r = dot_t(jnp.concatenate([h1a, ones], axis=0), g2)
        gw2[0] += r[0:HID]
        gw2b[0] += r[HID : HID + 8]
        g1 = (by_chunk(b2, 0, i, g2) * d1a).astype(BF)
        w = dot_t(xw, g1)
        gaw1[...] += w[0:24] + w[24:48]
        gmisc[2:3, :] += fold(closs)
        gmisc[3:4, :] += fold(mask * (alpha * lp - sm))
        gmisc[4:5, :] += fold(mask * (lp - 6.0))
        gmisc[5:6, :] += fold(mask)

    def pack(at, value):
        k = 0 if at < R_CUT else 1
        put(sums[k].mine, at - k * R_CUT, value)

    row8 = lax.broadcasted_iota(jnp.int32, (8, HID), 0)
    cols = jnp.zeros((8, HID), F32)
    for k in range(2):
        s = scale[k : k + 1, :]
        cols = jnp.where(row8 == k, gw2b[1 + k] * s, cols)
        cols = jnp.where(row8 == 2 + k, gcw3[k, 0:1, :] + gcw3[k, 1:2, :], cols)
    cols = jnp.where(row8 == 4, gw2b[0], cols)
    for t in sums:
        rows = t.mine.shape[1]
        full = R_CUT if t is sums[0] else R_END - R_CUT
        for p in range(full // rows, n):
            t.mine[p] = jnp.zeros((rows, 128), F32)
    for m in range(3):
        for h in range(2):
            at = slice(h * 128, (h + 1) * 128)
            w = gw2[m, :, at]
            if m > 0:
                w = w * scale[m - 1 : m, at]
            pack((2 * m + h) * HID, w)
    for h in range(2):
        at = slice(h * 128, (h + 1) * 128)
        pack(R_AW1 + 24 * h, gaw1[:, at])
        for k in range(2):
            pack(R_CW1 + 48 * k + 24 * h, gcw1[k, :, at])
        pack(R_AW3 + 16 * h, gaw3[:, at])
        pack(R_COL + 8 * h, cols[:, at])
    pack(R_AB3, gcol[...])
    pack(R_MISC, gmisc[...])
    pl.semaphore_wait(barrier, len(partners))
    for j in range(2 * ns + 1):
        for t in sums:
            for c in range(len(t.parts)):
                t.step(j, c)
    for t in sums:
        t.all_sent()


def summed_grads(ready, n, cap):
    tab, got, idx_s, *weights, scal = ready
    slots = n * cap
    T = min(TILE, slots)
    heights = piece_rows(R_CUT, n), piece_rows(R_END - R_CUT, n)
    vm = pl.BlockSpec(memory_space=pltpu.VMEM)
    sm = pl.BlockSpec(memory_space=pltpu.SMEM)
    scratch = [
        pltpu.VMEM((T, 128), F32),
        pltpu.VMEM((3, HID, HID), F32),
        pltpu.VMEM((3, 8, HID), F32),
        pltpu.VMEM((24, HID), F32),
        pltpu.VMEM((2, 24, HID), F32),
        pltpu.VMEM((16, HID), F32),
        pltpu.VMEM((2, 16, HID), F32),
        pltpu.VMEM((16, 128), F32),
        pltpu.VMEM((8, 128), F32),
    ]
    for groups, height, chunks in zip(stage_groups(n), heights, CHUNKS):
        scratch += sum_scratch(groups, n, height, chunks)
    return pl.pallas_call(
        functools.partial(net_kernel, n=n, cap=cap, slots=slots),
        out_shape=[pltpu.VMEM((n, height, 128), F32) for height in heights],
        in_specs=[sm] * 2 + [vm] * (2 + len(weights)),
        out_specs=[vm, vm],
        scratch_shapes=scratch,
        compiler_params=pltpu.CompilerParams(collective_id=1, has_side_effects=True, vmem_limit_bytes=36 << 20),
        name="networks",
    )(idx_s, scal, tab, got, *weights)


def finish_kernel(scal, gq, gp, aw1, ab1, aw2, ab2, aw3, ab3, cw1, cb1, cw2, cb2, cw3, cb3, da, losses):
    def part(at, count):
        return gq[at : at + count, :] if at < R_CUT else gp[at - R_CUT : at - R_CUT + count, :]

    misc = jnp.sum(part(R_MISC, 8), axis=1, keepdims=True)
    inv = 1.0 / misc[5:6]

    def rows(at, count):
        return jnp.concatenate([part(at, count), part(at + count, count)], axis=1) * inv

    aw2[...] = rows(0, HID)
    cw2[0] = rows(2 * HID, HID)
    cw2[1] = rows(4 * HID, HID)
    w = rows(R_AW1, 24)
    aw1[0:16, :] = w[8:24]
    aw1[16:17, :] = w[7:8]
    ab1[...] = w[6:7]
    for k in range(2):
        w = rows(R_CW1 + 48 * k, 24)
        cw1[0:16, k, :] = w[8:24]
        cw1[16:17, k, :] = w[7:8]
        cw1[17:23, k, :] = w[0:6]
        cb1[k : k + 1, :] = w[6:7]
    w = rows(R_AW3, 16)
    aw3[0:6, :] = w[0:6]
    aw3[6:12, :] = w[8:14]
    c = rows(R_COL, 8)
    cb2[...] = c[0:2]
    cw3[...] = c[2:4]
    ab2[...] = c[4:5]
    b = jnp.sum(part(R_AB3, 16), axis=1, keepdims=True) * inv
    diag = lax.broadcasted_iota(jnp.int32, (16, 128), 0) == lax.broadcasted_iota(jnp.int32, (16, 128), 1)
    b = jnp.sum(jnp.where(diag, b, 0.0), axis=0, keepdims=True)
    ab3[...] = jnp.concatenate([b[:, 0:6], b[:, 8:14]], axis=1)
    m = misc * inv
    cb3[...] = jnp.concatenate([m[0:1], m[1:2]], axis=1)
    da[...] = -m[4:5]
    losses[...] = jnp.concatenate([m[2:3], m[3:4], -scal[4] * m[4:5]], axis=1)


def finish(first, second, scal):
    vm = pl.BlockSpec(memory_space=pltpu.VMEM)
    shapes = [
        (OBS, HID), (1, HID), (HID, HID), (1, HID), (12, HID), (1, 12),
        (23, 2, HID), (2, HID), (2, HID, HID), (2, HID), (2, HID), (1, 2), (1, 1), (1, 3),
    ]
    outs = list(pl.pallas_call(
        finish_kernel,
        out_shape=[jax.ShapeDtypeStruct(x, F32) for x in shapes],
        in_specs=[pl.BlockSpec(memory_space=pltpu.SMEM), vm, vm],
        out_specs=[vm] * len(shapes),
        compiler_params=pltpu.CompilerParams(vmem_limit_bytes=16 << 20),
        name="finish",
    )(scal, first.reshape(-1, 128), second.reshape(-1, 128)))
    outs[4] = outs[4].T
    outs[6] = outs[6].transpose(1, 0, 2)
    for k, shape in ((1, (HID,)), (3, (HID,)), (5, (12,)), (11, (2,)), (12, ()), (13, (3,))):
        outs[k] = outs[k].reshape(shape)
    return tuple(outs)


def body(experience_buffer, sampled_indices, filled_lengths, randomizer_numbers, *params):
    n, cap = sampled_indices.shape[1:]
    ready = prepare(experience_buffer, sampled_indices, randomizer_numbers, filled_lengths, params)
    return finish(*summed_grads(ready, n, cap), ready[-1])


def solution(mesh):
    in_specs = (P(None, "dp"), P("dp", None, None), P("dp", None), P("dp", None, None)) + (P(),) * 19
    return jax.shard_map(body, mesh=mesh, in_specs=in_specs, out_specs=(P(),) * 14, check_vma=False)
```

```python
import functools
import math

import jax
import jax.numpy as jnp
from jax import lax
from jax.experimental import pallas as pl
from jax.experimental.pallas import tpu as pltpu
from jax.sharding import PartitionSpec as P

OBS = 17
ACT = 6
HID = 256
GAMMA = 0.99
PRIME = 65521
TILE = 1024
CHUNKS = (2, 1)
VARIANTS = 4
R_AW1 = 6 * HID
R_CW1 = R_AW1 + 48
R_AW3 = R_CW1 + 96
R_COL = R_AW3 + 32
R_AB3 = R_COL + 16
R_MISC = R_AB3 + 16
R_END = R_MISC + 8
R_CUT = 5 * HID
BF = jnp.bfloat16
F32 = jnp.float32


def dot(a, b):
    return jnp.dot(a, b, preferred_element_type=F32)


def dot_t(a, b):
    return lax.dot_general(a, b, (((1,), (1,)), ((), ())), preferred_element_type=F32)


def split(x):
    hi = x.astype(BF).astype(F32)
    return hi, x - hi


def fold_prime(x):
    return (x >> 16) * 15 + (x & 65535)


def below_prime(x):
    return jnp.where(x >= PRIME, x - PRIME, x)


def noise(seeds, rows):
    comp = jnp.where(rows >= 8, rows - 2, rows)
    z = below_prime(fold_prime(seeds))
    h0 = below_prime(fold_prime(z * 257 + comp * 7919 + 1))
    h1 = below_prime(fold_prime(fold_prime(h0 * 32749 + 12345)))
    h2 = below_prime(fold_prime(fold_prime(h1 * 32749 + 54321)))
    u1 = (h1.astype(F32) + 0.5) * (1.0 / PRIME)
    x = jnp.abs((2 * h2 + (1 - PRIME)).astype(F32)) * (math.pi / PRIME) - 0.5 * math.pi
    x2 = x * x
    p = -1.0 / 39916800.0
    for c in (1.0 / 362880.0, -1.0 / 5040.0, 1.0 / 120.0, -1.0 / 6.0, 1.0):
        p = p * x2 + c
    return jnp.sqrt(-2.0 * jnp.log(u1)) * (p * x)


def fold(x):
    return functools.reduce(lambda a, b: a + b, [x[:, k * 128 : (k + 1) * 128] for k in range(x.shape[1] // 128)])


def message_rows(cap):
    return -(-cap // 128)


def prepare_kernel(
    idx_h, seed_h, cnt_h, buf_h, aw2_h, jw2_h, lw2_h,
    aw1_h, ab1_h, ab2_h, aw3_h, jw1_h, jb1_h, jb2_h, jw3_h, lw1_h, lb1_h, lb2_h, lw3_h,
    ab3_h, jb3_h, lb3_h, level,
    tab, got, idx_s, w1all, fa, f2, b2, head, headb, da_w, qw, col, scale, scal,
    idx_v, seed_v, cnt_v, buf, w2, aw1, ab1, ab2, aw3, jw1, jb1, jb2, jw3, lw1, lb1, lb2, lw3,
    ab3, jb3, lb3, msg, land, flat, tmp, rowbuf, in_sems, sems,
    *, n, cap,
):
    me = lax.axis_index("dp")
    rows = message_rows(cap)
    part = min(cap, 128)
    width = buf.shape[1]
    pairs = (
        (idx_h, idx_v), (seed_h, seed_v), (cnt_h, cnt_v), (buf_h, buf),
        (aw2_h, w2.at[0]), (jw2_h, w2.at[pl.ds(1, 2)]), (lw2_h, w2.at[pl.ds(3, 2)]),
        (aw1_h, aw1), (ab1_h, ab1), (ab2_h, ab2), (aw3_h, aw3), (jw1_h, jw1), (jb1_h, jb1), (jb2_h, jb2),
        (jw3_h, jw3), (lw1_h, lw1), (lb1_h, lb1), (lb2_h, lb2), (lw3_h, lw3),
        (ab3_h, ab3), (jb3_h, jb3), (lb3_h, lb3),
    )
    loads = [pltpu.make_async_copy(src, dst, in_sems.at[k]) for k, (src, dst) in enumerate(pairs)]
    for c in loads:
        c.start()
    barrier = pltpu.get_barrier_semaphore()

    @pl.loop(1, n)
    def _(k):
        pl.semaphore_signal(barrier, inc=1, device_id=(lax.rem(me + k, n),), device_id_type=pl.DeviceIdType.MESH)

    for c in loads[:3]:
        c.wait()
    msg[...] = jnp.zeros_like(msg)
    for r in range(rows):
        msg[:, r, 0:part] = idx_v[0, :, r * part : (r + 1) * part]
        msg[:, rows + r, 0:part] = seed_v[0, :, r * part : (r + 1) * part]
    diag = lax.broadcasted_iota(jnp.int32, (n, n), 0) == lax.broadcasted_iota(jnp.int32, (n, n), 1)
    counts = jnp.sum(jnp.where(diag, cnt_v[...].astype(F32), 0.0), axis=1, keepdims=True)
    msg[:, 2 * rows, :] = jnp.broadcast_to(counts, (n, 128)).astype(jnp.int32)
    for c in loads[4:]:
        c.wait()
    for l, (w1, b1, k) in enumerate(((aw1, ab1, None), (jw1, jb1, 0), (jw1, jb1, 1), (lw1, lb1, 0), (lw1, lb1, 1))):
        if k is None:
            tmp[0:6, :] = jnp.zeros((6, HID), F32)
            tmp[6:7, :] = b1[...]
            tmp[7:8, :] = w1[16:17, :]
            tmp[8:24, :] = w1[0:16, :]
        else:
            tmp[0:6, :] = w1[17:23, k, :]
            tmp[6:7, :] = b1[k : k + 1, :]
            tmp[7:8, :] = w1[16:17, k, :]
            tmp[8:24, :] = w1[0:16, k, :]
        hi, lo = split(0.5 * tmp[0:24, :])
        w1all[l * HID : (l + 1) * HID, :] = jnp.concatenate([hi, hi, lo], axis=0).T.astype(BF)
        if l in (1, 2):
            hi, lo = split(tmp[0:8, :])
            da_w[l - 1] = jnp.concatenate([hi, lo], axis=0).astype(BF)
    start = ((2 * me + 1).astype(F32) / n - 1.0) * 2.0**-8

    def roundings(ref, l, w):
        left = w.astype(BF).astype(F32) * start
        for v in range(VARIANTS):
            want = w + left
            got_ = want.astype(BF)
            ref[l, v] = got_
            left = want - got_.astype(F32)

    for l in range(5):
        w = 0.5 * w2[l]
        wt = w.T
        roundings(f2, l, wt)
        if l == 0:
            hi, lo = split(wt)
            fa[0:HID, :] = hi.astype(BF)
            fa[HID:, :] = lo.astype(BF)
        if l == 0:
            roundings(b2, l, w)
        elif l < 3:
            roundings(b2, l, w * (0.5 * jw3[l - 1 : l, :]))
    tmp[0:12, :] = aw3[...]
    r8 = lax.broadcasted_iota(jnp.int32, (8, HID), 0)
    w_head = jnp.concatenate([jnp.where(r8 < 6, tmp[0:8, :], 0.0), jnp.where(r8 < 6, tmp[6:14, :], 0.0)], axis=0)
    hi, lo = split(w_head)
    head[...] = jnp.concatenate([hi, lo], axis=0).astype(BF)
    headb[...] = (0.5 * jnp.concatenate([hi, lo], axis=0)).T.astype(BF)
    for k in range(4):
        w3 = jw3[k : k + 1, :] if k < 2 else lw3[k - 2 : k - 1, :]
        hi, lo = split(w3)
        qw[k] = jnp.concatenate([jnp.where(r8 == 0, hi, 0.0), jnp.where(r8 == 0, lo, 0.0)], axis=0).astype(BF)
    rowbuf[...] = jnp.zeros_like(rowbuf)
    rowbuf[0:1, :] = 0.5 * ab2[...]
    rowbuf[1:3, :] = 0.5 * jb2[...]
    rowbuf[3:5, :] = 0.5 * lb2[...]
    lane12 = lax.broadcasted_iota(jnp.int32, (1, HID), 1)
    hb = jnp.zeros((1, HID), F32)
    for k in range(12):
        hb = jnp.where(lane12 == (k if k < 6 else k + 2), ab3[k], hb)
    rowbuf[5:6, :] = hb
    col[...] = rowbuf[...].T
    scale[...] = jnp.zeros_like(scale)
    scale[0:2, :] = 0.5 * jw3[...]
    scale[7:8, :] = jnp.ones((1, HID), F32)
    for k in range(2):
        scal[k] = jb3[k]
        scal[2 + k] = lb3[k]
    scal[4] = level[0]

    pl.semaphore_wait(barrier, n - 1)

    def copy(k):
        return pltpu.make_async_remote_copy(
            src_ref=msg.at[lax.rem(me + k, n)], dst_ref=land.at[k], send_sem=sems.at[0, k], recv_sem=sems.at[1, k],
            device_id=(lax.rem(me + k, n),), device_id_type=pl.DeviceIdType.MESH,
        )

    @pl.loop(1, n)
    def _(k):
        copy(k).start()

    loads[3].wait()

    @pl.loop(0, width // 128, unroll=4)
    def _(c):
        blk = buf[:, pl.ds(pl.multiple_of(c * 128, 128), 128)]
        tab[pl.ds(pl.multiple_of(c * 128, 128), 128), 0:42] = blk.T

    land[0] = msg[me]

    @pl.loop(1, n)
    def _(k):
        copy(k).wait()

    @pl.loop(0, n)
    def _(k):
        got[lax.rem(me - k + n, n)] = land[k]

    for r in range(rows):
        flat[:, r, :] = got[:, r, :]
    c = pltpu.make_async_copy(flat, idx_s, in_sems.at[0])
    c.start()
    c.wait()


def prepare(experience_buffer, sampled, seeds, counts, params):
    (aw1, ab1, aw2, ab2, aw3, ab3, jw1, jb1, jw2, jb2, jw3, jb3, lw1, lb1, lw2, lb2, lw3, lb3, level) = params
    feats, width = experience_buffer.shape
    _, n, cap = sampled.shape
    rows = message_rows(cap)
    vm = pl.BlockSpec(memory_space=pltpu.VMEM)
    sm = pl.BlockSpec(memory_space=pltpu.SMEM)
    hbm = pl.BlockSpec(memory_space=pl.ANY)
    out = [
        pltpu.VMEM((width, 128), F32),
        pltpu.VMEM((n, 8, 128), jnp.int32),
        pltpu.SMEM((n, rows, 128), jnp.int32),
        pltpu.VMEM((5 * HID, 72), BF),
        pltpu.VMEM((2 * HID, HID), BF),
        pltpu.VMEM((5, VARIANTS, HID, HID), BF),
        pltpu.VMEM((3, VARIANTS, HID, HID), BF),
        pltpu.VMEM((32, HID), BF),
        pltpu.VMEM((HID, 32), BF),
        pltpu.VMEM((2, 16, HID), BF),
        pltpu.VMEM((4, 16, HID), BF),
        pltpu.VMEM((HID, 8), F32),
        pltpu.VMEM((8, HID), F32),
        pltpu.SMEM((8,), F32),
    ]
    return pl.pallas_call(
        functools.partial(prepare_kernel, n=n, cap=cap),
        out_shape=out,
        in_specs=[hbm] * 22 + [sm],
        out_specs=[vm, vm, sm] + [vm] * 10 + [sm],
        scratch_shapes=[
            pltpu.VMEM((1, n, cap), jnp.int32),
            pltpu.VMEM((1, n, cap), jnp.int32),
            pltpu.VMEM((1, n), jnp.int32),
            pltpu.VMEM((feats, width), F32),
            pltpu.VMEM((5, HID, HID), F32),
            pltpu.VMEM((OBS, HID), F32),
            pltpu.VMEM((1, HID), F32),
            pltpu.VMEM((1, HID), F32),
            pltpu.VMEM((12, HID), F32),
            pltpu.VMEM((23, 2, HID), F32),
            pltpu.VMEM((2, HID), F32),
            pltpu.VMEM((2, HID), F32),
            pltpu.VMEM((2, HID), F32),
            pltpu.VMEM((23, 2, HID), F32),
            pltpu.VMEM((2, HID), F32),
            pltpu.VMEM((2, HID), F32),
            pltpu.VMEM((2, HID), F32),
            pltpu.SMEM((12,), F32),
            pltpu.SMEM((2,), F32),
            pltpu.SMEM((2,), F32),
            pltpu.VMEM((n, 8, 128), jnp.int32),
            pltpu.VMEM((n, 8, 128), jnp.int32),
            pltpu.VMEM((n, rows, 128), jnp.int32),
            pltpu.VMEM((24, HID), F32),
            pltpu.VMEM((8, HID), F32),
            pltpu.SemaphoreType.DMA((22,)),
            pltpu.SemaphoreType.DMA((2, n)),
        ],
        compiler_params=pltpu.CompilerParams(collective_id=2, has_side_effects=True, vmem_limit_bytes=24 << 20),
        name="exchange_and_prepare",
    )(
        *[
            pltpu.with_memory_space_constraint(x, pltpu.HBM)
            for x in (
                sampled, seeds, counts, experience_buffer, aw2, jw2, lw2,
                aw1, ab1.reshape(1, HID), ab2.reshape(1, HID), aw3.T,
                jw1.transpose(1, 0, 2), jb1, jb2, jw3, lw1.transpose(1, 0, 2), lb1, lb2, lw3,
                ab3, jb3, lb3,
            )
        ],
        level.reshape(1),
    )


def stage_groups(n):
    groups, st = [(2, 1)], 2
    while st < n:
        f = 4 if (n // st) % 4 == 0 else 2
        groups.append((f, st))
        st *= f
    return groups, groups[:1] + groups[:0:-1]


def chunk_rows(rows, chunks):
    units = rows // 8
    k = min(chunks, units)
    cuts = [8 * (units * j // k) for j in range(k + 1)]
    return list(zip(cuts[:-1], cuts[1:]))


def piece_rows(end, n):
    return 8 * (-(-end // (8 * n)))


class DeviceSum:
    def __init__(self, groups, parts, mine, out, got, part, sems):
        self.sizes, self.strides = [f for f, _ in groups], [st for _, st in groups]
        self.parts, self.mine, self.out, self.got, self.part, self.sems = parts, mine, out, got, part, sems
        self.me = lax.axis_index("dp")
        self.digits = [lax.rem(self.me // st, f) for f, st in groups]
        self.spans, self.starts = [mine.shape[0]], [0]
        for s, f in enumerate(self.sizes):
            self.spans.append(self.spans[s] // f)
            self.starts.append(self.starts[s] + self.digits[s] * self.spans[s + 1])

    def member(self, s, k):
        d = lax.rem(self.digits[s] + k, self.sizes[s])
        return d, self.me + (d - self.digits[s]) * self.strides[s]

    def partners(self):
        return [self.member(s, k)[1] for s in range(len(self.sizes)) for k in range(1, self.sizes[s])]

    def copy(self, phase, s, k, c):
        lo, hi = self.parts[c]
        d, to = self.member(s, k)
        if phase == 0:
            src = self.source(s).at[pl.ds(d * self.spans[s + 1], self.spans[s + 1]), lo:hi]
            dst = self.got[s].at[k - 1, :, lo:hi]
        else:
            src = dst = self.out.at[pl.ds(self.starts[s + 1], self.spans[s + 1]), lo:hi]
        return pltpu.make_async_remote_copy(
            src_ref=src, dst_ref=dst, send_sem=self.sems.at[phase, c, s, k, 0], recv_sem=self.sems.at[phase, c, s, k, 1],
            device_id=(to,), device_id_type=pl.DeviceIdType.MESH,
        )

    def source(self, s):
        return self.mine if s == 0 else self.part[s - 1]

    def start(self, phase, s, c):
        for k in range(1, self.sizes[s]):
            self.copy(phase, s, k, c).start()

    def add(self, s, c):
        lo, hi = self.parts[c]
        span = self.spans[s + 1]
        acc = self.source(s)[pl.ds(self.digits[s] * span, span), lo:hi]
        for k in range(1, self.sizes[s]):
            self.copy(0, s, k, c).wait_recv()
            acc = acc + self.got[s][k - 1, :, lo:hi]
        if s == len(self.sizes) - 1:
            self.out[pl.ds(self.starts[s + 1], 1), lo:hi] = acc
        else:
            self.part[s][:, lo:hi] = acc

    def step(self, j, c):
        ns = len(self.sizes)
        if 1 <= j <= ns:
            self.add(j - 1, c)
        if j > ns:
            for k in range(1, self.sizes[2 * ns - j]):
                self.copy(1, 2 * ns - j, k, c).wait_recv()
        if j < ns:
            self.start(0, j, c)
        elif j < 2 * ns:
            self.start(1, 2 * ns - 1 - j, c)

    def steps(self):
        return 2 * len(self.sizes)

    def all_sent(self):
        for phase in range(2):
            for s in range(len(self.sizes)):
                for k in range(1, self.sizes[s]):
                    for c in range(len(self.parts)):
                        self.copy(phase, s, k, c).wait_send()


def sum_scratch(groups, n, rows, chunks):
    got, part, size = [], [], n
    sizes = [f for f, _ in groups]
    for f in sizes:
        size //= f
        got.append(pltpu.VMEM((f - 1, size, rows, 128), F32))
        part.append(pltpu.VMEM((size, rows, 128), F32))
    sems = pltpu.SemaphoreType.DMA((2, len(chunk_rows(rows, chunks)), len(sizes), max(sizes), 2))
    return [pltpu.VMEM((n, rows, 128), F32)] + got + part + [sems]


def put(dst, at, value):
    rows = dst.shape[1]
    r = 0
    while r < value.shape[0]:
        p, o = divmod(at + r, rows)
        k = min(rows - o, value.shape[0] - r)
        dst[p, o : o + k, :] = value[r : r + k]
        r += k


def net_kernel(
    idx_s, scal, tab, got, w1all, fa, f2, b2, head, headb, da_w, qw, col, scale,
    sum_q, sum_p,
    xrow, gw2, gw2b, gaw1, gcw1, gaw3, gcw3, gcol, gmisc, *rest,
    n, cap, slots,
):
    T = min(TILE, slots)
    nt = slots // T
    lists = T // cap
    rows = message_rows(cap)
    part = min(cap, 128)
    per = len(rest) // 2
    ns = (per - 2) // 2
    sums = [
        DeviceSum(groups, chunk_rows(r[0].shape[1], k), r[0], out, r[1 : 1 + ns], r[1 + ns : 1 + 2 * ns], r[1 + 2 * ns])
        for groups, r, out, k in zip(stage_groups(n), (rest[:per], rest[per:]), (sum_q, sum_p), CHUNKS)
    ]
    barrier = pltpu.get_barrier_semaphore()
    partners = sums[0].partners()
    for to in partners:
        pl.semaphore_signal(barrier, inc=1, device_id=(to,), device_id_type=pl.DeviceIdType.MESH)

    def gather(i):
        for t in range(T):
            r = idx_s[i * lists + t // cap, (t % cap) // 128, t % 128]
            xrow[t : t + 1, :] = tab[pl.ds(r, 1), :]

    gather(0)
    for ref in (gw2, gw2b, gaw1, gcw1, gaw3, gcw3, gcol, gmisc):
        ref[...] = jnp.zeros_like(ref)
    level = scal[4]
    jb3_s = (scal[0], scal[1])
    lb3_s = (scal[2], scal[3])

    one = scale[7:8, 0:1]

    def act32(u):
        t = jnp.tanh(u)
        p = one + t
        h = u * p
        return h, p + h * (2.0 - p)

    def act(u):
        h, d = act32(u)
        return h.astype(BF), d

    def layer2(i, l, h):
        return act(by_chunk(f2, l, i, h) + col[:, l : l + 1])

    def first(l0, l1, x24):
        hi, lo = split(x24)
        xs = jnp.concatenate([hi, lo, hi], axis=0).astype(BF)
        return dot(w1all[l0 * HID : l1 * HID, :], xs)

    def by_chunk(w, l, i, x):
        nq = T // HID
        return jnp.concatenate(
            [dot(w[l, q % VARIANTS if nq % VARIANTS == 0 else lax.rem(i * nq + q, VARIANTS)], x[:, q * HID : (q + 1) * HID]) for q in range(nq)],
            axis=1,
        )

    def exact(w, h):
        hb = h.astype(BF)
        r = dot(w[...], hb)
        half = r.shape[0] // 2
        lo = dot(w[0:half, :], (h - hb.astype(F32)).astype(BF))
        return hb, r[:half] + (r[half:] + lo)

    def head_out(o):
        o = o + col[0:16, 5:6]
        mean = o[0:8]
        t = jnp.tanh(o[8:16])
        ls = -5.0 + 3.5 * (t + 1.0)
        return mean, t, ls

    def sample(mean, ls, e, live):
        sg = jnp.exp(ls)
        u = mean + sg * e
        a = jnp.tanh(u)
        au = jnp.abs(u)
        sq = 2.0 * (math.log(2.0) - au - jnp.log(1.0 + jnp.exp(-2.0 * au)))
        lp = -0.5 * e * e - ls - 0.5 * math.log(2.0 * math.pi) - sq
        return a, sg, jnp.sum(jnp.where(live, lp, 0.0), axis=0, keepdims=True)

    def q_of(k, h2, b):
        r = dot(qw[k], h2)
        return r[0:1] + r[8:9] + b

    def softmin(q, w):
        a, b = -4.0 * q, -4.0 * w
        return -0.25 * (jnp.maximum(a, b) + jnp.log(1.0 + jnp.exp(-jnp.abs(a - b))))

    ones = jnp.ones((16, T), BF)

    @pl.loop(0, nt)
    def _(i):
        xt = xrow[...].T
        gather(jnp.minimum(i + 1, nt - 1))
        row8 = lax.broadcasted_iota(jnp.int32, (8, T), 0)
        row16 = lax.broadcasted_iota(jnp.int32, (16, T), 0)
        live = row8 < ACT
        seeds = jnp.concatenate([got[i * lists + k, rows + r : rows + r + 1, 0:part] for k in range(lists) for r in range(rows)], axis=1)
        lane = lax.broadcasted_iota(jnp.int32, (1, cap), 1)
        mask = jnp.concatenate(
            [jnp.where(lane < got[i * lists + k, 2 * rows : 2 * rows + 1, 0:1], 1.0, 0.0).astype(F32) for k in range(lists)], axis=1
        )
        alpha = jnp.exp(jnp.full((1, T), level, F32))
        b1 = pltpu.roll(xt[16:24], 7, 0)
        reward = b1[6:7]
        xa = jnp.concatenate([jnp.where(row8 == 6, 1.0, b1), xt[0:16]], axis=0)
        b2_ = pltpu.roll(xt[40:48], 7, 0)
        done = b2_[0:1]
        n_lo = jnp.where(row8 == 7, b2_, jnp.where(row8 == 6, 1.0, 0.0))
        xn = jnp.concatenate([n_lo, xt[24:40]], axis=0)

        un = first(0, 1, xn)
        hi, lo = split(xa)
        xw = jnp.concatenate([hi, lo], axis=0).astype(BF)
        ua = dot(w1all[0 : 3 * HID, :], jnp.concatenate([hi, lo, hi], axis=0).astype(BF))
        eps = noise(seeds, row16)
        e = eps[0:8]
        hn, _ = act(un)
        h1a, d1a = act32(ua[0:HID])
        h1c, d1c = zip(*[act(ua[(1 + k) * HID : (2 + k) * HID]) for k in range(2)])
        hn, _ = layer2(i, 0, hn)
        r = dot(head[...], hn)
        mean, _, ls = head_out(r[0:16] + r[16:32])
        a2, _, lp2 = sample(mean, ls, eps[8:16], live)
        h1a, r = exact(fa, h1a)
        h2a, d2a = act32(r + col[:, 0:1])
        h2a, r = exact(head, h2a)
        mean, t, ls = head_out(r)
        a1, sg, lp = sample(mean, ls, e, live)
        un = first(3, 5, jnp.concatenate([jnp.where(live, a2, n_lo), xt[24:40]], axis=0))
        h2c, d2c = zip(*[layer2(i, 1 + k, h1c[k]) for k in range(2)])
        qc = [q_of(k, h2c[k], jb3_s[k]) for k in range(2)]
        uq = first(1, 3, jnp.concatenate([jnp.where(live, a1, xa[0:8]), xt[0:16]], axis=0))
        ht = [act(un[k * HID : (k + 1) * HID])[0] for k in range(2)]
        ht = [layer2(i, 3 + k, ht[k])[0] for k in range(2)]
        qt = [q_of(2 + k, ht[k], lb3_s[k]) for k in range(2)]
        h1q, d1q = zip(*[act(uq[k * HID : (k + 1) * HID]) for k in range(2)])
        y = reward + GAMMA * (1.0 - done) * (softmin(qt[0], qt[1]) - alpha * lp2)
        h2q, d2q = zip(*[layer2(i, 1 + k, h1q[k]) for k in range(2)])
        qq = [q_of(k, h2q[k], jb3_s[k]) for k in range(2)]

        closs = jnp.zeros((1, T), F32)
        g2c = []
        for k in range(2):
            dq = qc[k] - y
            mdq = dq * mask
            closs = closs + 0.5 * (mdq * dq)
            g2 = (mdq * d2c[k]).astype(BF)
            g2c.append(g2)
            mhi, mlo = split(mdq)
            m16 = jnp.where(row16 == 0, mhi, jnp.where(row16 == 1, mlo, 0.0)).astype(BF)
            gcw3[k] += dot_t(m16, h2c[k])
            r = dot_t(jnp.concatenate([h1c[k], ones], axis=0), g2)
            gw2[1 + k] += r[0:HID]
            gw2b[1 + k] += r[HID : HID + 8]
            gmisc[k : k + 1, :] += fold(mdq)
        sm = softmin(qq[0], qq[1])
        p0 = 1.0 / (1.0 + jnp.exp(4.0 * (qq[0] - qq[1])))
        da = jnp.zeros((8, T), F32)
        for k, pk in enumerate((p0, 1.0 - p0)):
            g1 = (by_chunk(b2, 1 + k, i, d2q[k].astype(BF)) * d1q[k]).astype(BF)
            w = dot(da_w[k], g1)
            da = da - (pk * mask) * (w[0:8] + w[8:16])
        for k in range(2):
            g1 = (by_chunk(b2, 1 + k, i, g2c[k]) * d1c[k]).astype(BF)
            w = dot_t(xw, g1)
            gcw1[k] += w[0:24] + w[24:48]
        ma = mask * alpha
        du = da * (1.0 - a1 * a1) + ma * (2.0 * a1)
        dls = (du * sg * e - ma) * (3.5 * (1.0 - t * t))
        do = jnp.concatenate([jnp.where(live, du, 0.0), jnp.where(live, dls, 0.0)], axis=0)
        gcol[...] += fold(do)
        dob = do.astype(BF)
        gaw3[...] += dot_t(dob, h2a)
        g2 = (dot(headb[...], jnp.concatenate([dob, dob], axis=0)) * d2a).astype(BF)
        r = dot_t(jnp.concatenate([h1a, ones], axis=0), g2)
        gw2[0] += r[0:HID]
        gw2b[0] += r[HID : HID + 8]
        g1 = (by_chunk(b2, 0, i, g2) * d1a).astype(BF)
        w = dot_t(xw, g1)
        gaw1[...] += w[0:24] + w[24:48]
        gmisc[2:3, :] += fold(closs)
        gmisc[3:4, :] += fold(mask * (alpha * lp - sm))
        gmisc[4:5, :] += fold(mask * (lp - 6.0))
        gmisc[5:6, :] += fold(mask)

    def pack(at, value):
        k = 0 if at < R_CUT else 1
        put(sums[k].mine, at - k * R_CUT, value)

    row8 = lax.broadcasted_iota(jnp.int32, (8, HID), 0)
    cols = jnp.zeros((8, HID), F32)
    for k in range(2):
        s = scale[k : k + 1, :]
        cols = jnp.where(row8 == k, gw2b[1 + k] * s, cols)
        cols = jnp.where(row8 == 2 + k, gcw3[k, 0:1, :] + gcw3[k, 1:2, :], cols)
    cols = jnp.where(row8 == 4, gw2b[0], cols)
    for t in sums:
        rows = t.mine.shape[1]
        full = R_CUT if t is sums[0] else R_END - R_CUT
        for p in range(full // rows, n):
            t.mine[p] = jnp.zeros((rows, 128), F32)
    for m in range(3):
        for h in range(2):
            at = slice(h * 128, (h + 1) * 128)
            w = gw2[m, :, at]
            if m > 0:
                w = w * scale[m - 1 : m, at]
            pack((2 * m + h) * HID, w)
    for h in range(2):
        at = slice(h * 128, (h + 1) * 128)
        pack(R_AW1 + 24 * h, gaw1[:, at])
        for k in range(2):
            pack(R_CW1 + 48 * k + 24 * h, gcw1[k, :, at])
        pack(R_AW3 + 16 * h, gaw3[:, at])
        pack(R_COL + 8 * h, cols[:, at])
    pack(R_AB3, gcol[...])
    pack(R_MISC, gmisc[...])
    pl.semaphore_wait(barrier, len(partners))
    for j in range(2 * ns + 1):
        for t in sums:
            for c in range(len(t.parts)):
                t.step(j, c)
    for t in sums:
        t.all_sent()


def summed_grads(ready, n, cap):
    tab, got, idx_s, *weights, scal = ready
    slots = n * cap
    T = min(TILE, slots)
    heights = piece_rows(R_CUT, n), piece_rows(R_END - R_CUT, n)
    vm = pl.BlockSpec(memory_space=pltpu.VMEM)
    sm = pl.BlockSpec(memory_space=pltpu.SMEM)
    scratch = [
        pltpu.VMEM((T, 128), F32),
        pltpu.VMEM((3, HID, HID), F32),
        pltpu.VMEM((3, 8, HID), F32),
        pltpu.VMEM((24, HID), F32),
        pltpu.VMEM((2, 24, HID), F32),
        pltpu.VMEM((16, HID), F32),
        pltpu.VMEM((2, 16, HID), F32),
        pltpu.VMEM((16, 128), F32),
        pltpu.VMEM((8, 128), F32),
    ]
    for groups, height, chunks in zip(stage_groups(n), heights, CHUNKS):
        scratch += sum_scratch(groups, n, height, chunks)
    return pl.pallas_call(
        functools.partial(net_kernel, n=n, cap=cap, slots=slots),
        out_shape=[pltpu.VMEM((n, height, 128), F32) for height in heights],
        in_specs=[sm] * 2 + [vm] * (2 + len(weights)),
        out_specs=[vm, vm],
        scratch_shapes=scratch,
        compiler_params=pltpu.CompilerParams(collective_id=1, has_side_effects=True, vmem_limit_bytes=36 << 20),
        name="networks",
    )(idx_s, scal, tab, got, *weights)


def finish_kernel(scal, gq, gp, aw1, ab1, aw2, ab2, aw3, ab3, cw1, cb1, cw2, cb2, cw3, cb3, da, losses):
    def part(at, count):
        return gq[at : at + count, :] if at < R_CUT else gp[at - R_CUT : at - R_CUT + count, :]

    misc = jnp.sum(part(R_MISC, 8), axis=1, keepdims=True)
    inv = 1.0 / misc[5:6]

    def rows(at, count):
        return jnp.concatenate([part(at, count), part(at + count, count)], axis=1) * inv

    aw2[...] = rows(0, HID)
    cw2[0] = rows(2 * HID, HID)
    cw2[1] = rows(4 * HID, HID)
    w = rows(R_AW1, 24)
    aw1[0:16, :] = w[8:24]
    aw1[16:17, :] = w[7:8]
    ab1[...] = w[6:7]
    for k in range(2):
        w = rows(R_CW1 + 48 * k, 24)
        cw1[0:16, k, :] = w[8:24]
        cw1[16:17, k, :] = w[7:8]
        cw1[17:23, k, :] = w[0:6]
        cb1[k : k + 1, :] = w[6:7]
    w = rows(R_AW3, 16)
    aw3[0:6, :] = w[0:6]
    aw3[6:12, :] = w[8:14]
    c = rows(R_COL, 8)
    cb2[...] = c[0:2]
    cw3[...] = c[2:4]
    ab2[...] = c[4:5]
    b = jnp.sum(part(R_AB3, 16), axis=1, keepdims=True) * inv
    diag = lax.broadcasted_iota(jnp.int32, (16, 128), 0) == lax.broadcasted_iota(jnp.int32, (16, 128), 1)
    b = jnp.sum(jnp.where(diag, b, 0.0), axis=0, keepdims=True)
    ab3[...] = jnp.concatenate([b[:, 0:6], b[:, 8:14]], axis=1)
    m = misc * inv
    cb3[...] = jnp.concatenate([m[0:1], m[1:2]], axis=1)
    da[...] = -m[4:5]
    losses[...] = jnp.concatenate([m[2:3], m[3:4], -scal[4] * m[4:5]], axis=1)


def finish(first, second, scal):
    vm = pl.BlockSpec(memory_space=pltpu.VMEM)
    shapes = [
        (OBS, HID), (1, HID), (HID, HID), (1, HID), (12, HID), (1, 12),
        (23, 2, HID), (2, HID), (2, HID, HID), (2, HID), (2, HID), (1, 2), (1, 1), (1, 3),
    ]
    outs = list(pl.pallas_call(
        finish_kernel,
        out_shape=[jax.ShapeDtypeStruct(x, F32) for x in shapes],
        in_specs=[pl.BlockSpec(memory_space=pltpu.SMEM), vm, vm],
        out_specs=[vm] * len(shapes),
        compiler_params=pltpu.CompilerParams(vmem_limit_bytes=16 << 20),
        name="finish",
    )(scal, first.reshape(-1, 128), second.reshape(-1, 128)))
    outs[4] = outs[4].T
    outs[6] = outs[6].transpose(1, 0, 2)
    for k, shape in ((1, (HID,)), (3, (HID,)), (5, (12,)), (11, (2,)), (12, ()), (13, (3,))):
        outs[k] = outs[k].reshape(shape)
    return tuple(outs)


def body(experience_buffer, sampled_indices, filled_lengths, randomizer_numbers, *params):
    n, cap = sampled_indices.shape[1:]
    ready = prepare(experience_buffer, sampled_indices, randomizer_numbers, filled_lengths, params)
    return finish(*summed_grads(ready, n, cap), ready[-1])


def solution(mesh):
    in_specs = (P(None, "dp"), P("dp", None, None), P("dp", None), P("dp", None, None)) + (P(),) * 19
    return jax.shard_map(body, mesh=mesh, in_specs=in_specs, out_specs=(P(),) * 14, check_vma=False)
```

```python
import functools
import math

import jax
import jax.numpy as jnp
from jax import lax
from jax.experimental import pallas as pl
from jax.experimental.pallas import tpu as pltpu
from jax.sharding import PartitionSpec as P

OBS = 17
ACT = 6
HID = 256
GAMMA = 0.99
PRIME = 65521
TILE = 1024
CHUNKS = (2, 1)
VARIANTS = 4
R_AW1 = 6 * HID
R_CW1 = R_AW1 + 48
R_AW3 = R_CW1 + 96
R_COL = R_AW3 + 32
R_AB3 = R_COL + 16
R_MISC = R_AB3 + 16
R_END = R_MISC + 8
R_CUT = 5 * HID
BF = jnp.bfloat16
F32 = jnp.float32


def dot(a, b):
    return jnp.dot(a, b, preferred_element_type=F32)


def dot_t(a, b):
    return lax.dot_general(a, b, (((1,), (1,)), ((), ())), preferred_element_type=F32)


def split(x):
    hi = x.astype(BF).astype(F32)
    return hi, x - hi


def fold_prime(x):
    return (x >> 16) * 15 + (x & 65535)


def below_prime(x):
    return jnp.where(x >= PRIME, x - PRIME, x)


def noise(seeds, rows):
    comp = jnp.where(rows >= 8, rows - 2, rows)
    z = below_prime(fold_prime(seeds))
    h0 = below_prime(fold_prime(z * 257 + comp * 7919 + 1))
    h1 = below_prime(fold_prime(fold_prime(h0 * 32749 + 12345)))
    h2 = below_prime(fold_prime(fold_prime(h1 * 32749 + 54321)))
    u1 = (h1.astype(F32) + 0.5) * (1.0 / PRIME)
    x = jnp.abs((2 * h2 + (1 - PRIME)).astype(F32)) * (math.pi / PRIME) - 0.5 * math.pi
    x2 = x * x
    p = -1.0 / 39916800.0
    for c in (1.0 / 362880.0, -1.0 / 5040.0, 1.0 / 120.0, -1.0 / 6.0, 1.0):
        p = p * x2 + c
    return jnp.sqrt(-2.0 * jnp.log(u1)) * (p * x)


def fold(x):
    return functools.reduce(lambda a, b: a + b, [x[:, k * 128 : (k + 1) * 128] for k in range(x.shape[1] // 128)])


def message_rows(cap):
    return -(-cap // 128)


def prepare_kernel(
    idx_h, seed_h, cnt_h, buf_h, aw2_h, jw2_h, lw2_h,
    aw1_h, ab1_h, ab2_h, aw3_h, jw1_h, jb1_h, jb2_h, jw3_h, lw1_h, lb1_h, lb2_h, lw3_h,
    ab3_h, jb3_h, lb3_h, level,
    tab, got, idx_s, w1all, f2, f2v, b2, b2v, head, headb, da_w, qw, col, scale, scal,
    idx_v, seed_v, cnt_v, buf, w2, aw1, ab1, ab2, aw3, jw1, jb1, jb2, jw3, lw1, lb1, lb2, lw3,
    ab3, jb3, lb3, msg, land, flat, tmp, rowbuf, in_sems, sems,
    *, n, cap,
):
    me = lax.axis_index("dp")
    rows = message_rows(cap)
    part = min(cap, 128)
    width = buf.shape[1]
    pairs = (
        (idx_h, idx_v), (seed_h, seed_v), (cnt_h, cnt_v), (buf_h, buf),
        (aw2_h, w2.at[0]), (jw2_h, w2.at[pl.ds(1, 2)]), (lw2_h, w2.at[pl.ds(3, 2)]),
        (aw1_h, aw1), (ab1_h, ab1), (ab2_h, ab2), (aw3_h, aw3), (jw1_h, jw1), (jb1_h, jb1), (jb2_h, jb2),
        (jw3_h, jw3), (lw1_h, lw1), (lb1_h, lb1), (lb2_h, lb2), (lw3_h, lw3),
        (ab3_h, ab3), (jb3_h, jb3), (lb3_h, lb3),
    )
    loads = [pltpu.make_async_copy(src, dst, in_sems.at[k]) for k, (src, dst) in enumerate(pairs)]
    for c in loads:
        c.start()
    barrier = pltpu.get_barrier_semaphore()

    @pl.loop(1, n)
    def _(k):
        pl.semaphore_signal(barrier, inc=1, device_id=(lax.rem(me + k, n),), device_id_type=pl.DeviceIdType.MESH)

    for c in loads[:3]:
        c.wait()
    msg[...] = jnp.zeros_like(msg)
    for r in range(rows):
        msg[:, r, 0:part] = idx_v[0, :, r * part : (r + 1) * part]
        msg[:, rows + r, 0:part] = seed_v[0, :, r * part : (r + 1) * part]
    diag = lax.broadcasted_iota(jnp.int32, (n, n), 0) == lax.broadcasted_iota(jnp.int32, (n, n), 1)
    counts = jnp.sum(jnp.where(diag, cnt_v[...].astype(F32), 0.0), axis=1, keepdims=True)
    msg[:, 2 * rows, :] = jnp.broadcast_to(counts, (n, 128)).astype(jnp.int32)
    for c in loads[4:]:
        c.wait()
    for l, (w1, b1, k) in enumerate(((aw1, ab1, None), (jw1, jb1, 0), (jw1, jb1, 1), (lw1, lb1, 0), (lw1, lb1, 1))):
        if k is None:
            tmp[0:6, :] = jnp.zeros((6, HID), F32)
            tmp[6:7, :] = b1[...]
            tmp[7:8, :] = w1[16:17, :]
            tmp[8:24, :] = w1[0:16, :]
        else:
            tmp[0:6, :] = w1[17:23, k, :]
            tmp[6:7, :] = b1[k : k + 1, :]
            tmp[7:8, :] = w1[16:17, k, :]
            tmp[8:24, :] = w1[0:16, k, :]
        hi, lo = split(0.5 * tmp[0:24, :])
        w1all[l * HID : (l + 1) * HID, :] = jnp.concatenate([hi, hi, lo], axis=0).T.astype(BF)
        if l in (1, 2):
            hi, lo = split(tmp[0:8, :])
            da_w[l - 1] = jnp.concatenate([hi, lo], axis=0).astype(BF)
    start = ((2 * me + 1).astype(F32) / n - 1.0) * 2.0**-8

    def roundings(ref, l, w):
        left = w.astype(BF).astype(F32) * start
        for v in range(VARIANTS):
            want = w + left
            got_ = want.astype(BF)
            ref[l, v] = got_
            left = want - got_.astype(F32)

    def pieces(ref, l, w):
        hi, lo = split(w)
        ref[l, 0:HID, :] = hi.astype(BF)
        ref[l, HID:, :] = lo.astype(BF)

    for l in range(5):
        w = 0.5 * w2[l]
        wt = w.T
        pieces(f2, l, wt)
        if l in (1, 2):
            roundings(f2v, l - 1, wt)
            w = w * (0.5 * jw3[l - 1 : l, :])
            pieces(b2, l - 1, w)
        if l < 3:
            roundings(b2v, l, w)
    tmp[0:12, :] = aw3[...]
    r8 = lax.broadcasted_iota(jnp.int32, (8, HID), 0)
    w_head = jnp.concatenate([jnp.where(r8 < 6, tmp[0:8, :], 0.0), jnp.where(r8 < 6, tmp[6:14, :], 0.0)], axis=0)
    hi, lo = split(w_head)
    head[...] = jnp.concatenate([hi, lo], axis=0).astype(BF)
    headb[...] = (0.5 * jnp.concatenate([hi, lo], axis=0)).T.astype(BF)
    for k in range(4):
        w3 = jw3[k : k + 1, :] if k < 2 else lw3[k - 2 : k - 1, :]
        hi, lo = split(w3)
        qw[k] = jnp.concatenate([jnp.where(r8 == 0, hi, 0.0), jnp.where(r8 == 0, lo, 0.0)], axis=0).astype(BF)
    rowbuf[...] = jnp.zeros_like(rowbuf)
    rowbuf[0:1, :] = 0.5 * ab2[...]
    rowbuf[1:3, :] = 0.5 * jb2[...]
    rowbuf[3:5, :] = 0.5 * lb2[...]
    lane12 = lax.broadcasted_iota(jnp.int32, (1, HID), 1)
    hb = jnp.zeros((1, HID), F32)
    for k in range(12):
        hb = jnp.where(lane12 == (k if k < 6 else k + 2), ab3[k], hb)
    rowbuf[5:6, :] = hb
    col[...] = rowbuf[...].T
    scale[...] = jnp.zeros_like(scale)
    scale[0:2, :] = 0.5 * jw3[...]
    scale[7:8, :] = jnp.ones((1, HID), F32)
    for k in range(2):
        scal[k] = jb3[k]
        scal[2 + k] = lb3[k]
    scal[4] = level[0]

    pl.semaphore_wait(barrier, n - 1)

    def copy(k):
        return pltpu.make_async_remote_copy(
            src_ref=msg.at[lax.rem(me + k, n)], dst_ref=land.at[k], send_sem=sems.at[0, k], recv_sem=sems.at[1, k],
            device_id=(lax.rem(me + k, n),), device_id_type=pl.DeviceIdType.MESH,
        )

    @pl.loop(1, n)
    def _(k):
        copy(k).start()

    loads[3].wait()

    @pl.loop(0, width // 128, unroll=4)
    def _(c):
        blk = buf[:, pl.ds(pl.multiple_of(c * 128, 128), 128)]
        tab[pl.ds(pl.multiple_of(c * 128, 128), 128), 0:42] = blk.T

    land[0] = msg[me]

    @pl.loop(1, n)
    def _(k):
        copy(k).wait()

    @pl.loop(0, n)
    def _(k):
        got[lax.rem(me - k + n, n)] = land[k]

    for r in range(rows):
        flat[:, r, :] = got[:, r, :]
    c = pltpu.make_async_copy(flat, idx_s, in_sems.at[0])
    c.start()
    c.wait()


def prepare(experience_buffer, sampled, seeds, counts, params):
    (aw1, ab1, aw2, ab2, aw3, ab3, jw1, jb1, jw2, jb2, jw3, jb3, lw1, lb1, lw2, lb2, lw3, lb3, level) = params
    feats, width = experience_buffer.shape
    _, n, cap = sampled.shape
    rows = message_rows(cap)
    vm = pl.BlockSpec(memory_space=pltpu.VMEM)
    sm = pl.BlockSpec(memory_space=pltpu.SMEM)
    hbm = pl.BlockSpec(memory_space=pl.ANY)
    out = [
        pltpu.VMEM((width, 128), F32),
        pltpu.VMEM((n, 8, 128), jnp.int32),
        pltpu.SMEM((n, rows, 128), jnp.int32),
        pltpu.VMEM((5 * HID, 72), BF),
        pltpu.VMEM((5, 2 * HID, HID), BF),
        pltpu.VMEM((2, VARIANTS, HID, HID), BF),
        pltpu.VMEM((2, 2 * HID, HID), BF),
        pltpu.VMEM((3, VARIANTS, HID, HID), BF),
        pltpu.VMEM((32, HID), BF),
        pltpu.VMEM((HID, 32), BF),
        pltpu.VMEM((2, 16, HID), BF),
        pltpu.VMEM((4, 16, HID), BF),
        pltpu.VMEM((HID, 8), F32),
        pltpu.VMEM((8, HID), F32),
        pltpu.SMEM((8,), F32),
    ]
    return pl.pallas_call(
        functools.partial(prepare_kernel, n=n, cap=cap),
        out_shape=out,
        in_specs=[hbm] * 22 + [sm],
        out_specs=[vm, vm, sm] + [vm] * 11 + [sm],
        scratch_shapes=[
            pltpu.VMEM((1, n, cap), jnp.int32),
            pltpu.VMEM((1, n, cap), jnp.int32),
            pltpu.VMEM((1, n), jnp.int32),
            pltpu.VMEM((feats, width), F32),
            pltpu.VMEM((5, HID, HID), F32),
            pltpu.VMEM((OBS, HID), F32),
            pltpu.VMEM((1, HID), F32),
            pltpu.VMEM((1, HID), F32),
            pltpu.VMEM((12, HID), F32),
            pltpu.VMEM((23, 2, HID), F32),
            pltpu.VMEM((2, HID), F32),
            pltpu.VMEM((2, HID), F32),
            pltpu.VMEM((2, HID), F32),
            pltpu.VMEM((23, 2, HID), F32),
            pltpu.VMEM((2, HID), F32),
            pltpu.VMEM((2, HID), F32),
            pltpu.VMEM((2, HID), F32),
            pltpu.SMEM((12,), F32),
            pltpu.SMEM((2,), F32),
            pltpu.SMEM((2,), F32),
            pltpu.VMEM((n, 8, 128), jnp.int32),
            pltpu.VMEM((n, 8, 128), jnp.int32),
            pltpu.VMEM((n, rows, 128), jnp.int32),
            pltpu.VMEM((24, HID), F32),
            pltpu.VMEM((8, HID), F32),
            pltpu.SemaphoreType.DMA((22,)),
            pltpu.SemaphoreType.DMA((2, n)),
        ],
        compiler_params=pltpu.CompilerParams(collective_id=2, has_side_effects=True, vmem_limit_bytes=24 << 20),
        name="exchange_and_prepare",
    )(
        *[
            pltpu.with_memory_space_constraint(x, pltpu.HBM)
            for x in (
                sampled, seeds, counts, experience_buffer, aw2, jw2, lw2,
                aw1, ab1.reshape(1, HID), ab2.reshape(1, HID), aw3.T,
                jw1.transpose(1, 0, 2), jb1, jb2, jw3, lw1.transpose(1, 0, 2), lb1, lb2, lw3,
                ab3, jb3, lb3,
            )
        ],
        level.reshape(1),
    )


def stage_groups(n):
    groups, st = [(2, 1)], 2
    while st < n:
        f = 4 if (n // st) % 4 == 0 else 2
        groups.append((f, st))
        st *= f
    return groups, groups[:1] + groups[:0:-1]


def chunk_rows(rows, chunks):
    units = rows // 8
    k = min(chunks, units)
    cuts = [8 * (units * j // k) for j in range(k + 1)]
    return list(zip(cuts[:-1], cuts[1:]))


def piece_rows(end, n):
    return 8 * (-(-end // (8 * n)))


class DeviceSum:
    def __init__(self, groups, parts, mine, out, got, part, sems):
        self.sizes, self.strides = [f for f, _ in groups], [st for _, st in groups]
        self.parts, self.mine, self.out, self.got, self.part, self.sems = parts, mine, out, got, part, sems
        self.me = lax.axis_index("dp")
        self.digits = [lax.rem(self.me // st, f) for f, st in groups]
        self.spans, self.starts = [mine.shape[0]], [0]
        for s, f in enumerate(self.sizes):
            self.spans.append(self.spans[s] // f)
            self.starts.append(self.starts[s] + self.digits[s] * self.spans[s + 1])

    def member(self, s, k):
        d = lax.rem(self.digits[s] + k, self.sizes[s])
        return d, self.me + (d - self.digits[s]) * self.strides[s]

    def partners(self):
        return [self.member(s, k)[1] for s in range(len(self.sizes)) for k in range(1, self.sizes[s])]

    def copy(self, phase, s, k, c):
        lo, hi = self.parts[c]
        d, to = self.member(s, k)
        if phase == 0:
            src = self.source(s).at[pl.ds(d * self.spans[s + 1], self.spans[s + 1]), lo:hi]
            dst = self.got[s].at[k - 1, :, lo:hi]
        else:
            src = dst = self.out.at[pl.ds(self.starts[s + 1], self.spans[s + 1]), lo:hi]
        return pltpu.make_async_remote_copy(
            src_ref=src, dst_ref=dst, send_sem=self.sems.at[phase, c, s, k, 0], recv_sem=self.sems.at[phase, c, s, k, 1],
            device_id=(to,), device_id_type=pl.DeviceIdType.MESH,
        )

    def source(self, s):
        return self.mine if s == 0 else self.part[s - 1]

    def start(self, phase, s, c):
        for k in range(1, self.sizes[s]):
            self.copy(phase, s, k, c).start()

    def add(self, s, c):
        lo, hi = self.parts[c]
        span = self.spans[s + 1]
        acc = self.source(s)[pl.ds(self.digits[s] * span, span), lo:hi]
        for k in range(1, self.sizes[s]):
            self.copy(0, s, k, c).wait_recv()
            acc = acc + self.got[s][k - 1, :, lo:hi]
        if s == len(self.sizes) - 1:
            self.out[pl.ds(self.starts[s + 1], 1), lo:hi] = acc
        else:
            self.part[s][:, lo:hi] = acc

    def step(self, j, c):
        ns = len(self.sizes)
        if 1 <= j <= ns:
            self.add(j - 1, c)
        if j > ns:
            for k in range(1, self.sizes[2 * ns - j]):
                self.copy(1, 2 * ns - j, k, c).wait_recv()
        if j < ns:
            self.start(0, j, c)
        elif j < 2 * ns:
            self.start(1, 2 * ns - 1 - j, c)

    def steps(self):
        return 2 * len(self.sizes)

    def all_sent(self):
        for phase in range(2):
            for s in range(len(self.sizes)):
                for k in range(1, self.sizes[s]):
                    for c in range(len(self.parts)):
                        self.copy(phase, s, k, c).wait_send()


def sum_scratch(groups, n, rows, chunks):
    got, part, size = [], [], n
    sizes = [f for f, _ in groups]
    for f in sizes:
        size //= f
        got.append(pltpu.VMEM((f - 1, size, rows, 128), F32))
        part.append(pltpu.VMEM((size, rows, 128), F32))
    sems = pltpu.SemaphoreType.DMA((2, len(chunk_rows(rows, chunks)), len(sizes), max(sizes), 2))
    return [pltpu.VMEM((n, rows, 128), F32)] + got + part + [sems]


def put(dst, at, value):
    rows = dst.shape[1]
    r = 0
    while r < value.shape[0]:
        p, o = divmod(at + r, rows)
        k = min(rows - o, value.shape[0] - r)
        dst[p, o : o + k, :] = value[r : r + k]
        r += k


def net_kernel(
    idx_s, scal, tab, got, w1all, f2, f2v, b2, b2v, head, headb, da_w, qw, col, scale,
    sum_q, sum_p,
    xrow, gw2, gw2b, gaw1, gcw1, gaw3, gcw3, gcol, gmisc, *rest,
    n, cap, slots,
):
    T = min(TILE, slots)
    nt = slots // T
    lists = T // cap
    rows = message_rows(cap)
    part = min(cap, 128)
    per = len(rest) // 2
    ns = (per - 2) // 2
    sums = [
        DeviceSum(groups, chunk_rows(r[0].shape[1], k), r[0], out, r[1 : 1 + ns], r[1 + ns : 1 + 2 * ns], r[1 + 2 * ns])
        for groups, r, out, k in zip(stage_groups(n), (rest[:per], rest[per:]), (sum_q, sum_p), CHUNKS)
    ]
    barrier = pltpu.get_barrier_semaphore()
    partners = sums[0].partners()
    for to in partners:
        pl.semaphore_signal(barrier, inc=1, device_id=(to,), device_id_type=pl.DeviceIdType.MESH)

    def gather(i):
        for t in range(T):
            r = idx_s[i * lists + t // cap, (t % cap) // 128, t % 128]
            xrow[t : t + 1, :] = tab[pl.ds(r, 1), :]

    gather(0)
    for ref in (gw2, gw2b, gaw1, gcw1, gaw3, gcw3, gcol, gmisc):
        ref[...] = jnp.zeros_like(ref)
    level = scal[4]
    jb3_s = (scal[0], scal[1])
    lb3_s = (scal[2], scal[3])

    one = scale[7:8, 0:1]

    def act32(u):
        t = jnp.tanh(u)
        p = one + t
        h = u * p
        return h, p + h * (2.0 - p)

    def act(u):
        h, d = act32(u)
        return h.astype(BF), d

    def both(w, x):
        r = dot(w, x)
        return r[:HID] + r[HID:]

    def layer2(l, h):
        return act(both(f2[l], h) + col[:, l : l + 1])

    def layer2_once(i, l, h):
        return act(by_chunk(f2v, l - 1, i, h) + col[:, l : l + 1])

    def first(l0, l1, x24):
        hi, lo = split(x24)
        xs = jnp.concatenate([hi, lo, hi], axis=0).astype(BF)
        return dot(w1all[l0 * HID : l1 * HID, :], xs)

    def by_chunk(w, l, i, x):
        nq = T // HID
        return jnp.concatenate(
            [dot(w[l, q % VARIANTS if nq % VARIANTS == 0 else lax.rem(i * nq + q, VARIANTS)], x[:, q * HID : (q + 1) * HID]) for q in range(nq)],
            axis=1,
        )

    def exact(w, h):
        hb = h.astype(BF)
        r = dot(w, hb)
        half = r.shape[0] // 2
        lo = dot(w[0:half], (h - hb.astype(F32)).astype(BF))
        return hb, r[:half] + (r[half:] + lo)

    def head_out(o):
        o = o + col[0:16, 5:6]
        mean = o[0:8]
        t = jnp.tanh(o[8:16])
        ls = -5.0 + 3.5 * (t + 1.0)
        return mean, t, ls

    def sample(mean, ls, e, live):
        sg = jnp.exp(ls)
        u = mean + sg * e
        a = jnp.tanh(u)
        au = jnp.abs(u)
        sq = 2.0 * (math.log(2.0) - au - jnp.log(1.0 + jnp.exp(-2.0 * au)))
        lp = -0.5 * e * e - ls - 0.5 * math.log(2.0 * math.pi) - sq
        return a, sg, jnp.sum(jnp.where(live, lp, 0.0), axis=0, keepdims=True)

    def q_of(k, h2, b):
        r = dot(qw[k], h2)
        return r[0:1] + r[8:9] + b

    def softmin(q, w):
        a, b = -4.0 * q, -4.0 * w
        return -0.25 * (jnp.maximum(a, b) + jnp.log(1.0 + jnp.exp(-jnp.abs(a - b))))

    ones = jnp.ones((16, T), BF)

    @pl.loop(0, nt)
    def _(i):
        xt = xrow[...].T
        gather(jnp.minimum(i + 1, nt - 1))
        row8 = lax.broadcasted_iota(jnp.int32, (8, T), 0)
        row16 = lax.broadcasted_iota(jnp.int32, (16, T), 0)
        live = row8 < ACT
        seeds = jnp.concatenate([got[i * lists + k, rows + r : rows + r + 1, 0:part] for k in range(lists) for r in range(rows)], axis=1)
        lane = lax.broadcasted_iota(jnp.int32, (1, cap), 1)
        mask = jnp.concatenate(
            [jnp.where(lane < got[i * lists + k, 2 * rows : 2 * rows + 1, 0:1], 1.0, 0.0).astype(F32) for k in range(lists)], axis=1
        )
        alpha = jnp.exp(jnp.full((1, T), level, F32))
        b1 = pltpu.roll(xt[16:24], 7, 0)
        reward = b1[6:7]
        xa = jnp.concatenate([jnp.where(row8 == 6, 1.0, b1), xt[0:16]], axis=0)
        b2_ = pltpu.roll(xt[40:48], 7, 0)
        done = b2_[0:1]
        n_lo = jnp.where(row8 == 7, b2_, jnp.where(row8 == 6, 1.0, 0.0))
        xn = jnp.concatenate([n_lo, xt[24:40]], axis=0)

        un = first(0, 1, xn)
        hi, lo = split(xa)
        xw = jnp.concatenate([hi, lo], axis=0).astype(BF)
        ua = dot(w1all[0 : 3 * HID, :], jnp.concatenate([hi, lo, hi], axis=0).astype(BF))
        eps = noise(seeds, row16)
        e = eps[0:8]
        hn, _ = act(un)
        h1a, d1a = act32(ua[0:HID])
        h1c, d1c = zip(*[act(ua[(1 + k) * HID : (2 + k) * HID]) for k in range(2)])
        hn, _ = layer2(0, hn)
        r = dot(head[...], hn)
        mean, _, ls = head_out(r[0:16] + r[16:32])
        a2, _, lp2 = sample(mean, ls, eps[8:16], live)
        h1a, r = exact(f2[0], h1a)
        h2a, d2a = act32(r + col[:, 0:1])
        h2a, r = exact(head[...], h2a)
        mean, t, ls = head_out(r)
        a1, sg, lp = sample(mean, ls, e, live)
        un = first(3, 5, jnp.concatenate([jnp.where(live, a2, n_lo), xt[24:40]], axis=0))
        h2c, d2c = zip(*[layer2(1 + k, h1c[k]) for k in range(2)])
        qc = [q_of(k, h2c[k], jb3_s[k]) for k in range(2)]
        uq = first(1, 3, jnp.concatenate([jnp.where(live, a1, xa[0:8]), xt[0:16]], axis=0))
        ht = [act(un[k * HID : (k + 1) * HID])[0] for k in range(2)]
        ht = [layer2(3 + k, ht[k])[0] for k in range(2)]
        qt = [q_of(2 + k, ht[k], lb3_s[k]) for k in range(2)]
        h1q, d1q = zip(*[act(uq[k * HID : (k + 1) * HID]) for k in range(2)])
        y = reward + GAMMA * (1.0 - done) * (softmin(qt[0], qt[1]) - alpha * lp2)
        h2q, d2q = zip(*[layer2_once(i, 1 + k, h1q[k]) for k in range(2)])
        qq = [q_of(k, h2q[k], jb3_s[k]) for k in range(2)]

        closs = jnp.zeros((1, T), F32)
        g2c = []
        for k in range(2):
            dq = qc[k] - y
            mdq = dq * mask
            closs = closs + 0.5 * (mdq * dq)
            g2 = (mdq * d2c[k]).astype(BF)
            g2c.append(g2)
            mhi, mlo = split(mdq)
            m16 = jnp.where(row16 == 0, mhi, jnp.where(row16 == 1, mlo, 0.0)).astype(BF)
            gcw3[k] += dot_t(m16, h2c[k])
            r = dot_t(jnp.concatenate([h1c[k], ones], axis=0), g2)
            gw2[1 + k] += r[0:HID]
            gw2b[1 + k] += r[HID : HID + 8]
            gmisc[k : k + 1, :] += fold(mdq)
        sm = softmin(qq[0], qq[1])
        p0 = 1.0 / (1.0 + jnp.exp(4.0 * (qq[0] - qq[1])))
        da = jnp.zeros((8, T), F32)
        for k, pk in enumerate((p0, 1.0 - p0)):
            g1 = (by_chunk(b2v, 1 + k, i, d2q[k].astype(BF)) * d1q[k]).astype(BF)
            w = dot(da_w[k], g1)
            da = da - (pk * mask) * (w[0:8] + w[8:16])
        for k in range(2):
            g1 = (both(b2[k], g2c[k]) * d1c[k]).astype(BF)
            w = dot_t(xw, g1)
            gcw1[k] += w[0:24] + w[24:48]
        ma = mask * alpha
        du = da * (1.0 - a1 * a1) + ma * (2.0 * a1)
        dls = (du * sg * e - ma) * (3.5 * (1.0 - t * t))
        do = jnp.concatenate([jnp.where(live, du, 0.0), jnp.where(live, dls, 0.0)], axis=0)
        gcol[...] += fold(do)
        dob = do.astype(BF)
        gaw3[...] += dot_t(dob, h2a)
        g2 = (dot(headb[...], jnp.concatenate([dob, dob], axis=0)) * d2a).astype(BF)
        r = dot_t(jnp.concatenate([h1a, ones], axis=0), g2)
        gw2[0] += r[0:HID]
        gw2b[0] += r[HID : HID + 8]
        g1 = (by_chunk(b2v, 0, i, g2) * d1a).astype(BF)
        w = dot_t(xw, g1)
        gaw1[...] += w[0:24] + w[24:48]
        gmisc[2:3, :] += fold(closs)
        gmisc[3:4, :] += fold(mask * (alpha * lp - sm))
        gmisc[4:5, :] += fold(mask * (lp - 6.0))
        gmisc[5:6, :] += fold(mask)

    def pack(at, value):
        k = 0 if at < R_CUT else 1
        put(sums[k].mine, at - k * R_CUT, value)

    row8 = lax.broadcasted_iota(jnp.int32, (8, HID), 0)
    cols = jnp.zeros((8, HID), F32)
    for k in range(2):
        s = scale[k : k + 1, :]
        cols = jnp.where(row8 == k, gw2b[1 + k] * s, cols)
        cols = jnp.where(row8 == 2 + k, gcw3[k, 0:1, :] + gcw3[k, 1:2, :], cols)
    cols = jnp.where(row8 == 4, gw2b[0], cols)
    for t in sums:
        rows = t.mine.shape[1]
        full = R_CUT if t is sums[0] else R_END - R_CUT
        for p in range(full // rows, n):
            t.mine[p] = jnp.zeros((rows, 128), F32)
    for m in range(3):
        for h in range(2):
            at = slice(h * 128, (h + 1) * 128)
            w = gw2[m, :, at]
            if m > 0:
                w = w * scale[m - 1 : m, at]
            pack((2 * m + h) * HID, w)
    for h in range(2):
        at = slice(h * 128, (h + 1) * 128)
        pack(R_AW1 + 24 * h, gaw1[:, at])
        for k in range(2):
            pack(R_CW1 + 48 * k + 24 * h, gcw1[k, :, at])
        pack(R_AW3 + 16 * h, gaw3[:, at])
        pack(R_COL + 8 * h, cols[:, at])
    pack(R_AB3, gcol[...])
    pack(R_MISC, gmisc[...])
    pl.semaphore_wait(barrier, len(partners))
    for j in range(2 * ns + 1):
        for t in sums:
            for c in range(len(t.parts)):
                t.step(j, c)
    for t in sums:
        t.all_sent()


def summed_grads(ready, n, cap):
    tab, got, idx_s, *weights, scal = ready
    slots = n * cap
    T = min(TILE, slots)
    heights = piece_rows(R_CUT, n), piece_rows(R_END - R_CUT, n)
    vm = pl.BlockSpec(memory_space=pltpu.VMEM)
    sm = pl.BlockSpec(memory_space=pltpu.SMEM)
    scratch = [
        pltpu.VMEM((T, 128), F32),
        pltpu.VMEM((3, HID, HID), F32),
        pltpu.VMEM((3, 8, HID), F32),
        pltpu.VMEM((24, HID), F32),
        pltpu.VMEM((2, 24, HID), F32),
        pltpu.VMEM((16, HID), F32),
        pltpu.VMEM((2, 16, HID), F32),
        pltpu.VMEM((16, 128), F32),
        pltpu.VMEM((8, 128), F32),
    ]
    for groups, height, chunks in zip(stage_groups(n), heights, CHUNKS):
        scratch += sum_scratch(groups, n, height, chunks)
    return pl.pallas_call(
        functools.partial(net_kernel, n=n, cap=cap, slots=slots),
        out_shape=[pltpu.VMEM((n, height, 128), F32) for height in heights],
        in_specs=[sm] * 2 + [vm] * (2 + len(weights)),
        out_specs=[vm, vm],
        scratch_shapes=scratch,
        compiler_params=pltpu.CompilerParams(collective_id=1, has_side_effects=True, vmem_limit_bytes=36 << 20),
        name="networks",
    )(idx_s, scal, tab, got, *weights)


def finish_kernel(scal, gq, gp, aw1, ab1, aw2, ab2, aw3, ab3, cw1, cb1, cw2, cb2, cw3, cb3, da, losses):
    def part(at, count):
        return gq[at : at + count, :] if at < R_CUT else gp[at - R_CUT : at - R_CUT + count, :]

    misc = jnp.sum(part(R_MISC, 8), axis=1, keepdims=True)
    inv = 1.0 / misc[5:6]

    def rows(at, count):
        return jnp.concatenate([part(at, count), part(at + count, count)], axis=1) * inv

    aw2[...] = rows(0, HID)
    cw2[0] = rows(2 * HID, HID)
    cw2[1] = rows(4 * HID, HID)
    w = rows(R_AW1, 24)
    aw1[0:16, :] = w[8:24]
    aw1[16:17, :] = w[7:8]
    ab1[...] = w[6:7]
    for k in range(2):
        w = rows(R_CW1 + 48 * k, 24)
        cw1[0:16, k, :] = w[8:24]
        cw1[16:17, k, :] = w[7:8]
        cw1[17:23, k, :] = w[0:6]
        cb1[k : k + 1, :] = w[6:7]
    w = rows(R_AW3, 16)
    aw3[0:6, :] = w[0:6]
    aw3[6:12, :] = w[8:14]
    c = rows(R_COL, 8)
    cb2[...] = c[0:2]
    cw3[...] = c[2:4]
    ab2[...] = c[4:5]
    b = jnp.sum(part(R_AB3, 16), axis=1, keepdims=True) * inv
    diag = lax.broadcasted_iota(jnp.int32, (16, 128), 0) == lax.broadcasted_iota(jnp.int32, (16, 128), 1)
    b = jnp.sum(jnp.where(diag, b, 0.0), axis=0, keepdims=True)
    ab3[...] = jnp.concatenate([b[:, 0:6], b[:, 8:14]], axis=1)
    m = misc * inv
    cb3[...] = jnp.concatenate([m[0:1], m[1:2]], axis=1)
    da[...] = -m[4:5]
    losses[...] = jnp.concatenate([m[2:3], m[3:4], -scal[4] * m[4:5]], axis=1)


def finish(first, second, scal):
    vm = pl.BlockSpec(memory_space=pltpu.VMEM)
    shapes = [
        (OBS, HID), (1, HID), (HID, HID), (1, HID), (12, HID), (1, 12),
        (23, 2, HID), (2, HID), (2, HID, HID), (2, HID), (2, HID), (1, 2), (1, 1), (1, 3),
    ]
    outs = list(pl.pallas_call(
        finish_kernel,
        out_shape=[jax.ShapeDtypeStruct(x, F32) for x in shapes],
        in_specs=[pl.BlockSpec(memory_space=pltpu.SMEM), vm, vm],
        out_specs=[vm] * len(shapes),
        compiler_params=pltpu.CompilerParams(vmem_limit_bytes=16 << 20),
        name="finish",
    )(scal, first.reshape(-1, 128), second.reshape(-1, 128)))
    outs[4] = outs[4].T
    outs[6] = outs[6].transpose(1, 0, 2)
    for k, shape in ((1, (HID,)), (3, (HID,)), (5, (12,)), (11, (2,)), (12, ()), (13, (3,))):
        outs[k] = outs[k].reshape(shape)
    return tuple(outs)


def body(experience_buffer, sampled_indices, filled_lengths, randomizer_numbers, *params):
    n, cap = sampled_indices.shape[1:]
    ready = prepare(experience_buffer, sampled_indices, randomizer_numbers, filled_lengths, params)
    return finish(*summed_grads(ready, n, cap), ready[-1])


def solution(mesh):
    in_specs = (P(None, "dp"), P("dp", None, None), P("dp", None), P("dp", None, None)) + (P(),) * 19
    return jax.shard_map(body, mesh=mesh, in_specs=in_specs, out_specs=(P(),) * 14, check_vma=False)
```
